32 devices in a mesh: dp: 16 (over z, y, core), mp: 2 (over x).
Axes of the slice: x: 2, y: 2, z: 4, core: 2. Of those that a mesh axis runs over, the one named last changes fastest.
Arguments:
- tokens: bfloat16 [6272, 768], P(('dp', 'mp')), may hold values from -6 to 6
- ln1_gain: bfloat16 [768], replicated, may hold values from 0.5 to 1.5
- ln1_bias: bfloat16 [768], replicated, may hold values from -1.75 to 1.75
- qkv_weight: bfloat16 [768, 2304], P(('dp', 'mp')), may hold values from -0.21875 to 0.21875
- qv_bias: bfloat16 [2, 768], replicated, may hold values from -1.75 to 1.75
- rel_pos_h: bfloat16 [27, 64], replicated, may hold values from -0.625 to 0.625
- rel_pos_w: bfloat16 [27, 64], replicated, may hold values from -0.625 to 0.625
- proj_weight: bfloat16 [768, 768], P(('dp', 'mp')), may hold values from -1.5 to 1.5
- proj_bias: bfloat16 [768], replicated, may hold values from -1.75 to 1.75
- ln2_gain: bfloat16 [768], replicated, may hold values from 0.5 to 1.5
- ln2_bias: bfloat16 [768], replicated, may hold values from -1.75 to 1.75
- fc1_weight: bfloat16 [768, 3072], P(None, 'mp'), may hold values from -0.21875 to 0.21875
- fc1_bias: bfloat16 [3072], P('mp'), may hold values from -1.75 to 1.75
- fc2_weight: bfloat16 [3072, 768], P('mp'), may hold values from -0.109375 to 0.109375
- fc2_bias: bfloat16 [768], replicated, may hold values from -1.75 to 1.75
- keep_mask: int32 [32, 2], P(('dp', 'mp')), may hold values from 0 to 1, as said below
- key_mask: int32 [32, 196], P(('dp', 'mp')), may hold values from 0 to 1, as said below
- out_grad: bfloat16 [6272, 768], P(('dp', 'mp')), may hold values from -6 to 6
Outputs:
- result: bfloat16 [6272, 768], P(('dp', 'mp'))
- tokens_grad: bfloat16 [6272, 768], P(('dp', 'mp'))
- ln1_gain_grad: float32 [768], replicated
- ln1_bias_grad: float32 [768], replicated
- qkv_weight_grad: float32 [768, 2304], P(('dp', 'mp'))
- qv_bias_grad: float32 [2, 768], replicated
- rel_pos_h_grad: float32 [27, 64], replicated
- rel_pos_w_grad: float32 [27, 64], replicated
- proj_weight_grad: float32 [768, 768], P(('dp', 'mp'))
- proj_bias_grad: float32 [768], replicated
- ln2_gain_grad: float32 [768], replicated
- ln2_bias_grad: float32 [768], replicated
- fc1_weight_grad: float32 [768, 3072], P('dp', 'mp')
- fc1_bias_grad: float32 [3072], P(('mp', 'dp'))
- fc2_weight_grad: float32 [3072, 768], P('mp', 'dp')
- fc2_bias_grad: float32 [768], replicated
The draws below stay inside these ranges and needn't reach their ends.
Inputs may be any that keep to these rules, and one draw needn't show every extreme that they name: `keep_mask`: windows come nine to an image, in order, as its 3 x 3 grid of windows (the last image may hold fewer, its first windows in that order); a window's two flags equal those of the other windows of its image. `key_mask`: windows come nine to an image, in order, as its 3 x 3 grid; each window's mask is 1 exactly on a rectangle at its top-left corner, of all 14 rows (columns) in the first two rows (columns) of windows and of 1 to 4 in the last.
All inputs are finite; a program needn't handle non-finite values.
Results may differ from the reference program's by a relative error of at most 0.018.
Values may be sent and summed in bfloat16 or wider, within the bound.
No kernel may reach another device: no remote copies, remote signals or barrier semaphores. Data moves between devices by JAX's collectives and lax.ppermute only.
A program may use at most 128 MiB of HBM per device.

```python
import jax
import jax.numpy as jnp
from jax import lax

D = 768
HEADS = 12
HEAD = 64
FF = 3072
WIN = 14
IMG = 32
WIN_DEV = 1
WINDOWS = 32
TOKENS = 6272


def draw_keep_mask(key, part):
    images = WINDOWS // 9 + 1
    votes = jax.random.randint(jax.random.fold_in(key, 11), (images, 2), 0, 10)
    flags = (votes > 0).astype(jnp.int32)
    return jnp.repeat(flags, 9, axis=0, total_repeat_length=images * 9)[:WINDOWS]


def draw_key_mask(key, part):
    images = WINDOWS // 9 + 1
    sides = jax.random.randint(jax.random.fold_in(key, 23), (images, 2), 2 * WIN + 1, IMG + 1)
    place = jnp.arange(WINDOWS)
    image = place // 9
    spot = place % 9
    height = sides[image, 0] - spot // 3 * WIN
    breadth = sides[image, 1] - spot % 3 * WIN
    cell = jnp.arange(WIN * WIN)
    inside = (cell[None, :] // WIN < height[:, None]) & (cell[None, :] % WIN < breadth[:, None])
    return inside.astype(jnp.int32)


def levels(rng, shape, cuts, smallest, high):
    def one(axis_at, shards_of):
        heights = jax.random.uniform(jax.random.fold_in(jax.random.fold_in(rng, 6), axis_at), (shards_of,), jnp.float32, smallest / len(cuts), high / len(cuts))
        return jnp.repeat(jnp.exp(heights), shape[axis_at] // shards_of).reshape((-1,) + (1,) * (len(shape) - axis_at - 1))

    loudness = one(*cuts[0])
    for cut in cuts[1:]:
        loudness = loudness * one(*cut)
    return loudness


def noise(rng, shape, width, limit, split=(), kind=jnp.bfloat16):
    array = width * jax.random.normal(rng, shape, jnp.float32)
    if split:
        array = array * levels(rng, shape, split, -0.22, 0.18)
    return jnp.clip(array, -limit, limit).astype(kind)


def setup_inputs(seed: int = 0) -> dict:
    key_of = jax.random.split(jax.random.key(seed), 19)
    return {
        "tokens": noise(key_of[0], (TOKENS, D), 1.0, 6.0, ((0, 32),)),
        "ln1_gain": jnp.clip(1.0 + 0.1 * jax.random.normal(key_of[1], (D,), jnp.float32), 0.5, 1.5).astype(jnp.bfloat16),
        "ln1_bias": noise(key_of[2], (D,), 0.3, 1.75),
        "qkv_weight": noise(key_of[3], (D, 3 * D), D ** -0.5, 0.21875, ((0, 32),)),
        "qv_bias": noise(key_of[4], (2, D), 0.3, 1.75),
        "rel_pos_h": noise(key_of[5], (2 * WIN - 1, HEAD), 0.1, 0.625),
        "rel_pos_w": noise(key_of[6], (2 * WIN - 1, HEAD), 0.1, 0.625),
        "proj_weight": noise(key_of[7], (D, D), (D // 48) ** -0.5, 1.5, ((0, 32),)),
        "proj_bias": noise(key_of[8], (D,), 0.3, 1.75),
        "ln2_gain": jnp.clip(1.0 + 0.1 * jax.random.normal(key_of[9], (D,), jnp.float32), 0.5, 1.5).astype(jnp.bfloat16),
        "ln2_bias": noise(key_of[10], (D,), 0.3, 1.75),
        "fc1_weight": noise(key_of[11], (D, FF), D ** -0.5, 0.21875, ((1, 2),)),
        "fc1_bias": noise(key_of[12], (FF,), 0.3, 1.75, ((0, 2),)),
        "fc2_weight": noise(key_of[13], (FF, D), FF ** -0.5, 0.109375, ((0, 2),)),
        "fc2_bias": noise(key_of[14], (D,), 0.3, 1.75),
        "keep_mask": draw_keep_mask(jax.random.fold_in(key_of[18], 71), 0),
        "key_mask": draw_key_mask(jax.random.fold_in(key_of[18], 71), 0),
        "out_grad": noise(key_of[17], (TOKENS, D), 1.0, 6.0, ((0, 32),)),
    }


@jax.custom_vjp
def low(v):
    return lax.optimization_barrier(v.astype(jnp.bfloat16)).astype(jnp.float32)

@jax.custom_vjp
def low_back(v):
    return v

def low_keep(v):
    return (low(v), None)

def low_pass(kept, grad):
    return (grad,)

def back_keep(v):
    return (v, None)

def back_low(kept, grad):
    return (low(grad),)
low.defvjp(low_keep, low_pass)
low_back.defvjp(back_keep, back_low)

def both_ways(value):
    return low(low_back(value))

def norm_rows(rows, gain, shift):
    center = rows - lax.optimization_barrier(jnp.mean(rows, axis=-1, keepdims=True))
    spread = lax.optimization_barrier(jnp.mean(center * center, axis=-1, keepdims=True))
    return center * lax.rsqrt(spread + 1e-06) * gain + shift

def rel_table(table):
    index = (jnp.arange(WIN)[:, None] - jnp.arange(WIN)[None, :] + WIN - 1).astype(jnp.int32)
    return table[index]

def block(params, rows_in, mask, keep):
    gain_one, shift_one, qkv_w, qv_b, rel_h, rel_w, proj_w, proj_b, gain_two, shift_two, up_w, up_b, down_w, down_b = params
    highest = lax.Precision.HIGHEST
    windows_here = mask.shape[0]
    window_area = WIN * WIN
    normed_one = low(norm_rows(rows_in, gain_one, shift_one))
    bias_full = jnp.concatenate([qv_b[0], jnp.zeros((D,), jnp.float32), qv_b[1]])
    qkv = both_ways(jnp.dot(normed_one, qkv_w, precision=highest) + bias_full)
    blocks = qkv.reshape(windows_here, WIN, WIN, 3, HEADS, HEAD)
    queries, key_part, values = (blocks[:, :, :, 0], blocks[:, :, :, 1], blocks[:, :, :, 2])
    scores = jnp.einsum('nabhc,nxyhc->nhabxy', queries, key_part, precision=highest) * HEAD ** (-0.5)
    part_h = jnp.einsum('nabhc,axc->nhabx', queries, rel_table(rel_h), precision=highest)
    part_w = jnp.einsum('nabhc,byc->nhaby', queries, rel_table(rel_w), precision=highest)
    scores = scores + part_h[..., :, None] + part_w[..., None, :]
    scores = low_back(scores.reshape(windows_here, HEADS, window_area, window_area))
    scores = jnp.where(mask[:, None, None, :] > 0, scores, -1000000000.0)
    row_top = lax.optimization_barrier(jnp.max(scores, axis=-1, keepdims=True))
    expo = jnp.exp(scores - row_top)
    attn_probs = low(expo / lax.optimization_barrier(jnp.sum(expo, axis=-1, keepdims=True)))
    flat_values = values.reshape(windows_here, window_area, HEADS, HEAD)
    attended = jnp.einsum('nhqk,nkhc->nqhc', attn_probs, flat_values, precision=highest)
    attended = both_ways(attended.reshape(windows_here * window_area, D))
    branch = low_back(jnp.dot(attended, proj_w, precision=highest) + proj_b)
    keep_rows = jnp.repeat(keep.astype(jnp.float32), window_area, axis=0) / 0.9
    middle = rows_in + keep_rows[:, 0:1] * branch
    normed_two = low(norm_rows(middle, gain_two, shift_two))
    hidden = low_back(jnp.dot(normed_two, up_w, precision=highest) + up_b)
    activated = low(jax.nn.gelu(hidden, approximate=False))
    feed_out = low_back(jnp.dot(activated, down_w, precision=highest) + down_b)
    return middle + keep_rows[:, 1:2] * feed_out

def reference(tokens, ln1_gain, ln1_bias, qkv_weight, qv_bias, rel_pos_h, rel_pos_w, proj_weight, proj_bias, ln2_gain, ln2_bias, fc1_weight, fc1_bias, fc2_weight, fc2_bias, keep_mask, key_mask, out_grad):
    params = tuple((item.astype(jnp.float32) for item in (ln1_gain, ln1_bias, qkv_weight, qv_bias, rel_pos_h, rel_pos_w, proj_weight, proj_bias, ln2_gain, ln2_bias, fc1_weight, fc1_bias, fc2_weight, fc2_bias)))
    groups = WINDOWS // WIN_DEV
    group_rows = WIN_DEV * WIN * WIN
    rows_in = tokens.astype(jnp.float32).reshape(groups, group_rows, D)
    masks = key_mask.reshape(groups, WIN_DEV, WIN * WIN)
    keeps = keep_mask.reshape(groups, WIN_DEV, 2)

    def whole(params_now, rows_now):
        step_fn = jax.checkpoint(lambda rows_part, mask_part, keep_part: block(params_now, rows_part, mask_part, keep_part))
        return lax.map(lambda item: step_fn(item[0], item[1], item[2]), (rows_now, masks, keeps))
    outputs, pull = jax.vjp(whole, params, rows_in)
    grads, rows_grad = pull(out_grad.astype(jnp.float32).reshape(groups, group_rows, D))
    return (outputs.reshape(TOKENS, D).astype(jnp.bfloat16), rows_grad.reshape(TOKENS, D).astype(jnp.bfloat16), grads[0], grads[1], grads[2], grads[3], grads[4], grads[5], grads[6], grads[7], grads[8], grads[9], grads[10], grads[11], grads[12], grads[13])
```

```python
from functools import partial

import jax
import jax.numpy as jnp
from jax import lax
from jax.sharding import PartitionSpec as P

D = 768
HEADS = 12
HEAD = 64
WIN = 14


def dp_pairs(count, dz=0, dy=0, dc=0):
    depth = count // 4
    pairs = []
    for place in range(count):
        z, y, c = place // 4, place // 2 % 2, place % 2
        pairs.append((place, (z + dz) % depth * 4 + (y + dy) % 2 * 2 + (c + dc) % 2))
    return pairs


def move_z(value, step):
    count = lax.axis_size("dp")
    return lax.ppermute(value, "dp", dp_pairs(count, dz=step))


def move_y(value, step=1):
    return lax.ppermute(value, "dp", dp_pairs(lax.axis_size("dp"), dy=step))


def move_c(value, step=1):
    return lax.ppermute(value, "dp", dp_pairs(lax.axis_size("dp"), dc=step))


def move_x(value, step=1):
    count = lax.axis_size("mp")
    return lax.ppermute(value, "mp", [(i, (i + step) % count) for i in range(count)])


def pick(value, index, axis):
    return lax.dynamic_index_in_dim(value, index, axis, keepdims=False)


def in_order(blocks, index):
    count = len(blocks)
    if count == 2:
        first, second = blocks
        swap = index == 1
        return jnp.stack([jnp.where(swap, second, first), jnp.where(swap, first, second)])
    twice = jnp.stack([blocks[-j % count] for j in range(count)] * 2)
    return lax.dynamic_slice_in_dim(twice, count - index, count, axis=0)


def places():
    dp = lax.axis_index("dp")
    return dp // 4, dp // 2 % 2, dp % 2, lax.axis_index("mp")


def gather_rows(shard, chunks):
    z, y, c, x = places()
    depth, wide = lax.axis_size("dp") // 4, lax.axis_size("mp")
    rows, columns = shard.shape
    width = columns // chunks
    lines = []
    for k in range(chunks):
        part = shard[:, k * width : (k + 1) * width]
        lines.append(in_order([part] + [move_z(part, s) for s in range(1, depth)], z))
    outs = []
    for line in lines:
        half = width // 2
        along_x = [line] + [move_x(line, s) for s in range(1, wide)]
        along_y = move_y(line)
        left = [move_y(b[..., :half]) for b in along_x[1:]]
        right = [move_x(along_y[..., half:], s) for s in range(1, wide)]
        far = [along_y] + [jnp.concatenate([p, q], -1) for p, q in zip(left, right)]
        both = in_order([in_order(along_x, x), in_order(far, x)], y)
        both = in_order([both, move_c(both)], c)
        outs.append(both.transpose(3, 1, 0, 2, 4, 5).reshape(-1, width))
    return jnp.concatenate(outs, -1)


def scatter_axis(value, axis, size, index, move):
    total = pick(value, index, axis).astype(jnp.float32)
    for step in range(1, size):
        block = pick(value, (index + step) % size, axis).astype(jnp.bfloat16)
        total = total + move(block, step).astype(jnp.float32)
    return total


def scatter_rows(grad):
    z, y, c, x = places()
    depth, wide = lax.axis_size("dp") // 4, lax.axis_size("mp")
    columns = grad.shape[1]
    blocks = grad.reshape(depth, 2, 2, wide, -1, columns)
    blocks = scatter_axis(blocks, 2, 2, c, move_c)
    half = columns // 2
    first, second = blocks[..., :half], blocks[..., half:]
    first = scatter_axis(first, 2, wide, x, move_x)
    second = scatter_axis(second, 1, 2, y, move_y)
    first = scatter_axis(first, 1, 2, y, move_y)
    second = scatter_axis(second, 1, wide, x, move_x)
    first = scatter_axis(first, 0, depth, z, move_z)
    second = scatter_axis(second, 0, depth, z, move_z)
    return jnp.concatenate([first, second], -1)


def scatter_dp(grad):
    z, y, c, x = places()
    depth = lax.axis_size("dp") // 4
    blocks = grad.reshape(depth, 2, 2, -1, grad.shape[1])
    blocks = scatter_axis(blocks, 2, 2, c, move_c)
    blocks = scatter_axis(blocks, 1, 2, y, move_y)
    return scatter_axis(blocks, 0, depth, z, move_z)


def sum_all(parts):
    depth, wide = lax.axis_size("dp") // 4, lax.axis_size("mp")
    flat = jnp.concatenate([p.reshape(-1) for p in parts])
    size = flat.shape[0]
    flat = jnp.pad(flat, (0, -size % 1024)).reshape(-1, 128)
    flat = flat + move_c(flat)
    flat = sum([move_x(flat, s) for s in range(1, wide)], flat)
    flat = flat + move_y(flat)
    flat = sum([move_z(flat, s) for s in range(1, depth)], flat)
    flat = flat.reshape(-1)
    outs, at = [], 0
    for p in parts:
        outs.append(flat[at : at + p.size].reshape(p.shape))
        at += p.size
    return outs


def sum_back(partial_rows, wide):
    blocks = partial_rows.reshape(wide, -1, partial_rows.shape[-1])
    total = blocks[0]
    for step in range(1, wide):
        total = total + move_x(blocks[step].astype(jnp.bfloat16), -step).astype(jnp.float32)
    return total


def norm_parts(rows_in, gain, shift):
    center = rows_in - jnp.mean(rows_in, axis=-1, keepdims=True)
    factor = lax.rsqrt(jnp.mean(center * center, axis=-1, keepdims=True) + 1e-06)
    unit = center * factor
    return (unit * gain + shift, unit, factor)


def norm_back(grad, unit, factor, gain):
    inner = grad * gain
    return factor * (
        inner
        - jnp.mean(inner, axis=-1, keepdims=True)
        - unit * jnp.mean(inner * unit, axis=-1, keepdims=True)
    )


def shift_table(width):
    first = jnp.arange(width)[:, None, None]
    second = jnp.arange(width)[None, :, None]
    offset = jnp.arange(2 * width - 1)[None, None, :]
    return (first - second + width - 1 == offset).astype(jnp.float32)


def attn_scores(queries, key_part, tab_h, tab_w, mask):
    windows_here = queries.shape[0]
    scores = jnp.einsum(
        "nabhc,nxyhc->nhabxy", queries, key_part, preferred_element_type=jnp.float32
    ) * HEAD ** (-0.5)
    part_h = jnp.einsum("nabhc,axc->nhabx", queries, tab_h, preferred_element_type=jnp.float32)
    part_w = jnp.einsum("nabhc,byc->nhaby", queries, tab_w, preferred_element_type=jnp.float32)
    scores = scores + part_h[..., :, None] + part_w[..., None, :]
    scores = scores.reshape(windows_here, HEADS, WIN * WIN, WIN * WIN)
    return jnp.where(mask[:, None, None, :] > 0, scores, -1000000000.0)


def per_device(
    tokens,
    ln1_gain,
    ln1_bias,
    qkv_weight,
    qv_bias,
    rel_pos_h,
    rel_pos_w,
    proj_weight,
    proj_bias,
    ln2_gain,
    ln2_bias,
    fc1_weight,
    fc1_bias,
    fc2_weight,
    fc2_bias,
    keep_mask,
    key_mask,
    out_grad,
):
    f32 = jnp.float32
    bf16 = jnp.bfloat16
    highest = lax.Precision.HIGHEST
    windows_here = key_mask.shape[0]
    window_area = WIN * WIN
    local_rows = tokens.shape[0]
    wide = lax.axis_size("mp")
    weights = gather_rows(jnp.concatenate([qkv_weight, proj_weight], -1), 2)
    qkv_full, proj_full = weights[:, : 3 * D], weights[:, 3 * D :]
    gain_one = ln1_gain.astype(f32)
    gain_two = ln2_gain.astype(f32)
    residual = tokens.astype(f32)
    normed_in, unit_one, factor_one = norm_parts(residual, gain_one, ln1_bias.astype(f32))
    normed_one = normed_in.astype(bf16)
    qv_wide = qv_bias.astype(f32)
    bias_full = jnp.concatenate([qv_wide[0], jnp.zeros((D,), f32), qv_wide[1]])
    qkv = (jnp.dot(normed_one, qkv_full, preferred_element_type=f32) + bias_full).astype(bf16)
    blocks = qkv.reshape(windows_here, WIN, WIN, 3, HEADS, HEAD)
    queries, key_part, values = (blocks[:, :, :, 0], blocks[:, :, :, 1], blocks[:, :, :, 2])
    onehot = shift_table(WIN)
    tab_h = jnp.einsum("axr,rc->axc", onehot, rel_pos_h.astype(f32), precision=highest)
    tab_w = jnp.einsum("axr,rc->axc", onehot, rel_pos_w.astype(f32), precision=highest)
    scores = attn_scores(queries, key_part, tab_h.astype(bf16), tab_w.astype(bf16), key_mask)
    row_top = jnp.max(scores, axis=-1, keepdims=True)
    expo = jnp.exp(scores - row_top)
    row_total = jnp.sum(expo, axis=-1, keepdims=True)
    log_total = row_top + jnp.log(row_total)
    attn_probs = expo / row_total
    flat_values = values.reshape(windows_here, window_area, HEADS, HEAD)
    attended = jnp.einsum(
        "nhqk,nkhc->nqhc", attn_probs.astype(bf16), flat_values, preferred_element_type=f32
    )
    attended = attended.reshape(local_rows, D).astype(bf16)
    branch = jnp.dot(attended, proj_full, preferred_element_type=f32) + proj_bias.astype(f32)
    keep_rows = jnp.repeat(keep_mask.astype(f32), window_area, axis=0) / 0.9
    middle = residual + keep_rows[:, 0:1] * branch
    normed_mid, unit_two, factor_two = norm_parts(middle, gain_two, ln2_bias.astype(f32))
    normed_two = normed_mid.astype(bf16)
    activate = partial(jax.nn.gelu, approximate=False)
    gathered = jnp.concatenate([normed_two] + [move_x(normed_two, s) for s in range(1, wide)])
    hidden = jnp.dot(gathered, fc1_weight, preferred_element_type=f32) + fc1_bias.astype(f32)
    activated_f, gelu_pull = jax.vjp(activate, hidden)
    activated = activated_f.astype(bf16)
    feed_out = sum_back(jnp.dot(activated, fc2_weight, preferred_element_type=f32), wide)
    feed_out = feed_out + fc2_bias.astype(f32)
    result = (middle + keep_rows[:, 1:2] * feed_out).astype(bf16)
    grad_out = out_grad.astype(f32)
    grad_feed = (keep_rows[:, 1:2] * grad_out).astype(bf16)
    down_bias_grad = jnp.sum(grad_feed, axis=0, dtype=f32)
    grad_gathered = jnp.concatenate([grad_feed] + [move_x(grad_feed, s) for s in range(1, wide)])
    grad_act = jnp.dot(grad_gathered, fc2_weight.T, preferred_element_type=f32)
    grad_hidden = gelu_pull(grad_act)[0].astype(bf16)
    down_grad = jnp.dot(grad_gathered.T, activated, preferred_element_type=f32)
    up_grad = jnp.dot(gathered.T, grad_hidden, preferred_element_type=f32)
    up_bias_grad = jnp.sum(grad_hidden, axis=0, dtype=f32)
    grad_second = sum_back(jnp.dot(grad_hidden, fc1_weight.T, preferred_element_type=f32), wide)
    up_grad = scatter_dp(up_grad)
    down_grad = scatter_dp(down_grad).T
    up_bias_all = lax.dynamic_update_slice(
        jnp.zeros((wide, up_bias_grad.shape[0]), f32), up_bias_grad[None], (lax.axis_index("mp"), 0)
    )
    gain_two_grad = jnp.sum(grad_second * unit_two, axis=0)
    shift_two_grad = jnp.sum(grad_second, axis=0)
    grad_middle = grad_out + norm_back(grad_second, unit_two, factor_two, gain_two)
    grad_branch = (keep_rows[:, 0:1] * grad_middle).astype(bf16)
    proj_bias_grad = jnp.sum(grad_branch, axis=0, dtype=f32)
    proj_grad = jnp.dot(attended.T, grad_branch, preferred_element_type=f32)
    grad_att = jnp.dot(grad_branch, proj_full.T, preferred_element_type=f32).astype(bf16)
    grad_att = grad_att.reshape(windows_here, window_area, HEADS, HEAD)
    scores = attn_scores(queries, key_part, tab_h.astype(bf16), tab_w.astype(bf16), key_mask)
    attn_probs = jnp.exp(scores - log_total)
    values_grad = jnp.einsum(
        "nhqk,nqhc->nkhc", attn_probs.astype(bf16), grad_att, preferred_element_type=f32
    )
    probs_grad = jnp.einsum("nqhc,nkhc->nhqk", grad_att, flat_values, preferred_element_type=f32)
    score_grad = attn_probs * (
        probs_grad - jnp.sum(attn_probs * probs_grad, axis=-1, keepdims=True)
    )
    grid_grad = score_grad.astype(bf16).reshape(windows_here, HEADS, WIN, WIN, WIN, WIN)
    row_grad = jnp.sum(grid_grad, axis=5, dtype=f32)
    col_grad = jnp.sum(grid_grad, axis=4, dtype=f32)
    queries_grad = jnp.einsum(
        "nhabxy,nxyhc->nabhc", grid_grad, key_part, preferred_element_type=f32
    ) * HEAD ** (-0.5)
    queries_grad = queries_grad + jnp.einsum("nhabx,axc->nabhc", row_grad, tab_h, precision=highest)
    queries_grad = queries_grad + jnp.einsum("nhaby,byc->nabhc", col_grad, tab_w, precision=highest)
    keys_grad = jnp.einsum(
        "nhabxy,nabhc->nxyhc", grid_grad, queries, preferred_element_type=f32
    ) * HEAD ** (-0.5)
    query_wide = queries.astype(f32)
    tabh_grad = jnp.einsum("nhabx,nabhc->axc", row_grad, query_wide, precision=highest)
    tabw_grad = jnp.einsum("nhaby,nabhc->byc", col_grad, query_wide, precision=highest)
    relh_grad = jnp.einsum("axr,axc->rc", onehot, tabh_grad, precision=highest)
    relw_grad = jnp.einsum("axr,axc->rc", onehot, tabw_grad, precision=highest)
    values_grad = values_grad.reshape(windows_here, WIN, WIN, HEADS, HEAD)
    qkv_grad = (
        jnp.stack([queries_grad, keys_grad, values_grad], axis=3)
        .astype(bf16)
        .reshape(local_rows, 3 * D)
    )
    qv_grad = jnp.stack(
        [
            jnp.sum(qkv_grad[:, :D], axis=0, dtype=f32),
            jnp.sum(qkv_grad[:, 2 * D :], axis=0, dtype=f32),
        ]
    )
    qkv_w_grad = jnp.dot(normed_one.T, qkv_grad, preferred_element_type=f32)
    grad_first = jnp.dot(qkv_grad, qkv_full.T, preferred_element_type=f32)
    gain_one_grad = jnp.sum(grad_first * unit_one, axis=0)
    shift_one_grad = jnp.sum(grad_first, axis=0)
    grad_input = grad_middle + norm_back(grad_first, unit_one, factor_one, gain_one)
    both_grad = scatter_rows(jnp.concatenate([qkv_w_grad, proj_grad], -1))
    qkv_w_grad, proj_grad = both_grad[:, : 3 * D], both_grad[:, 3 * D :]
    (
        gain_one_grad,
        shift_one_grad,
        qv_grad,
        relh_grad,
        relw_grad,
        proj_bias_grad,
        gain_two_grad,
        shift_two_grad,
        down_bias_grad,
        up_bias_all,
    ) = sum_all(
        (
            gain_one_grad,
            shift_one_grad,
            qv_grad,
            relh_grad,
            relw_grad,
            proj_bias_grad,
            gain_two_grad,
            shift_two_grad,
            down_bias_grad,
            up_bias_all,
        )
    )
    up_bias_grad = pick(
        pick(up_bias_all, lax.axis_index("mp"), 0).reshape(lax.axis_size("dp"), -1),
        lax.axis_index("dp"),
        0,
    )
    return (
        result,
        grad_input.astype(bf16),
        gain_one_grad,
        shift_one_grad,
        qkv_w_grad,
        qv_grad,
        relh_grad,
        relw_grad,
        proj_grad,
        proj_bias_grad,
        gain_two_grad,
        shift_two_grad,
        up_grad,
        up_bias_grad,
        down_grad,
        down_bias_grad,
    )


def solution(mesh):
    in_specs = (
        P(("dp", "mp"), None),
        P(),
        P(),
        P(("dp", "mp"), None),
        P(),
        P(),
        P(),
        P(("dp", "mp"), None),
        P(),
        P(),
        P(),
        P(None, "mp"),
        P("mp"),
        P("mp", None),
        P(),
        P(("dp", "mp"), None),
        P(("dp", "mp"), None),
        P(("dp", "mp"), None),
    )
    out_specs = (
        P(("dp", "mp"), None),
        P(("dp", "mp"), None),
        P(),
        P(),
        P(("dp", "mp"), None),
        P(),
        P(),
        P(),
        P(("dp", "mp"), None),
        P(),
        P(),
        P(),
        P("dp", "mp"),
        P(("mp", "dp")),
        P("mp", "dp"),
        P(),
    )
    return jax.shard_map(
        per_device, mesh=mesh, in_specs=in_specs, out_specs=out_specs, check_vma=False
    )
```

```python
from functools import partial

import jax
import jax.numpy as jnp
from jax import lax
from jax.experimental import pallas as pl
from jax.experimental.pallas import tpu as pltpu
from jax.sharding import PartitionSpec as P

D = 768
HEADS = 12
HEAD = 64
WIN = 14
ROW = 16
R = WIN * ROW
PAIRS = HEADS // 2
LANES = 128
F32 = jnp.float32
BF16 = jnp.bfloat16
VMEM = pl.BlockSpec(memory_space=pltpu.VMEM)
SMEM = pl.BlockSpec(memory_space=pltpu.SMEM)
LIMIT = 56 * 2**20


def dp_pairs(count, dz=0, dy=0, dc=0):
    depth = count // 4
    pairs = []
    for place in range(count):
        z, y, c = place // 4, place // 2 % 2, place % 2
        pairs.append((place, (z + dz) % depth * 4 + (y + dy) % 2 * 2 + (c + dc) % 2))
    return pairs


def move_z(value, step):
    count = lax.axis_size("dp")
    return lax.ppermute(value, "dp", dp_pairs(count, dz=step))


def move_y(value, step=1):
    return lax.ppermute(value, "dp", dp_pairs(lax.axis_size("dp"), dy=step))


def move_c(value, step=1):
    return lax.ppermute(value, "dp", dp_pairs(lax.axis_size("dp"), dc=step))


def move_x(value, step=1):
    count = lax.axis_size("mp")
    return lax.ppermute(value, "mp", [(i, (i + step) % count) for i in range(count)])


def pick(value, index, axis):
    return lax.dynamic_index_in_dim(value, index, axis, keepdims=False)


def in_order(blocks, index):
    count = len(blocks)
    if count == 2:
        first, second = blocks
        swap = index == 1
        return jnp.stack([jnp.where(swap, second, first), jnp.where(swap, first, second)])
    twice = jnp.stack([blocks[-j % count] for j in range(count)] * 2)
    return lax.dynamic_slice_in_dim(twice, count - index, count, axis=0)


def places():
    dp = lax.axis_index("dp")
    return dp // 4, dp // 2 % 2, dp % 2, lax.axis_index("mp")


def gather_rows(shard, chunks):
    z, y, c, x = places()
    depth, wide = lax.axis_size("dp") // 4, lax.axis_size("mp")
    rows, columns = shard.shape
    width = columns // chunks
    lines = []
    for k in range(chunks):
        part = shard[:, k * width : (k + 1) * width]
        lines.append(in_order([part] + [move_z(part, s) for s in range(1, depth)], z))
    outs = []
    for line in lines:
        half = width // 2
        along_x = [line] + [move_x(line, s) for s in range(1, wide)]
        along_y = move_y(line)
        left = [move_y(b[..., :half]) for b in along_x[1:]]
        right = [move_x(along_y[..., half:], s) for s in range(1, wide)]
        far = [along_y] + [jnp.concatenate([p, q], -1) for p, q in zip(left, right)]
        both = in_order([in_order(along_x, x), in_order(far, x)], y)
        both = in_order([both, move_c(both)], c)
        outs.append(both.transpose(3, 1, 0, 2, 4, 5).reshape(-1, width))
    return jnp.concatenate(outs, -1)


def scatter_axis(value, axis, size, index, move):
    total = pick(value, index, axis).astype(F32)
    for step in range(1, size):
        block = pick(value, (index + step) % size, axis).astype(BF16)
        total = total + move(block, step).astype(F32)
    return total


def scatter_all(keep, send):
    z, y, _, x = places()
    depth, wide = lax.axis_size("dp") // 4, lax.axis_size("mp")
    columns = keep.shape[1]
    blocks = keep.astype(F32) + move_c(send).astype(F32)
    blocks = blocks.reshape(depth, 2, wide, -1, columns)
    half = columns // 2
    first, second = blocks[..., :half], blocks[..., half:]
    first = scatter_axis(first, 2, wide, x, move_x)
    second = scatter_axis(second, 1, 2, y, move_y)
    first = scatter_axis(first, 1, 2, y, move_y)
    second = scatter_axis(second, 1, wide, x, move_x)
    first = scatter_axis(first, 0, depth, z, move_z)
    second = scatter_axis(second, 0, depth, z, move_z)
    return jnp.concatenate([first, second], -1)


def scatter_dp(keep, send):
    z, y, _, _ = places()
    depth = lax.axis_size("dp") // 4
    blocks = keep.astype(F32) + move_c(send).astype(F32)
    blocks = blocks.reshape(depth, 2, -1, keep.shape[1])
    blocks = scatter_axis(blocks, 1, 2, y, move_y)
    return scatter_axis(blocks, 0, depth, z, move_z)


def sum_all(parts):
    depth, wide = lax.axis_size("dp") // 4, lax.axis_size("mp")
    flat = jnp.concatenate([p.reshape(-1) for p in parts])
    size = flat.shape[0]
    flat = jnp.pad(flat, (0, -size % 1024)).reshape(-1, 128)
    flat = flat + move_c(flat)
    flat = sum([move_x(flat, s) for s in range(1, wide)], flat)
    flat = flat + move_y(flat)
    flat = sum([move_z(flat, s) for s in range(1, depth)], flat)
    flat = flat.reshape(-1)
    outs, at = [], 0
    for p in parts:
        outs.append(flat[at : at + p.size].reshape(p.shape))
        at += p.size
    return outs


def dot_nn(a, b):
    return lax.dot_general(a, b, (((1,), (0,)), ((), ())), preferred_element_type=F32)


def dot_nt(a, b):
    return lax.dot_general(a, b, (((1,), (1,)), ((), ())), preferred_element_type=F32)


def dot_tn(a, b):
    return lax.dot_general(a, b, (((0,), (0,)), ((), ())), preferred_element_type=F32)


def norm_parts(rows_in):
    center = rows_in - jnp.mean(rows_in, axis=-1, keepdims=True)
    factor = lax.rsqrt(jnp.mean(center * center, axis=-1, keepdims=True) + 1e-06)
    return center * factor, factor


def norm_back(grad, unit, factor, gain):
    inner = grad * gain
    return factor * (
        inner
        - jnp.mean(inner, axis=-1, keepdims=True)
        - unit * jnp.mean(inner * unit, axis=-1, keepdims=True)
    )


def lane_ids():
    return lax.broadcasted_iota(jnp.int32, (R, LANES), 1)


def row_masks():
    lane = lane_ids() % HEAD
    key = lax.broadcasted_iota(jnp.int32, (R, LANES), 0)
    spot = lane % ROW
    part = lane // ROW % 2
    here = jnp.where(part == 0, key // ROW, key % ROW)
    return (spot == here).astype(F32)


def query_offsets(table, base):
    lane = lax.broadcasted_iota(jnp.int32, (ROW, LANES), 1)
    in_h = (lane >= base) & (lane < base + ROW)
    in_w = (lane >= base + ROW) & (lane < base + 2 * ROW)
    outs = []
    for a in range(WIN):
        group = table[a * ROW : (a + 1) * ROW]
        at_h = pltpu.roll(group, (base - 13 + a) % LANES, 1)
        at_w = pltpu.roll(group, (base + ROW - HEAD - 13) % LANES, 1, stride=1, stride_axis=0)
        both = jnp.where(in_h, at_h, jnp.where(in_w, at_w, 0.0))
        high = both.astype(BF16).astype(F32)
        outs.append(high + pltpu.roll(both - high, 2 * ROW, 1))
    return jnp.concatenate(outs, axis=0)


def offset_grads(grad, base):
    lane = lax.broadcasted_iota(jnp.int32, (ROW, LANES), 1)
    in_h = (lane >= base) & (lane < base + ROW)
    in_w = (lane >= base + ROW) & (lane < base + 2 * ROW)
    outs = []
    for a in range(WIN):
        group = grad[a * ROW : (a + 1) * ROW]
        from_h = pltpu.roll(jnp.where(in_h, group, 0.0), (13 - a - base) % LANES, 1)
        flipped = jnp.where(in_w, group, 0.0)
        from_w = jnp.concatenate(
            [
                pltpu.roll(flipped[b : b + 1], (HEAD + 13 - b - base - ROW) % LANES, 1)
                for b in range(ROW)
            ],
            axis=0,
        )
        outs.append(from_h + from_w)
    return jnp.concatenate(outs, axis=0)


def augmented(q2, k2, tables, ones):
    lane = lane_ids()
    left = lane < HEAD
    q2 = q2.astype(F32)
    k2 = k2.astype(F32)
    products = dot_nn(q2.astype(BF16), tables)
    heads = []
    for side in range(2):
        offsets = query_offsets(products[:, side * LANES : (side + 1) * LANES], HEAD * (1 - side))
        mine = left if side == 0 else ~left
        heads.append(
            (
                jnp.where(mine, q2 * HEAD**-0.5, offsets).astype(BF16),
                jnp.where(mine, k2, ones).astype(BF16),
            )
        )
    return heads


def attend_kernel(
    x_ref, w_ref, gain1_ref, bias1_ref, qkvb_ref, table_ref, projb_ref, gain2_ref, bias2_ref, fill_ref, keep_ref,
    a1_ref, qkv_ref, p_ref, o_ref, mid_ref, a2_ref,
):
    x = x_ref[...].astype(F32)
    unit, _ = norm_parts(x)
    a1 = (unit * gain1_ref[...] + bias1_ref[...]).astype(BF16)
    a1_ref[...] = a1
    qkv_ref[...] = (dot_nn(a1, w_ref[:, : 3 * D]) + qkvb_ref[...]).astype(BF16)
    ones = row_masks()
    left = lane_ids() < HEAD
    fill = fill_ref[...]
    for pair in range(PAIRS):
        at = pair * LANES
        q2 = qkv_ref[:, at : at + LANES]
        k2 = qkv_ref[:, D + at : D + at + LANES]
        v2 = qkv_ref[:, 2 * D + at : 2 * D + at + LANES]
        outs = []
        for side, (q_aug, k_aug) in enumerate(augmented(q2, k2, table_ref[...], ones)):
            scores = dot_nt(q_aug, k_aug)
            scores = jnp.where(fill < 0.0, fill, scores)
            expo = jnp.exp(scores - jnp.max(scores, axis=-1, keepdims=True))
            probs = (expo / jnp.sum(expo, axis=-1, keepdims=True)).astype(BF16)
            p_ref[2 * pair + side] = probs
            outs.append(dot_nn(probs, v2))
        o_ref[:, at : at + LANES] = jnp.where(left, outs[0], outs[1]).astype(BF16)
    branch = dot_nn(o_ref[...], w_ref[:, 3 * D :]) + projb_ref[...]
    middle = x + keep_ref[0] * branch
    mid_ref[...] = middle
    unit, _ = norm_parts(middle)
    a2_ref[...] = (unit * gain2_ref[...] + bias2_ref[...]).astype(BF16)


def attend(*args):
    shape = jax.ShapeDtypeStruct
    return pl.pallas_call(
        attend_kernel,
        in_specs=[VMEM] * 10 + [SMEM],
        out_specs=[VMEM] * 6,
        out_shape=[
            shape((R, D), BF16),
            shape((R, 3 * D), BF16),
            shape((HEADS, R, R), BF16),
            shape((R, D), BF16),
            shape((R, D), F32),
            shape((R, D), BF16),
        ],
        compiler_params=pltpu.CompilerParams(vmem_limit_bytes=LIMIT),
        cost_estimate=pl.CostEstimate(flops=2 * R * D * 4 * D, bytes_accessed=12 * 2**20, transcendentals=HEADS * R * R),
    )(*args)


def attend_back_kernel(
    own_ref, got_ref, mid_ref, grad_ref, x_ref, w_ref, qkv_ref, p_ref, table_ref, gain1_ref, gain2_ref, keep_ref,
    dy_ref, dqkv_ref, dx_ref, gain1_out, bias1_out, qkvb_out, table_out, projb_out, gain2_out, bias2_out,
    do_ref,
):
    da2 = own_ref[...] + got_ref[...]
    unit, factor = norm_parts(mid_ref[...])
    gain2_out[...] = jnp.sum(da2 * unit, axis=0, keepdims=True)
    bias2_out[...] = jnp.sum(da2, axis=0, keepdims=True)
    dmid = grad_ref[...].astype(F32) + norm_back(da2, unit, factor, gain2_ref[...])
    dy = (keep_ref[0] * dmid).astype(BF16)
    dy_ref[...] = dy
    projb_out[...] = jnp.sum(dy.astype(F32), axis=0, keepdims=True)
    do_ref[...] = dot_nt(dy, w_ref[:, 3 * D :]).astype(BF16)
    ones = row_masks()
    left = lane_ids() < HEAD
    tables = table_ref[...]
    table_grad = jnp.zeros((LANES, 2 * LANES), F32)
    for pair in range(PAIRS):
        at = pair * LANES
        q2 = qkv_ref[:, at : at + LANES].astype(F32)
        k2 = qkv_ref[:, D + at : D + at + LANES].astype(F32)
        v2 = qkv_ref[:, 2 * D + at : 2 * D + at + LANES]
        do2 = do_ref[:, at : at + LANES].astype(F32)
        dq2 = jnp.zeros((R, LANES), F32)
        dk2 = jnp.zeros((R, LANES), F32)
        dv2 = jnp.zeros((R, LANES), F32)
        offsets = []
        for side in range(2):
            mine = left if side == 0 else ~left
            probs = p_ref[2 * pair + side]
            do_mine = jnp.where(mine, do2, 0.0).astype(BF16)
            dv2 = dv2 + dot_tn(probs, do_mine)
            dp = dot_nt(do_mine, v2)
            wide = probs.astype(F32)
            ds = (wide * (dp - jnp.sum(wide * dp, axis=-1, keepdims=True))).astype(BF16)
            k_aug = jnp.where(mine, k2, ones).astype(BF16)
            dq_aug = dot_nn(ds, k_aug)
            dq2 = jnp.where(mine, dq_aug, dq2)
            offsets.append(offset_grads(dq_aug, HEAD * (1 - side)))
            dk2 = dk2 + dot_tn(ds, jnp.where(mine, q2, 0.0).astype(BF16))
        spread = jnp.concatenate(offsets, axis=1).astype(BF16)
        dq2 = dq2 * HEAD**-0.5 + dot_nt(spread, tables)
        table_grad = table_grad + dot_tn(q2.astype(BF16), spread)
        dqkv_ref[:, at : at + LANES] = dq2.astype(BF16)
        dqkv_ref[:, D + at : D + at + LANES] = (dk2 * HEAD**-0.5).astype(BF16)
        dqkv_ref[:, 2 * D + at : 2 * D + at + LANES] = dv2.astype(BF16)
    table_out[...] = table_grad
    qkvb_out[...] = jnp.sum(dqkv_ref[...].astype(F32), axis=0, keepdims=True)
    da1 = dot_nt(dqkv_ref[...], w_ref[:, : 3 * D])
    unit, factor = norm_parts(x_ref[...].astype(F32))
    gain1_out[...] = jnp.sum(da1 * unit, axis=0, keepdims=True)
    bias1_out[...] = jnp.sum(da1, axis=0, keepdims=True)
    dx_ref[...] = (dmid + norm_back(da1, unit, factor, gain1_ref[...])).astype(BF16)


def attend_back(*args):
    shape = jax.ShapeDtypeStruct
    return pl.pallas_call(
        attend_back_kernel,
        in_specs=[VMEM] * 11 + [SMEM],
        out_specs=[VMEM] * 10,
        out_shape=[
            shape((R, D), BF16),
            shape((R, 3 * D), BF16),
            shape((R, D), BF16),
            shape((1, D), F32),
            shape((1, D), F32),
            shape((1, 3 * D), F32),
            shape((LANES, 2 * LANES), F32),
            shape((1, D), F32),
            shape((1, D), F32),
            shape((1, D), F32),
        ],
        scratch_shapes=[pltpu.VMEM((R, D), BF16)],
        compiler_params=pltpu.CompilerParams(vmem_limit_bytes=LIMIT),
        cost_estimate=pl.CostEstimate(flops=2 * R * D * 6 * D, bytes_accessed=14 * 2**20, transcendentals=0),
    )(*args)


def feed_kernel(a2_ref, up_ref, upb_ref, gact_ref, g_ref, dh_ref, da2_ref, acc_ref):
    step = pl.program_id(0)
    hidden = dot_nn(a2_ref[...], up_ref[...]) + upb_ref[...]
    phi = 0.5 + 0.5 * lax.erf(hidden * 0.5**0.5)
    g_ref[...] = (hidden * phi).astype(BF16)
    slope = phi + hidden * (jnp.exp(-0.5 * hidden * hidden) * 0.3989422804014327)
    dh = (gact_ref[...] * slope).astype(BF16)
    dh_ref[...] = dh
    part = dot_nt(dh, up_ref[...])

    @pl.when(step == 0)
    def _():
        acc_ref[...] = part

    @pl.when(step > 0)
    def _():
        acc_ref[...] += part

    @pl.when(step == pl.num_programs(0) - 1)
    def _():
        da2_ref[...] = acc_ref[...].astype(da2_ref.dtype)


def feed(a2, up, upb, gact, kind):
    hidden = up.shape[1]
    width = 384
    shape = jax.ShapeDtypeStruct
    return pl.pallas_call(
        feed_kernel,
        grid=(hidden // width,),
        in_specs=[
            pl.BlockSpec((R, D), lambda i: (0, 0)),
            pl.BlockSpec((D, width), lambda i: (0, i)),
            pl.BlockSpec((1, width), lambda i: (0, i)),
            pl.BlockSpec((R, width), lambda i: (0, i)),
        ],
        out_specs=[
            pl.BlockSpec((R, width), lambda i: (0, i)),
            pl.BlockSpec((R, width), lambda i: (0, i)),
            pl.BlockSpec((R, D), lambda i: (0, 0)),
        ],
        out_shape=[shape((R, hidden), BF16), shape((R, hidden), BF16), shape((R, D), kind)],
        scratch_shapes=[pltpu.VMEM((R, D), F32)],
        compiler_params=pltpu.CompilerParams(vmem_limit_bytes=LIMIT),
        cost_estimate=pl.CostEstimate(flops=4 * R * D * hidden, bytes_accessed=6 * 2**20, transcendentals=2 * R * hidden),
    )(a2, up, upb, gact)


def weights_kernel(count, core_ref, *refs):
    lefts, rights = refs[:count], refs[count : 2 * count]
    keep_ref, send_ref = refs[2 * count : 2 * count + 2]
    sides = refs[2 * count + 2 :]
    core = core_ref[0]
    rows = keep_ref.shape[0]
    block = rows // (D // 96)

    @pl.when(pl.program_id(0) == 0)
    def _():
        for j in range(count):
            turned = lefts[j][...].astype(F32).T.astype(BF16)
            sides[2 * count][...] = turned
            for k in range(D // 96):
                for s in range(2):
                    which = core if s == 0 else 1 - core
                    start = pl.multiple_of(k * 96 + which * 48, 48)
                    sides[2 * j + s][k * block : (k + 1) * block, :] = sides[2 * count][pl.ds(start, 48), :]

    for s, out in enumerate((keep_ref, send_ref)):
        total = dot_nn(sides[s][...], rights[0][...])
        for j in range(1, count):
            total = total + dot_nn(sides[2 * j + s][...], rights[j][...])
        out[...] = total.astype(BF16)


def weight_grads(core, lefts, rights, width):
    count = len(lefts)
    columns = rights[0].shape[1]
    shape = jax.ShapeDtypeStruct
    half = D // 2
    return pl.pallas_call(
        partial(weights_kernel, count),
        grid=(columns // width,),
        in_specs=[SMEM]
        + [pl.BlockSpec((R, D), lambda i: (0, 0))] * count
        + [pl.BlockSpec((R, width), lambda i: (0, i))] * count,
        out_specs=[pl.BlockSpec((half, width), lambda i: (0, i))] * 2,
        out_shape=[shape((half, columns), BF16)] * 2,
        scratch_shapes=[pltpu.VMEM((half, R), BF16)] * (2 * count) + [pltpu.VMEM((D, R), BF16)],
        compiler_params=pltpu.CompilerParams(vmem_limit_bytes=LIMIT),
        cost_estimate=pl.CostEstimate(
            flops=2 * count * R * D * columns, bytes_accessed=6 * 2**20, transcendentals=0
        ),
    )(core, *lefts, *rights)


def pad_rows(rows):
    rows = rows.reshape(WIN, WIN, rows.shape[-1])
    return jnp.pad(rows, ((0, 0), (0, ROW - WIN), (0, 0))).reshape(R, -1)


def cut_rows(rows):
    return rows.reshape(WIN, ROW, -1)[:, :WIN].reshape(WIN * WIN, -1)


def per_device(
    tokens, ln1_gain, ln1_bias, qkv_weight, qv_bias, rel_pos_h, rel_pos_w, proj_weight, proj_bias,
    ln2_gain, ln2_bias, fc1_weight, fc1_bias, fc2_weight, fc2_bias, keep_mask, key_mask, out_grad,
):
    wide = lax.axis_size("mp")
    z, y, c, x = places()
    core = c.astype(jnp.int32).reshape(1)
    keep = keep_mask.astype(F32).reshape(2) / 0.9
    keep_att, keep_feed = keep[0:1], keep[1]

    def line(v):
        return v.astype(F32).reshape(1, -1)

    rows_in = pad_rows(tokens)
    grad_out = pad_rows(out_grad)
    grad_feed = (keep_feed * grad_out.astype(F32)).astype(BF16)
    dms = [grad_feed] + [move_x(grad_feed, s) for s in range(1, wide)]
    weights = gather_rows(jnp.concatenate([qkv_weight, proj_weight], -1), 2)
    gacts = [jnp.dot(dm, fc2_weight.T, preferred_element_type=F32) for dm in dms]

    reverse_h, reverse_w = rel_pos_h[::-1].T, rel_pos_w[::-1].T
    one = jnp.concatenate(
        [jnp.pad(reverse_h, ((0, 0), (0, HEAD - 27))), jnp.pad(reverse_w, ((0, 0), (0, HEAD - 27)))], axis=1
    )
    blank = jnp.zeros_like(one)
    tables = jnp.concatenate(
        [jnp.concatenate([one, blank], axis=1), jnp.concatenate([blank, one], axis=1)], axis=0
    )
    qv_wide = qv_bias.astype(F32)
    qkv_bias = jnp.concatenate([qv_wide[0], jnp.zeros((D,), F32), qv_wide[1]]).reshape(1, -1)
    mask = jnp.where(key_mask > 0, 0.0, -1e9).astype(F32).reshape(WIN, WIN)
    fill = jnp.pad(mask, ((0, 0), (0, ROW - WIN)), constant_values=-3e38).reshape(1, R)
    gain_one, gain_two = line(ln1_gain), line(ln2_gain)
    a1, qkv, probs, attended, middle, a2 = attend(
        rows_in, weights, gain_one, line(ln1_bias), qkv_bias, tables, line(proj_bias), gain_two, line(ln2_bias),
        fill, keep_att,
    )
    a2s = [a2] + [move_x(a2, s) for s in range(1, wide)]
    upb = line(fc1_bias)
    fed = [feed(a2s[j], fc1_weight, upb, gacts[j], F32 if j == 0 else BF16) for j in range(wide)]
    da2 = fed[0][2]
    got = move_x(fed[1][2], -1).astype(F32)
    for step in range(2, wide):
        got = got + move_x(fed[step][2], -step).astype(F32)
    feeds = [jnp.dot(f[0], fc2_weight, preferred_element_type=F32) for f in fed]
    feed_out = feeds[0]
    for step in range(1, wide):
        feed_out = feed_out + move_x(feeds[step].astype(BF16), -step).astype(F32)
    result = (middle + keep_feed * (feed_out + fc2_bias.astype(F32))).astype(BF16)

    down_keep, down_send = weight_grads(core, dms, [f[0] for f in fed], 768)
    up_keep, up_send = weight_grads(core, a2s, [f[1] for f in fed], 768)
    down_grad = scatter_dp(down_keep, down_send)
    up_grad = scatter_dp(up_keep, up_send)
    up_bias_grad = sum(jnp.sum(f[1].astype(F32), axis=0) for f in fed)
    down_bias_grad = jnp.sum(grad_feed.astype(F32), axis=0)

    (
        grad_branch, grad_qkv, grad_in, gain_one_grad, shift_one_grad, qkv_bias_grad, table_grad,
        proj_bias_grad, gain_two_grad, shift_two_grad,
    ) = attend_back(
        da2, got, middle, grad_out, rows_in, weights, qkv, probs, tables, gain_one, gain_two, keep_att
    )
    qkv_keep, qkv_send = weight_grads(core, [a1], [grad_qkv], 768)
    proj_keep, proj_send = weight_grads(core, [attended], [grad_branch], 768)
    qkv_w_grad = scatter_all(qkv_keep, qkv_send)
    proj_grad = scatter_all(proj_keep, proj_send)
    table_one = table_grad[:HEAD, :LANES] + table_grad[HEAD:, LANES:]
    relh_grad = table_one[:, :27].T[::-1]
    relw_grad = table_one[:, HEAD : HEAD + 27].T[::-1]
    qv_grad = jnp.concatenate([qkv_bias_grad[:, :D], qkv_bias_grad[:, 2 * D :]], axis=0)
    up_bias_all = lax.dynamic_update_slice(
        jnp.zeros((wide, up_bias_grad.shape[0]), F32), up_bias_grad[None], (lax.axis_index("mp"), 0)
    )
    (
        gain_one_grad, shift_one_grad, qv_grad, relh_grad, relw_grad, proj_bias_grad, gain_two_grad,
        shift_two_grad, down_bias_grad, up_bias_all,
    ) = sum_all(
        (
            gain_one_grad.reshape(D), shift_one_grad.reshape(D), qv_grad, relh_grad, relw_grad,
            proj_bias_grad.reshape(D), gain_two_grad.reshape(D), shift_two_grad.reshape(D), down_bias_grad,
            up_bias_all,
        )
    )
    up_bias_grad = pick(
        pick(up_bias_all, lax.axis_index("mp"), 0).reshape(lax.axis_size("dp"), -1), lax.axis_index("dp"), 0
    )
    return (
        cut_rows(result), cut_rows(grad_in), gain_one_grad, shift_one_grad, qkv_w_grad, qv_grad, relh_grad,
        relw_grad, proj_grad, proj_bias_grad, gain_two_grad, shift_two_grad, up_grad, up_bias_grad,
        down_grad.T, down_bias_grad,
    )


def solution(mesh):
    in_specs = (
        P(("dp", "mp"), None),
        P(),
        P(),
        P(("dp", "mp"), None),
        P(),
        P(),
        P(),
        P(("dp", "mp"), None),
        P(),
        P(),
        P(),
        P(None, "mp"),
        P("mp"),
        P("mp", None),
        P(),
        P(("dp", "mp"), None),
        P(("dp", "mp"), None),
        P(("dp", "mp"), None),
    )
    out_specs = (
        P(("dp", "mp"), None),
        P(("dp", "mp"), None),
        P(),
        P(),
        P(("dp", "mp"), None),
        P(),
        P(),
        P(),
        P(("dp", "mp"), None),
        P(),
        P(),
        P(),
        P("dp", "mp"),
        P(("mp", "dp")),
        P("mp", "dp"),
        P(),
    )
    return jax.shard_map(
        per_device, mesh=mesh, in_specs=in_specs, out_specs=out_specs, check_vma=False
    )
```

```python
from functools import partial

import jax
import jax.numpy as jnp
import numpy as np
from jax import lax
from jax.experimental import pallas as pl
from jax.experimental.pallas import tpu as pltpu
from jax.sharding import PartitionSpec as P

D = 768
HEADS = 12
HEAD = 64
WIN = 14
AREA = WIN * WIN
ROW = 16
R = WIN * ROW
PAIRS = HEADS // 2
LANES = 128
TABLE = 2 * WIN - 1
HALF = D // 2
STEP = 384
TIER = 3 * HALF
F32 = jnp.float32
BF16 = jnp.bfloat16
VMEM = pl.BlockSpec(memory_space=pltpu.VMEM)
SMEM = pl.BlockSpec(memory_space=pltpu.SMEM)
LIMIT = 20 * 2**20
CHEAP = pl.CostEstimate(flops=1, bytes_accessed=1, transcendentals=0)
SMALL = {"gain1": 0, "shift1": 6, "qbias": 12, "vbias": 18, "projb": 24, "gain2": 30, "shift2": 36, "downb": 42}
SMALL_TABLE = 48
SMALL_UP = SMALL_TABLE + HEAD


def shape_of(shape, kind):
    return jax.ShapeDtypeStruct(shape, kind)


def kernel_call(name, body, n_in, outs, *, smem=0, scratch=(), far=()):
    call = pl.pallas_call(
        body,
        name=name,
        in_specs=[SMEM] * smem + [VMEM] * (n_in - smem),
        out_specs=[VMEM] * len(outs),
        out_shape=[pltpu.VMEM(o.shape, o.dtype) for o in outs],
        scratch_shapes=list(scratch),
        compiler_params=pltpu.CompilerParams(vmem_limit_bytes=LIMIT),
        cost_estimate=CHEAP,
    )

    def run(*args):
        spaces = [pltpu.HBM if i in far else pltpu.VMEM for i in range(smem, n_in)]
        return call(*args[:smem], *map(pltpu.with_memory_space_constraint, args[smem:], spaces))

    return run


def after(value, *others):
    return lax.optimization_barrier((value,) + others)[0]


def dp_pairs(count, dz=0, dy=0, dc=0):
    depth = count // 4
    pairs = []
    for place in range(count):
        z, y, c = place // 4, place // 2 % 2, place % 2
        pairs.append((place, (z + dz) % depth * 4 + (y + dy) % 2 * 2 + (c + dc) % 2))
    return pairs


def move_z(value, step):
    return lax.ppermute(value, "dp", dp_pairs(lax.axis_size("dp"), dz=step))


def move_y(value):
    return lax.ppermute(value, "dp", dp_pairs(lax.axis_size("dp"), dy=1))


def move_c(value):
    return lax.ppermute(value, "dp", dp_pairs(lax.axis_size("dp"), dc=1))


def move_x(value, step=1):
    count = lax.axis_size("mp")
    return lax.ppermute(value, "mp", [(i, (i + step) % count) for i in range(count)])


def places():
    dp = lax.axis_index("dp")
    return dp // 4, dp // 2 % 2, dp % 2, lax.axis_index("mp")


def row_maps(count, wide):
    depth = count // 4
    place = np.arange(D)
    rows = D // (count * wide)
    block = place // rows
    att = [block % depth, block // depth % 2, block // (2 * depth) % wide, block // (2 * depth * wide), place % rows]
    rows = D // count
    block = place // rows
    feed = [block % depth, block // depth % 2, 0 * block, block // (2 * depth), place % rows]
    return np.stack(att + feed, axis=1).astype(np.int32)


def rows_from(maps_ref, start, rows, wide):
    depth = lax.axis_size("dp") // 4
    dp = lax.axis_index("dp")

    def turned(i, here, size):
        there = maps_ref[:, start + i : start + i + 1] + here
        return jnp.where(there >= size, there - size, there)

    block = (turned(0, dp // 4, depth) * 2 + turned(1, dp // 2 % 2, 2)) * 2 + turned(3, dp % 2, 2)
    if wide > 1:
        block = block * wide + turned(2, lax.axis_index("mp"), wide)
    return block * rows + maps_ref[:, start + 4 : start + 5]


def gather_z(part):
    depth = lax.axis_size("dp") // 4
    return jnp.concatenate([part] + [move_z(part, -s) for s in range(1, depth)])


def gather_near(line):
    wide = lax.axis_size("mp")
    return [move_x(line, -s) for s in range(1, wide)], move_y(line)


def gather_far(near):
    along_x, along_y = near
    half = along_y.shape[1] // 2
    left = [move_y(b[:, :half]) for b in along_x]
    right = [move_x(along_y[:, half:], -s) for s in range(1, lax.axis_size("mp"))]
    return left, right


def gather_join(line, near, far):
    blocks = [line, near[1]]
    for along_x, first, second in zip(near[0], *far):
        blocks += [along_x, jnp.concatenate([first, second], axis=1)]
    return jnp.concatenate(blocks)


def add_up(first, *others):
    total = first.astype(F32)
    for other in others:
        total = total + other.astype(F32)
    return total


def scatter_x(rows):
    wide = lax.axis_size("mp")
    size = rows.shape[0] // wide
    return add_up(rows[:size], *[move_x(rows[s * size : (s + 1) * size].astype(BF16), s) for s in range(1, wide)])


def scatter_y(rows, *others):
    size = rows.shape[0] // 2
    return add_up(rows[:size], after(move_y(rows[size:].astype(BF16)), *others))


def scatter_z(rows):
    depth = lax.axis_size("dp") // 4
    size = rows.shape[0] // depth
    return add_up(rows[:size], *[move_z(rows[s * size : (s + 1) * size].astype(BF16), s) for s in range(1, depth)])


def sum_small(flat):
    depth, wide = lax.axis_size("dp") // 4, lax.axis_size("mp")
    flat = flat + move_c(flat)
    flat = sum([move_x(flat, s) for s in range(1, wide)], flat)
    flat = flat + move_y(flat)
    return sum([move_z(flat, s) for s in range(1, depth)], flat)


def dot_nn(a, b):
    return lax.dot_general(a, b, (((1,), (0,)), ((), ())), preferred_element_type=F32)


def dot_nt(a, b):
    return lax.dot_general(a, b, (((1,), (1,)), ((), ())), preferred_element_type=F32)


def dot_tn(a, b):
    return lax.dot_general(a, b, (((0,), (0,)), ((), ())), preferred_element_type=F32)


def iota(shape, axis):
    return lax.broadcasted_iota(jnp.int32, shape, axis)


def norm_parts(rows_in):
    center = rows_in - jnp.mean(rows_in, axis=-1, keepdims=True)
    factor = lax.rsqrt(jnp.mean(center * center, axis=-1, keepdims=True) + 1e-06)
    return center * factor, factor


def norm_back(grad, unit, factor, gain):
    inner = grad * gain
    return factor * (
        inner
        - jnp.mean(inner, axis=-1, keepdims=True)
        - unit * jnp.mean(inner * unit, axis=-1, keepdims=True)
    )


def spread_rows():
    row, patch = iota((R, AREA), 0), iota((R, AREA), 1)
    return ((row % ROW < WIN) & (patch == row // ROW * WIN + row % ROW)).astype(F32).astype(BF16)


def row_masks():
    lane = iota((R, LANES), 1) % HEAD
    key = iota((R, LANES), 0)
    here = jnp.where(lane // ROW % 2 == 0, key // ROW, key % ROW)
    return (lane % ROW == here).astype(F32)


def offset_lanes(rows, base):
    lane = iota((rows, LANES), 1)
    in_h = (lane >= base) & (lane < base + ROW)
    in_w = (lane >= base + ROW) & (lane < base + 2 * ROW)
    return in_h, in_w


def query_offsets(table, base):
    in_h, in_w = offset_lanes(ROW, base)
    outs = []
    for a in range(WIN):
        group = table[a * ROW : (a + 1) * ROW]
        at_h = pltpu.roll(group, (HEAD - 13 + a) % LANES, 1)
        at_w = pltpu.roll(group, LANES - ROW + 1, 1, stride=1, stride_axis=0)
        both = jnp.where(in_h, at_h, jnp.where(in_w, at_w, 0.0))
        high = both.astype(BF16).astype(F32)
        outs.append(high + pltpu.roll(both - high, 2 * ROW, 1))
    return jnp.concatenate(outs, axis=0)


def offset_grads(grad, base):
    in_h, in_w = offset_lanes(R, base)
    column = iota((R, LANES), 0) % ROW
    from_w = jnp.where(in_w, grad, 0.0)
    for bit in (1, 2, 4, 8):
        from_w = jnp.where((ROW - 1 - column) & bit > 0, pltpu.roll(from_w, bit, 1), from_w)
    only_h = jnp.where(in_h, grad, 0.0)
    from_h = [pltpu.roll(only_h[a * ROW : (a + 1) * ROW], (HEAD + 13 - a) % LANES, 1) for a in range(WIN)]
    return jnp.concatenate(from_h, axis=0) + from_w


def table_places(kind):
    row, lane = iota((TABLE, LANES), 0), iota((TABLE, LANES), 1)
    start = 0 if kind == "h" else HEAD + ROW + 2
    return (lane - start == TABLE - 1 - row).astype(F32)


def pack_kernel(qkv_ref, proj_ref, gain1_ref, shift1_ref, projb_ref, gain2_ref, shift2_ref, downb_ref, qvb_ref, first_ref, second_ref, params_ref):
    for tier, out in enumerate((first_ref, second_ref)):
        for i in range(3):
            out[:, i * HALF : (i + 1) * HALF] = qkv_ref[:, i * D + tier * HALF : i * D + (tier + 1) * HALF]
    second_ref[:, TIER:] = proj_ref[...]
    for i, ref in enumerate((gain1_ref, shift1_ref, projb_ref, gain2_ref, shift2_ref, downb_ref)):
        params_ref[i : i + 1] = ref[...].astype(F32).reshape(1, D)
    params_ref[6:8] = qvb_ref[...].astype(F32)


def pack(qkv_weight, *args):
    rows = qkv_weight.shape[0]
    return kernel_call(
        "pack",
        pack_kernel, 9, [shape_of((rows, TIER), BF16), shape_of((rows, TIER + D), BF16), shape_of((8, D), F32)], far=range(9)
    )(qkv_weight, *args)


def prepare_kernel(
    count, wide, keep_ref, tokens_ref, grad_ref, maps_ref, params_ref, relh_ref, relw_ref, mask_ref, upb_ref,
    x_ref, a1_ref, turned_ref, g_ref, dm_ref, att_ref, feed_ref, table_ref, fill_ref, downb_ref, wideb_ref,
):
    wideb_ref[...] = upb_ref[...].astype(F32).reshape(wideb_ref.shape)
    spread = spread_rows()
    x = dot_nn(spread, tokens_ref[...])
    x_ref[...] = x.astype(BF16)
    grad = dot_nn(spread, grad_ref[...])
    g_ref[...] = grad.astype(BF16)
    dm = (jnp.where(keep_ref[0, 1] > 0, 1.0 / 0.9, 0.0).astype(F32) * grad).astype(BF16)
    dm_ref[...] = dm
    downb_ref[...] = jnp.sum(dm.astype(F32), axis=0, keepdims=True)
    source = iota((D, D), 1)
    att = (rows_from(maps_ref, 0, D // (count * wide), wide) == source).astype(F32).astype(BF16)
    att_ref[...] = att
    feed_ref[...] = (rows_from(maps_ref, 5, D // count, 1) == source).astype(F32).astype(BF16)
    unit, _ = norm_parts(x)
    a1 = (unit * params_ref[0:1] + params_ref[1:2]).astype(BF16)
    a1_ref[...] = dot_nt(a1, att).astype(BF16)
    turned_ref[...] = dot_nt(att, a1).astype(BF16)
    one = dot_tn(relh_ref[...], table_places("h").astype(BF16)) + dot_tn(relw_ref[...], table_places("w").astype(BF16))
    blank = jnp.zeros((HEAD, LANES), F32)
    table_ref[:HEAD, :] = jnp.concatenate([one, blank], axis=1).astype(BF16)
    table_ref[HEAD:, :] = jnp.concatenate([blank, pltpu.roll(one, HEAD, 1)], axis=1).astype(BF16)
    seen = dot_nt((mask_ref[...] > 0).astype(F32).astype(BF16), spread)
    key = iota((1, R), 1)
    fill_ref[...] = jnp.where(key % ROW >= WIN, -3e38, jnp.where(seen > 0.5, 0.0, -1e9))


def prepare(keep, tokens, grad, params, rel_h, rel_w, mask, upb):
    count, wide = lax.axis_size("dp"), lax.axis_size("mp")
    return kernel_call(
        "prepare",
        partial(prepare_kernel, count, wide),
        9,
        [
            shape_of((R, D), BF16), shape_of((R, D), BF16), shape_of((D, R), BF16), shape_of((R, D), BF16),
            shape_of((R, D), BF16), shape_of((D, D), BF16), shape_of((D, D), BF16),
            shape_of((LANES, 2 * LANES), BF16), shape_of((1, R), F32), shape_of((1, D), F32),
            shape_of((1, upb.shape[0]), F32),
        ],
        smem=1, far=(1, 2, 3, 5, 6, 7, 8),
    )(keep, tokens, grad, row_maps(count, wide), params, rel_h, rel_w, mask, upb)


def act_kernel(dm_ref, down_ref, out_ref):
    out_ref[...] = dot_nt(dm_ref[...], down_ref[...])


def act_grad(dm, down):
    return kernel_call("act", act_kernel, 2, [shape_of((R, down.shape[0]), F32)])(dm, down)[0]


def heads_forward(qkv_ref, tables, fill, p_ref, out):
    ones = row_masks()
    left = iota((R, LANES), 1) < HEAD
    for pair in range(PAIRS // 2):
        at = pair * LANES
        q2 = qkv_ref[:, at : at + LANES]
        k2 = qkv_ref[:, HALF + at : HALF + at + LANES].astype(F32)
        v2 = qkv_ref[:, 2 * HALF + at : 2 * HALF + at + LANES]
        products = dot_nn(q2, tables)
        q2 = q2.astype(F32) * HEAD**-0.5
        outs = []
        for side in range(2):
            mine = left if side == 0 else ~left
            offsets = query_offsets(products[:, side * LANES : (side + 1) * LANES], HEAD * (1 - side))
            q_aug = jnp.where(mine, q2, offsets).astype(BF16)
            k_aug = jnp.where(mine, k2, ones).astype(BF16)
            scores = dot_nt(q_aug, k_aug)
            scores = jnp.where(fill < 0.0, fill, scores)
            expo = jnp.exp(scores - jnp.max(scores, axis=-1, keepdims=True))
            probs = (expo / jnp.sum(expo, axis=-1, keepdims=True)).astype(BF16)
            p_ref[2 * pair + side] = probs
            outs.append(dot_nn(probs, v2))
        out(at, jnp.where(left, outs[0], outs[1]).astype(BF16))


def project(a1_ref, own_ref, other_ref, bias, qkv_ref):
    total = dot_nn(a1_ref[:, :HALF], own_ref[:, :TIER]) + dot_nn(a1_ref[:, HALF:], other_ref[:, :TIER])
    qkv_ref[...] = (total + bias).astype(BF16)


def tier_bias(params_ref, tier):
    at = tier * HALF
    return jnp.concatenate(
        [
            params_ref[6:7, at : at + HALF],
            jnp.zeros((1, HALF), F32),
            params_ref[7:8, at : at + HALF],
        ],
        axis=1,
    )


def attend_first_kernel(a1_ref, own_ref, other_ref, params_ref, table_ref, fill_ref, qkv_ref, p_ref, o_ref):
    project(a1_ref, own_ref, other_ref, tier_bias(params_ref, 0), qkv_ref)

    def out(at, value):
        o_ref[:, at : at + LANES] = value

    heads_forward(qkv_ref, table_ref[...], fill_ref[...], p_ref, out)


def attend_first(*args):
    return kernel_call(
        "attend1",
        attend_first_kernel,
        6,
        [shape_of((R, TIER), BF16), shape_of((HEADS // 2, R, R), BF16), shape_of((R, HALF), BF16)],
    )(*args)


def attend_second_kernel(
    keep_ref, a1_ref, own_ref, other_ref, params_ref, table_ref, fill_ref, first_ref, x_ref, att_ref,
    qkv_ref, p_ref, turned_ref, mid_ref, a2_ref,
    o_ref,
):
    project(a1_ref, own_ref, other_ref, tier_bias(params_ref, 1), qkv_ref)
    o_ref[:, :HALF] = first_ref[...]

    def out(at, value):
        o_ref[:, HALF + at : HALF + at + LANES] = value

    heads_forward(qkv_ref, table_ref[...], fill_ref[...], p_ref, out)
    moved = dot_nt(o_ref[...], att_ref[...]).astype(BF16)
    branch = dot_nn(moved[:, :HALF], own_ref[:, TIER:]) + dot_nn(moved[:, HALF:], other_ref[:, TIER:])
    turned_ref[...] = dot_nt(att_ref[...], o_ref[...]).astype(BF16)
    rate = jnp.where(keep_ref[0, 0] > 0, 1.0 / 0.9, 0.0).astype(F32)
    middle = x_ref[...].astype(F32) + rate * (branch + params_ref[2:3])
    mid_ref[...] = middle
    unit, _ = norm_parts(middle)
    a2_ref[...] = (unit * params_ref[3:4] + params_ref[4:5]).astype(BF16)


def attend_second(*args):
    return kernel_call(
        "attend2",
        attend_second_kernel,
        10,
        [
            shape_of((R, TIER), BF16), shape_of((HEADS // 2, R, R), BF16), shape_of((D, R), BF16),
            shape_of((R, D), F32), shape_of((R, D), BF16),
        ],
        smem=1, scratch=[pltpu.VMEM((R, D), BF16)],
    )(*args)


def feed_kernel(a2_ref, up_ref, upb_ref, gact_ref, g_ref, dh_ref, da2_ref):
    total = None
    for at in range(0, up_ref.shape[1], STEP):
        here = slice(at, at + STEP)
        hidden = dot_nn(a2_ref[...], up_ref[:, here]) + upb_ref[:, here]
        phi = 0.5 + 0.5 * lax.erf(hidden * 0.5**0.5)
        g_ref[:, here] = (hidden * phi).astype(BF16)
        slope = phi + hidden * (jnp.exp(-0.5 * hidden * hidden) * 0.3989422804014327)
        dh = (gact_ref[:, here] * slope).astype(BF16)
        dh_ref[:, here] = dh
        part = dot_nt(dh, up_ref[:, here])
        total = part if total is None else total + part
    da2_ref[...] = total.astype(da2_ref.dtype)


def feed(a2, up, upb, gact, kind):
    hidden = up.shape[1]
    return kernel_call(
        "feed",
        feed_kernel,
        4,
        [shape_of((R, hidden), BF16), shape_of((R, hidden), BF16), shape_of((R, D), kind)],
    )(a2, up, upb, gact)


def feed_weights_kernel(count, map_ref, down_ref, *refs):
    dms, acts, a2s, dhs = (refs[i * count : (i + 1) * count] for i in range(4))
    downk_ref, downs_ref, upk_ref, ups_ref, sum_ref, *outs = refs[4 * count :]
    for lefts, rights, keep_ref, send_ref in ((dms, acts, downk_ref, downs_ref), (a2s, dhs, upk_ref, ups_ref)):
        turned = [dot_nt(map_ref[...], left[...]).astype(BF16) for left in lefts]
        for at in range(0, keep_ref.shape[1], STEP):
            here = slice(at, at + STEP)
            total = dot_nn(turned[0], rights[0][:, here])
            for j in range(1, count):
                total = total + dot_nn(turned[j], rights[j][:, here])
            keep_ref[:, here] = total[:HALF].astype(BF16)
            send_ref[:, here] = total[HALF:].astype(BF16)
    for j in range(count):
        outs[j][...] = dot_nn(acts[j][...], down_ref[...]).astype(outs[j].dtype)
    sums = jnp.sum(dhs[0][...].astype(F32), axis=0, keepdims=True)
    for j in range(1, count):
        sums = sums + jnp.sum(dhs[j][...].astype(F32), axis=0, keepdims=True)
    sum_ref[...] = sums


def feed_weights(row_map, down, dms, acts, a2s, dhs):
    count = len(dms)
    columns = acts[0].shape[1]
    return kernel_call(
        "feedw",
        partial(feed_weights_kernel, count),
        2 + 4 * count,
        [shape_of((HALF, columns), BF16)] * 4
        + [shape_of((1, columns), F32)]
        + [shape_of((R, D), F32 if j == 0 else BF16) for j in range(count)],
    )(row_map, down, *dms, *acts, *a2s, *dhs)


def heads_back(qkv_ref, p_ref, do_at, tables, dqkv_ref):
    ones = row_masks()
    left = iota((R, LANES), 1) < HEAD
    table_grad = jnp.zeros((LANES, 2 * LANES), F32)
    for pair in range(PAIRS // 2):
        at = pair * LANES
        q2 = qkv_ref[:, at : at + LANES]
        q_wide = q2.astype(F32)
        k2 = qkv_ref[:, HALF + at : HALF + at + LANES].astype(F32)
        v2 = qkv_ref[:, 2 * HALF + at : 2 * HALF + at + LANES]
        do2 = do_at(at).astype(F32)
        dq2 = dk2 = dv2 = None
        offsets = []
        for side in range(2):
            mine = left if side == 0 else ~left
            probs = p_ref[2 * pair + side]
            do_mine = jnp.where(mine, do2, 0.0).astype(BF16)
            dv = dot_tn(probs, do_mine)
            dp = dot_nt(do_mine, v2)
            wide = probs.astype(F32)
            ds = (wide * (dp - jnp.sum(wide * dp, axis=-1, keepdims=True))).astype(BF16)
            k_aug = jnp.where(mine, k2, ones).astype(BF16)
            dq_aug = dot_nn(ds, k_aug)
            offsets.append(offset_grads(dq_aug, HEAD * (1 - side)))
            dk = dot_tn(ds, jnp.where(mine, q_wide, 0.0).astype(BF16))
            if side == 0:
                dq2, dk2, dv2 = dq_aug, dk, dv
            else:
                dq2, dk2, dv2 = jnp.where(mine, dq_aug, dq2), dk2 + dk, dv2 + dv
        spread = jnp.concatenate(offsets, axis=1).astype(BF16)
        dq2 = dq2 * HEAD**-0.5 + dot_nt(spread, tables)
        table_grad = table_grad + dot_tn(q2, spread)
        dqkv_ref[:, at : at + LANES] = dq2.astype(BF16)
        dqkv_ref[:, HALF + at : HALF + at + LANES] = (dk2 * HEAD**-0.5).astype(BF16)
        dqkv_ref[:, 2 * HALF + at : 2 * HALF + at + LANES] = dv2.astype(BF16)
    return table_grad[:HEAD, :LANES] + pltpu.roll(table_grad[HEAD:, LANES:], HEAD, 1)


def back_norm_kernel(
    keep_ref, da2_ref, got_ref, mid_ref, g_ref, params_ref, own_ref, other_ref, att_ref, dmid_ref, dy_ref, do_ref, sums_ref
):
    da2 = da2_ref[...] + got_ref[...].astype(F32)
    unit, factor = norm_parts(mid_ref[...])
    dmid = g_ref[...].astype(F32) + norm_back(da2, unit, factor, params_ref[3:4])
    dmid_ref[...] = dmid
    rate = jnp.where(keep_ref[0, 0] > 0, 1.0 / 0.9, 0.0).astype(F32)
    dy = (rate * dmid).astype(BF16)
    dy_ref[...] = dy
    moved = jnp.concatenate(
        [dot_nt(dy, own_ref[:, TIER:]).astype(BF16), dot_nt(dy, other_ref[:, TIER:]).astype(BF16)], axis=1
    )
    do_ref[...] = dot_nn(moved, att_ref[...]).astype(BF16)
    sums_ref[0:1] = jnp.sum(dy.astype(F32), axis=0, keepdims=True)
    sums_ref[1:2] = jnp.sum(da2 * unit, axis=0, keepdims=True)
    sums_ref[2:3] = jnp.sum(da2, axis=0, keepdims=True)


def back_norm(*args):
    return kernel_call(
        "backnorm",
        back_norm_kernel,
        9,
        [shape_of((R, D), F32), shape_of((R, D), BF16), shape_of((R, D), BF16), shape_of((3, D), F32)],
        smem=1,
    )(*args)


def back_first_kernel(
    dy_ref, do_ref, turned_ref, o_ref, qkv_ref, p_ref, table_ref,
    dqkv_ref, weights_ref, send_ref, sums_ref, tablegrad_ref,
):
    tablegrad_ref[...] = heads_back(qkv_ref, p_ref, lambda at: do_ref[:, at : at + LANES], table_ref[...], dqkv_ref)
    for s, out in enumerate((weights_ref, send_ref)):
        rows = slice(s * HALF, (s + 1) * HALF)
        out[:, :TIER] = dot_nn(turned_ref[rows], dqkv_ref[...]).astype(BF16)
        out[:, TIER:] = dot_nn(o_ref[rows], dy_ref[...]).astype(BF16)
    sums_ref[:, :HALF] = jnp.sum(dqkv_ref[:, :HALF].astype(F32), axis=0, keepdims=True)
    sums_ref[:, HALF:] = jnp.sum(dqkv_ref[:, 2 * HALF :].astype(F32), axis=0, keepdims=True)


def back_first(*args):
    return kernel_call(
        "back1",
        back_first_kernel,
        7,
        [
            shape_of((R, TIER), BF16), shape_of((HALF, TIER + D), BF16), shape_of((HALF, TIER + D), BF16),
            shape_of((1, D), F32), shape_of((HEAD, LANES), F32),
        ],
    )(*args)


def back_second_kernel(
    do_ref, turned_ref, qkv_ref, p_ref, table_ref, dqkv_ref, keep_ref, send_ref, sums_ref, tablegrad_ref
):
    tablegrad_ref[...] = heads_back(qkv_ref, p_ref, lambda at: do_ref[:, HALF + at : HALF + at + LANES], table_ref[...], dqkv_ref)
    for s, out in enumerate((keep_ref, send_ref)):
        out[...] = dot_nn(turned_ref[s * HALF : (s + 1) * HALF], dqkv_ref[...]).astype(BF16)
    sums_ref[:, :HALF] = jnp.sum(dqkv_ref[:, :HALF].astype(F32), axis=0, keepdims=True)
    sums_ref[:, HALF:] = jnp.sum(dqkv_ref[:, 2 * HALF :].astype(F32), axis=0, keepdims=True)


def back_second(*args):
    return kernel_call(
        "back2",
        back_second_kernel,
        5,
        [
            shape_of((R, TIER), BF16), shape_of((HALF, TIER), BF16), shape_of((HALF, TIER), BF16),
            shape_of((1, D), F32), shape_of((HEAD, LANES), F32),
        ],
    )(*args)


def finish_kernel(
    wide, keep_ref, dq1_ref, dq2_ref, own1_ref, other1_ref, own2_ref, other2_ref, att_ref, x_ref, dmid_ref,
    params_ref, mid_ref, m_ref, mgot_ref, downb_ref, upb_ref, sums0_ref, sums1_ref, sums2_ref, tab1_ref, tab2_ref,
    dx_ref, result_ref, small_ref,
):
    halves = []
    for first, second in ((own1_ref, own2_ref), (other1_ref, other2_ref)):
        halves.append(dot_nt(dq1_ref[...], first[...]) + dot_nt(dq2_ref[...], second[:, :TIER]))
    moved = jnp.concatenate(halves, axis=1)
    high = moved.astype(BF16)
    low = (moved - high.astype(F32)).astype(BF16)
    da1 = dot_nn(high, att_ref[...]) + dot_nn(low, att_ref[...])
    unit, factor = norm_parts(x_ref[...].astype(F32))
    dx = (dmid_ref[...] + norm_back(da1, unit, factor, params_ref[0:1])).astype(BF16)
    rate = jnp.where(keep_ref[0, 1] > 0, 1.0 / 0.9, 0.0).astype(F32)
    total = m_ref[...] + mgot_ref[...].astype(F32) + params_ref[5:6]
    result = (mid_ref[...] + rate * total).astype(BF16)
    spread = spread_rows()
    dx_ref[...] = dot_tn(spread, dx).astype(BF16)
    result_ref[...] = dot_tn(spread, result).astype(BF16)

    def put(name, value):
        for i in range(D // LANES):
            small_ref[SMALL[name] + i : SMALL[name] + i + 1] = value[:, i * LANES : (i + 1) * LANES]

    put("gain1", jnp.sum(da1 * unit, axis=0, keepdims=True))
    put("shift1", jnp.sum(da1, axis=0, keepdims=True))
    put("projb", sums0_ref[0:1])
    put("gain2", sums0_ref[1:2])
    put("shift2", sums0_ref[2:3])
    put("qbias", jnp.concatenate([sums1_ref[:, :HALF], sums2_ref[:, :HALF]], axis=1))
    put("vbias", jnp.concatenate([sums1_ref[:, HALF:], sums2_ref[:, HALF:]], axis=1))
    put("downb", downb_ref[...])
    small_ref[SMALL_TABLE : SMALL_TABLE + HEAD] = tab1_ref[...] + tab2_ref[...]
    rows = upb_ref.shape[1] // LANES
    for m in range(wide):
        for i in range(rows):
            value = upb_ref[:, i * LANES : (i + 1) * LANES]
            at = SMALL_UP + m * rows + i
            small_ref[at : at + 1] = jnp.where(lax.axis_index("mp") == m, value, 0.0)


def finish(wide, rows, *args):
    return kernel_call(
        "finish",
        partial(finish_kernel, wide),
        21,
        [shape_of((AREA, D), BF16), shape_of((AREA, D), BF16), shape_of((rows, LANES), F32)],
        smem=1,
    )(*args)


def per_device(
    tokens, ln1_gain, ln1_bias, qkv_weight, qv_bias, rel_pos_h, rel_pos_w, proj_weight, proj_bias,
    ln2_gain, ln2_bias, fc1_weight, fc1_bias, fc2_weight, fc2_bias, keep_mask, key_mask, out_grad,
):
    wide = lax.axis_size("mp")
    hidden = fc1_weight.shape[1]
    first, second, params = pack(
        qkv_weight, proj_weight, ln1_gain, ln1_bias, proj_bias, ln2_gain, ln2_bias, fc2_bias, qv_bias
    )
    line1 = gather_z(first)
    line2 = gather_z(second)
    rows_in, a1, a1_turned, grad_out, dm, att_map, feed_map, tables, fill, downb, upb = prepare(
        keep_mask, tokens, out_grad, params, rel_pos_h, rel_pos_w, key_mask, fc1_bias
    )
    dms = [dm] + [move_x(dm, -s) for s in range(1, wide)]
    line1 = after(line1, a1)
    near1 = gather_near(line1)
    gacts = [act_grad(dm, fc2_weight)]
    near1, line2, dms, gacts = lax.optimization_barrier((near1, line2, dms, gacts))
    far1 = gather_far(near1)
    near2 = gather_near(line2)
    for v in dms[1:]:
        gacts.append(act_grad(after(v, gacts[-1]), fc2_weight))
    far1, near2, gacts = lax.optimization_barrier((far1, near2, gacts))
    own1 = gather_join(line1, near1, far1)
    other1 = move_c(own1)
    far2 = gather_far(near2)
    qkv1, probs1, att1 = attend_first(a1, own1, other1, params, tables, fill)
    far2, att1 = lax.optimization_barrier((far2, att1))
    own2 = gather_join(line2, near2, far2)
    other2 = move_c(own2)
    qkv2, probs2, att_turned, middle, a2 = attend_second(
        keep_mask, a1, own2, other2, params, tables, fill, att1, rows_in, att_map
    )

    a2s = [a2] + [move_x(a2, -s) for s in range(1, wide)]
    fed = [feed(a2, fc1_weight, upb, gacts[0], F32)]
    for j in range(1, wide):
        fed.append(feed(after(a2s[j], fed[-1][2]), fc1_weight, upb, gacts[j], BF16))
    da2 = fed[0][2]
    got = [move_x(fed[s][2], s) for s in range(1, wide)]
    down_keep, down_send, up_keep, up_send, upb_sum, *outs = feed_weights(
        after(feed_map, fed[-1][2]), fc2_weight, dms, [f[0] for f in fed], a2s, [f[1] for f in fed]
    )
    got, down_send, up_send, outs = lax.optimization_barrier((got, down_send, up_send, outs))
    got = got[0] if wide == 2 else add_up(*got)
    down_rows = add_up(down_keep, move_c(down_send))
    up_rows = add_up(up_keep, move_c(up_send))
    dmid, dy, do, sums0 = back_norm(keep_mask, da2, got, middle, grad_out, params, own2, other2, att_map)
    down_rows, up_rows, do = lax.optimization_barrier((down_rows, up_rows, do))
    out_got = [move_x(outs[s], s) for s in range(1, wide)]
    dqkv1, keep1, send1, sums1, tab1 = back_first(dy, do, a1_turned, att_turned, qkv1, probs1, tables)
    rows1 = add_up(keep1, move_c(send1))
    rows1, do = lax.optimization_barrier((rows1, do))
    down_rows = scatter_y(down_rows)
    out_got = out_got[0] if wide == 2 else add_up(*out_got)
    rows1 = scatter_x(rows1)
    down_grad = scatter_z(down_rows)
    dqkv2, keep2, send2, sums2, tab2 = back_second(do, a1_turned, qkv2, probs2, tables)
    up_rows = scatter_y(up_rows, send2)
    rows2 = add_up(keep2, move_c(send2))
    rows1, rows2, dqkv2 = lax.optimization_barrier((rows1, rows2, dqkv2))
    rows1 = scatter_y(rows1)
    rows2 = scatter_x(rows2)
    up_grad = scatter_z(up_rows)
    small_rows = SMALL_UP + wide * hidden // LANES
    small_rows += -small_rows % 8
    grad_in, result, small = finish(
        wide, small_rows, keep_mask, dqkv1, dqkv2, own1, other1, own2, other2, att_map, rows_in, dmid, params,
        middle, outs[0], out_got, downb, upb_sum, sums0, sums1, sums2, tab1, tab2,
    )
    rows1, rows2, small = lax.optimization_barrier((rows1, rows2, small))
    rows1 = scatter_z(rows1)
    rows2 = scatter_z(scatter_y(rows2))
    small = sum_small(small)

    pieces = [
        piece
        for i in range(3)
        for piece in (rows1[:, i * HALF : (i + 1) * HALF], rows2[:, i * HALF : (i + 1) * HALF])
    ]
    qkv_grad = jnp.concatenate(pieces, axis=1)
    proj_grad = rows1[:, TIER:]

    def vector(name):
        return small[SMALL[name] : SMALL[name] + D // LANES].reshape(D)

    table = small[SMALL_TABLE : SMALL_TABLE + HEAD]
    relh_grad = table[:, :TABLE].T[::-1]
    relw_grad = table[:, HEAD + ROW + 2 : HEAD + ROW + 2 + TABLE].T[::-1]
    up_all = small[SMALL_UP : SMALL_UP + wide * hidden // LANES].reshape(-1)
    size = hidden // lax.axis_size("dp")
    up_bias_grad = lax.dynamic_slice(up_all, (lax.axis_index("mp") * hidden + lax.axis_index("dp") * size,), (size,))
    qv_grad = jnp.stack([vector("qbias"), vector("vbias")])
    return (
        result, grad_in, vector("gain1"), vector("shift1"), qkv_grad, qv_grad, relh_grad, relw_grad, proj_grad,
        vector("projb"), vector("gain2"), vector("shift2"), up_grad, up_bias_grad, down_grad.T, vector("downb"),
    )


def solution(mesh):
    in_specs = (
        P(("dp", "mp"), None),
        P(),
        P(),
        P(("dp", "mp"), None),
        P(),
        P(),
        P(),
        P(("dp", "mp"), None),
        P(),
        P(),
        P(),
        P(None, "mp"),
        P("mp"),
        P("mp", None),
        P(),
        P(("dp", "mp"), None),
        P(("dp", "mp"), None),
        P(("dp", "mp"), None),
    )
    out_specs = (
        P(("dp", "mp"), None),
        P(("dp", "mp"), None),
        P(),
        P(),
        P(("dp", "mp"), None),
        P(),
        P(),
        P(),
        P(("dp", "mp"), None),
        P(),
        P(),
        P(),
        P("dp", "mp"),
        P(("mp", "dp")),
        P("mp", "dp"),
        P(),
    )
    return jax.shard_map(
        per_device, mesh=mesh, in_specs=in_specs, out_specs=out_specs, check_vma=False
    )
```

```python
from functools import partial

import jax
import jax.numpy as jnp
import numpy as np
from jax import lax
from jax.experimental import pallas as pl
from jax.experimental.pallas import tpu as pltpu
from jax.sharding import PartitionSpec as P

D = 768
HEADS = 12
HEAD = 64
WIN = 14
AREA = WIN * WIN
ROW = 16
R = WIN * ROW
PAIRS = HEADS // 2
LANES = 128
TABLE = 2 * WIN - 1
W_START = HEAD + ROW + 2
HALF = D // 2
STEP = 384
TIER = 3 * HALF
F32 = jnp.float32
BF16 = jnp.bfloat16
VMEM = pl.BlockSpec(memory_space=pltpu.VMEM)
SMEM = pl.BlockSpec(memory_space=pltpu.SMEM)
LIMIT = 20 * 2**20
Z_FIRST = (False, False)
FRONT = ('dm', 'z1', 'prep', 'act1', 'z2', 'n1', 'n2', 'act0', 'f2', 'f1', 'c1', 'attend1', 'c2')
ORDER = ('dc', 'dy', 'm', 'norm', 'back2', 'bc', 'back1', 'finish', 'ac', 'sc', 'by', 'uc', 'bx', 'dz', 'bz', 'uy', 'ax', 'ay', 'uz', 'az')
GATES = {'n1:s': ['prep', 'dm'], 'n2:s': ['z2'], 'f1:s': ['n1'], 'act1:s': ['dm'], 'attend1:s': ['dm', 'f1'], 'z1:s': ['dm'], 'back1:s': ['dc'], 'back2:s': ['m'], 'finish:s': ['bc'], 'ay:r': ['ac', 'back1', 'dz'], 'uc:s': ['dc'], 'bc:s': ['dy'], 'bx:r': ['uc', 'dy'], 'm:s': ['dc'], 'bz:r': ['bc'], 'dz:s': ['finish'], 'ac:r': ['bc'], 'bx:s': ['ac'], 'uy:r': ['finish'], 'uc:r': ['back1'], 'dz:r': ['uc']}
CHEAP = pl.CostEstimate(flops=1, bytes_accessed=1, transcendentals=0)
SMALL = {"gain1": 0, "shift1": 6, "qbias": 12, "vbias": 18, "projb": 24, "gain2": 30, "shift2": 36, "downb": 42}
SMALL_TABLE = 48
SMALL_UP = SMALL_TABLE + HEAD // 2
PIECES = TIER // LANES


def piece(place):
    return slice(place // PIECES, place // PIECES + 1), slice(place % PIECES * LANES, (place % PIECES + 1) * LANES)


def shape_of(shape, kind):
    return jax.ShapeDtypeStruct(shape, kind)


def kernel_call(name, body, n_in, outs, *, smem=0, scratch=(), far=(), out_far=()):
    call = pl.pallas_call(
        body,
        name=name,
        in_specs=[SMEM] * smem + [VMEM] * (n_in - smem),
        out_specs=[VMEM] * len(outs),
        out_shape=[o if i in out_far else pltpu.VMEM(o.shape, o.dtype) for i, o in enumerate(outs)],
        scratch_shapes=list(scratch),
        compiler_params=pltpu.CompilerParams(vmem_limit_bytes=LIMIT),
        cost_estimate=CHEAP,
    )

    def run(*args):
        spaces = [pltpu.HBM if i in far else pltpu.VMEM for i in range(smem, n_in)]
        return call(*args[:smem], *map(pltpu.with_memory_space_constraint, args[smem:], spaces))

    return run


def after(value, *others):
    return lax.optimization_barrier((value,) + others)[0]


def dp_pairs(count, dz=0, dy=0, dc=0):
    depth = count // 4
    pairs = []
    for place in range(count):
        z, y, c = place // 4, place // 2 % 2, place % 2
        pairs.append((place, (z + dz) % depth * 4 + (y + dy) % 2 * 2 + (c + dc) % 2))
    return pairs


def move_z(value, step):
    return lax.ppermute(value, "dp", dp_pairs(lax.axis_size("dp"), dz=step))


def move_y(value):
    return lax.ppermute(value, "dp", dp_pairs(lax.axis_size("dp"), dy=1))


def move_c(value):
    return lax.ppermute(value, "dp", dp_pairs(lax.axis_size("dp"), dc=1))


def move_x(value, step=1):
    count = lax.axis_size("mp")
    return lax.ppermute(value, "mp", [(i, (i + step) % count) for i in range(count)])


def places():
    dp = lax.axis_index("dp")
    return dp // 4, dp // 2 % 2, dp % 2, lax.axis_index("mp")


def row_maps(count, wide):
    depth = count // 4
    place = np.arange(D)
    rows = D // (count * wide)
    block = place // rows
    att = [block % depth, block // depth % 2, block // (2 * depth) % wide, block // (2 * depth * wide), place % rows]
    rows = D // count
    block = place // rows
    feed = [block % depth, block // depth % 2, 0 * block, block // (2 * depth), place % rows]
    return np.stack(att + feed, axis=1).astype(np.int32)


def rows_from(maps_ref, start, rows, wide):
    depth = lax.axis_size("dp") // 4
    dp = lax.axis_index("dp")

    def turned(i, here, size):
        there = maps_ref[:, start + i : start + i + 1] + here
        return jnp.where(there >= size, there - size, there)

    block = (turned(0, dp // 4, depth) * 2 + turned(1, dp // 2 % 2, 2)) * 2 + turned(3, dp % 2, 2)
    if wide > 1:
        block = block * wide + turned(2, lax.axis_index("mp"), wide)
    return block * rows + maps_ref[:, start + 4 : start + 5]


def gather_z(part):
    depth = lax.axis_size("dp") // 4
    return jnp.concatenate([part] + [move_z(part, -s) for s in range(1, depth)])


def gather_near(line):
    wide = lax.axis_size("mp")
    return [move_x(line, -s) for s in range(1, wide)], move_y(line)


def gather_far(near):
    along_x, along_y = near
    half = along_y.shape[1] // 2
    left = [move_y(b[:, :half]) for b in along_x]
    right = [move_x(along_y[:, half:], -s) for s in range(1, lax.axis_size("mp"))]
    return left, right


def gather_join(line, near, far):
    blocks = [line, near[1]]
    for along_x, first, second in zip(near[0], *far):
        blocks += [along_x, jnp.concatenate([first, second], axis=1)]
    return jnp.concatenate(blocks)


def add_up(first, *others):
    total = first.astype(F32)
    for other in others:
        total = total + other.astype(F32)
    return total


def blocks_of(rows, count):
    size = rows.shape[0] // count
    return [rows[i * size : (i + 1) * size] for i in range(count)]


def split(parts, count):
    return list(zip(*[blocks_of(v, count) for v in parts]))


def turn_y(value, step):
    return move_y(value)


def dot_nn(a, b):
    return lax.dot_general(a, b, (((1,), (0,)), ((), ())), preferred_element_type=F32)


def dot_nt(a, b):
    return lax.dot_general(a, b, (((1,), (1,)), ((), ())), preferred_element_type=F32)


def dot_tn(a, b):
    return lax.dot_general(a, b, (((0,), (0,)), ((), ())), preferred_element_type=F32)


def iota(shape, axis):
    return lax.broadcasted_iota(jnp.int32, shape, axis)


def norm_parts(rows_in):
    center = rows_in - jnp.mean(rows_in, axis=-1, keepdims=True)
    factor = lax.rsqrt(jnp.mean(center * center, axis=-1, keepdims=True) + 1e-06)
    return center * factor, factor


def norm_back(grad, unit, factor, gain):
    inner = grad * gain
    return factor * (
        inner
        - jnp.mean(inner, axis=-1, keepdims=True)
        - unit * jnp.mean(inner * unit, axis=-1, keepdims=True)
    )


def spread_rows():
    row, patch = iota((R, AREA), 0), iota((R, AREA), 1)
    return ((row % ROW < WIN) & (patch == row // ROW * WIN + row % ROW)).astype(F32).astype(BF16)


def row_masks():
    lane = iota((R, LANES), 1) % HEAD
    key = iota((R, LANES), 0)
    here = jnp.where(lane // ROW % 2 == 0, key // ROW, key % ROW)
    return (lane % ROW == here).astype(F32)


def offset_lanes(rows, base):
    lane = iota((rows, LANES), 1)
    in_h = (lane >= base) & (lane < base + ROW)
    in_w = (lane >= base + ROW) & (lane < base + 2 * ROW)
    return in_h, in_w


def query_offsets(table, base):
    in_h, in_w = offset_lanes(ROW, base)
    outs = []
    for a in range(WIN):
        group = table[a * ROW : (a + 1) * ROW]
        at_h = pltpu.roll(group, (HEAD - 13 + a) % LANES, 1)
        at_w = pltpu.roll(group, LANES - ROW + 1, 1, stride=1, stride_axis=0)
        both = jnp.where(in_h, at_h, jnp.where(in_w, at_w, 0.0))
        high = both.astype(BF16).astype(F32)
        outs.append(high + pltpu.roll(both - high, 2 * ROW, 1))
    return jnp.concatenate(outs, axis=0)


def offset_grads(grad, base):
    in_h, in_w = offset_lanes(R, base)
    column = iota((R, LANES), 0) % ROW
    from_w = jnp.where(in_w, grad, 0.0)
    for bit in (1, 2, 4, 8):
        from_w = jnp.where((ROW - 1 - column) & bit > 0, pltpu.roll(from_w, bit, 1), from_w)
    only_h = jnp.where(in_h, grad, 0.0)
    from_h = [pltpu.roll(only_h[a * ROW : (a + 1) * ROW], (HEAD + 13 - a) % LANES, 1) for a in range(WIN)]
    return jnp.concatenate(from_h, axis=0) + from_w


def table_places(start):
    row, lane = iota((TABLE, LANES), 0), iota((TABLE, LANES), 1)
    return (lane - start == TABLE - 1 - row).astype(F32)


def rate_of(keep_ref, branch):
    return jnp.where(keep_ref[0, branch] > 0, 1.0 / 0.9, 0.0).astype(F32)


def pack_kernel(
    keep_ref, qkv_ref, proj_ref, gain1_ref, shift1_ref, projb_ref, gain2_ref, shift2_ref, downb_ref, qvb_ref, grad_ref,
    first_ref, second_ref, params_ref, dm_ref,
):
    for tier, out in enumerate((first_ref, second_ref)):
        for i in range(3):
            out[:, i * HALF : (i + 1) * HALF] = qkv_ref[:, i * D + tier * HALF : i * D + (tier + 1) * HALF]
    second_ref[:, TIER:] = proj_ref[...]
    for i, ref in enumerate((gain1_ref, shift1_ref, projb_ref, gain2_ref, shift2_ref, downb_ref)):
        params_ref[i : i + 1] = ref[...].astype(F32).reshape(1, D)
    params_ref[6:8] = qvb_ref[...].astype(F32)
    dm_ref[...] = (rate_of(keep_ref, 1) * grad_ref[...].astype(F32)).astype(BF16)


def pack(keep, qkv_weight, *args):
    rows = qkv_weight.shape[0]
    return kernel_call(
        "pack",
        pack_kernel,
        11,
        [
            shape_of((rows, TIER), BF16), shape_of((rows, TIER + D), BF16), shape_of((8, D), F32),
            shape_of((AREA, D), BF16),
        ],
        smem=1, far=range(1, 11),
    )(keep, qkv_weight, *args)


def prepare_kernel(
    count, wide, tokens_ref, maps_ref, params_ref, relh_ref, relw_ref, mask_ref, upb_ref,
    a1_ref, turned_ref, att_ref, feed_ref, table_ref, fill_ref, wideb_ref,
):
    wideb_ref[...] = upb_ref[...].astype(F32).reshape(wideb_ref.shape)
    spread = spread_rows()
    x = dot_nn(spread, tokens_ref[...])
    source = iota((D, D), 1)
    att = (rows_from(maps_ref, 0, D // (count * wide), wide) == source).astype(F32).astype(BF16)
    att_ref[...] = att
    feed_ref[...] = (rows_from(maps_ref, 5, D // count, 1) == source).astype(F32).astype(BF16)
    unit, _ = norm_parts(x)
    a1 = (unit * params_ref[0:1] + params_ref[1:2]).astype(BF16)
    a1_ref[...] = dot_nt(a1, att).astype(BF16)
    turned_ref[...] = dot_nt(att, a1).astype(BF16)
    one = dot_tn(relh_ref[...], table_places(0).astype(BF16)) + dot_tn(relw_ref[...], table_places(W_START).astype(BF16))
    blank = jnp.zeros((HEAD, LANES), F32)
    table_ref[:HEAD, :] = jnp.concatenate([one, blank], axis=1).astype(BF16)
    table_ref[HEAD:, :] = jnp.concatenate([blank, pltpu.roll(one, HEAD, 1)], axis=1).astype(BF16)
    seen = dot_nt((mask_ref[...] > 0).astype(F32).astype(BF16), spread)
    key = iota((1, R), 1)
    fill_ref[...] = jnp.where(key % ROW >= WIN, -3e38, jnp.where(seen > 0.5, 0.0, -1e9))


def prepare(tokens, params, rel_h, rel_w, mask, upb):
    count, wide = lax.axis_size("dp"), lax.axis_size("mp")
    return kernel_call(
        "prepare",
        partial(prepare_kernel, count, wide),
        7,
        [
            shape_of((R, D), BF16), shape_of((D, R), BF16), shape_of((D, D), BF16), shape_of((D, D), BF16),
            shape_of((LANES, 2 * LANES), BF16), shape_of((1, R), F32), shape_of((1, upb.shape[0]), F32),
        ],
        far=(0, 1, 3, 4, 5, 6),
    )(tokens, row_maps(count, wide), params, rel_h, rel_w, mask, upb)


def act_kernel(dm_ref, down_ref, out_ref, sum_ref):
    sum_ref[...] = jnp.sum(dm_ref[...].astype(F32), axis=0, keepdims=True)
    out_ref[...] = dot_nt(dm_ref[...], down_ref[...])


def act_grad(dm, down):
    return kernel_call("act", act_kernel, 2, [shape_of((AREA, down.shape[0]), F32), shape_of((1, D), F32)])(dm, down)


def heads_forward(qkv_ref, tables, fill, p_ref, out):
    ones = row_masks()
    left = iota((R, LANES), 1) < HEAD
    for pair in range(PAIRS // 2):
        at = pair * LANES
        q2 = qkv_ref[:, at : at + LANES]
        k2 = qkv_ref[:, HALF + at : HALF + at + LANES].astype(F32)
        v2 = qkv_ref[:, 2 * HALF + at : 2 * HALF + at + LANES]
        products = dot_nn(q2, tables)
        q2 = q2.astype(F32) * HEAD**-0.5
        outs = []
        for side in range(2):
            mine = left if side == 0 else ~left
            offsets = query_offsets(products[:, side * LANES : (side + 1) * LANES], HEAD * (1 - side))
            q_aug = jnp.where(mine, q2, offsets).astype(BF16)
            k_aug = jnp.where(mine, k2, ones).astype(BF16)
            scores = dot_nt(q_aug, k_aug)
            scores = jnp.where(fill < 0.0, fill, scores)
            expo = jnp.exp(scores - jnp.max(scores, axis=-1, keepdims=True))
            probs = (expo / jnp.sum(expo, axis=-1, keepdims=True)).astype(BF16)
            p_ref[2 * pair + side] = probs
            outs.append(dot_nn(probs, v2))
        out(at, jnp.where(left, outs[0], outs[1]).astype(BF16))


def project(a1_ref, own_ref, other_ref, bias, qkv_ref):
    total = dot_nn(a1_ref[:, :HALF], own_ref[:, :TIER]) + dot_nn(a1_ref[:, HALF:], other_ref[:, :TIER])
    qkv_ref[...] = (total + bias).astype(BF16)


def tier_bias(params_ref, tier):
    at = tier * HALF
    return jnp.concatenate(
        [
            params_ref[6:7, at : at + HALF],
            jnp.zeros((1, HALF), F32),
            params_ref[7:8, at : at + HALF],
        ],
        axis=1,
    )


def attend_first_kernel(a1_ref, own_ref, other_ref, params_ref, table_ref, fill_ref, qkv_ref, p_ref, o_ref):
    project(a1_ref, own_ref, other_ref, tier_bias(params_ref, 0), qkv_ref)

    def out(at, value):
        o_ref[:, at : at + LANES] = value

    heads_forward(qkv_ref, table_ref[...], fill_ref[...], p_ref, out)


def attend_first(*args):
    return kernel_call(
        "attend1",
        attend_first_kernel,
        6,
        [shape_of((R, TIER), BF16), shape_of((HEADS // 2, R, R), BF16), shape_of((R, HALF), BF16)],
    )(*args)


def attend_second_kernel(
    keep_ref, a1_ref, own_ref, other_ref, params_ref, table_ref, fill_ref, first_ref, x_ref, att_ref,
    qkv_ref, p_ref, turned_ref, mid_ref, a2_ref,
    o_ref,
):
    project(a1_ref, own_ref, other_ref, tier_bias(params_ref, 1), qkv_ref)
    o_ref[:, :HALF] = first_ref[...]

    def out(at, value):
        o_ref[:, HALF + at : HALF + at + LANES] = value

    heads_forward(qkv_ref, table_ref[...], fill_ref[...], p_ref, out)
    rows = dot_tn(spread_rows(), o_ref[...]).astype(BF16)
    moved = dot_nt(rows, att_ref[...]).astype(BF16)
    branch = dot_nn(moved[:, :HALF], own_ref[:, TIER:]) + dot_nn(moved[:, HALF:], other_ref[:, TIER:])
    turned_ref[...] = dot_nt(att_ref[...], rows).astype(BF16)
    rate = rate_of(keep_ref, 0)
    middle = x_ref[...].astype(F32) + rate * (branch + params_ref[2:3])
    mid_ref[...] = middle
    unit, _ = norm_parts(middle)
    a2_ref[...] = (unit * params_ref[3:4] + params_ref[4:5]).astype(BF16)


def attend_second(*args):
    return kernel_call(
        "attend2",
        attend_second_kernel,
        10,
        [
            shape_of((R, TIER), BF16), shape_of((HEADS // 2, R, R), BF16), shape_of((D, AREA), BF16),
            shape_of((AREA, D), F32), shape_of((AREA, D), BF16),
        ],
        smem=1, scratch=[pltpu.VMEM((R, D), BF16)],
    )(*args)


def feed_kernel(a2_ref, up_ref, upb_ref, gact_ref, g_ref, dh_ref, da2_ref):
    total = None
    for at in range(0, up_ref.shape[1], STEP):
        here = slice(at, at + STEP)
        hidden = dot_nn(a2_ref[...], up_ref[:, here]) + upb_ref[:, here]
        phi = 0.5 + 0.5 * lax.erf(hidden * 0.5**0.5)
        g_ref[:, here] = (hidden * phi).astype(BF16)
        slope = phi + hidden * (jnp.exp(-0.5 * hidden * hidden) * 0.3989422804014327)
        dh = (gact_ref[:, here] * slope).astype(BF16)
        dh_ref[:, here] = dh
        part = dot_nt(dh, up_ref[:, here])
        total = part if total is None else total + part
    da2_ref[...] = total.astype(da2_ref.dtype)


def feed(a2, up, upb, gact, kind):
    hidden = up.shape[1]
    return kernel_call(
        "feed",
        feed_kernel,
        4,
        [shape_of((AREA, hidden), BF16), shape_of((AREA, hidden), BF16), shape_of((AREA, D), kind)],
    )(a2, up, upb, gact)


def feed_weights_kernel(count, map_ref, down_ref, *refs):
    dms, acts, a2s, dhs = (refs[i * count : (i + 1) * count] for i in range(4))
    refs = refs[4 * count :]
    depth = lax.axis_size("dp") // 4
    rows = HALF // (2 * depth)
    for lefts, rights, by_z in ((dms, acts, Z_FIRST[0]), (a2s, dhs, Z_FIRST[1])):
        blocks = depth if by_z else 2
        outs, refs = refs[: 2 * blocks], refs[2 * blocks :]
        turned = [dot_nt(map_ref[...], left[...]).astype(BF16) for left in lefts]
        for at in range(0, rights[0].shape[1], STEP):
            here = slice(at, at + STEP)
            total = dot_nn(turned[0], rights[0][:, here])
            for j in range(1, count):
                total = total + dot_nn(turned[j], rights[j][:, here])
            total = total.astype(BF16)
            for s in range(2):
                for y in range(2):
                    if not by_z:
                        start = s * HALF + y * HALF // 2
                        outs[2 * s + y][:, here] = total[start : start + HALF // 2]
                        continue
                    for z in range(depth):
                        start = s * HALF + (y * depth + z) * rows
                        outs[depth * s + z][y * rows : (y + 1) * rows, here] = total[start : start + rows]
    sum_ref, *outs = refs
    for j in range(count):
        outs[j][...] = dot_nn(acts[j][...], down_ref[...]).astype(outs[j].dtype)
    sums = jnp.sum(dhs[0][...].astype(F32), axis=0, keepdims=True)
    for j in range(1, count):
        sums = sums + jnp.sum(dhs[j][...].astype(F32), axis=0, keepdims=True)
    sum_ref[...] = sums


def feed_weights(row_map, down, dms, acts, a2s, dhs):
    count = len(dms)
    columns = acts[0].shape[1]
    blocks = [lax.axis_size("dp") // 4 if by_z else 2 for by_z in Z_FIRST]
    made = kernel_call(
        "feedw",
        partial(feed_weights_kernel, count),
        2 + 4 * count,
        [shape_of((HALF // n, columns), BF16) for n in blocks for _ in range(2 * n)]
        + [shape_of((1, columns), F32)]
        + [shape_of((AREA, D), F32 if j == 0 else BF16) for j in range(count)],
    )(row_map, down, *dms, *acts, *a2s, *dhs)
    grads = []
    for n in blocks:
        grads += [made[:n], made[n : 2 * n]]
        made = made[2 * n :]
    return *grads, *made


def heads_back(qkv_ref, p_ref, do_at, tables, dqkv_ref):
    ones = row_masks()
    left = iota((R, LANES), 1) < HEAD
    table_grad = jnp.zeros((LANES, 2 * LANES), F32)
    for pair in range(PAIRS // 2):
        at = pair * LANES
        q2 = qkv_ref[:, at : at + LANES]
        q_wide = q2.astype(F32)
        k2 = qkv_ref[:, HALF + at : HALF + at + LANES].astype(F32)
        v2 = qkv_ref[:, 2 * HALF + at : 2 * HALF + at + LANES]
        do2 = do_at(at).astype(F32)
        dq2 = dk2 = dv2 = None
        offsets = []
        for side in range(2):
            mine = left if side == 0 else ~left
            probs = p_ref[2 * pair + side]
            do_mine = jnp.where(mine, do2, 0.0).astype(BF16)
            dv = dot_tn(probs, do_mine)
            dp = dot_nt(do_mine, v2)
            wide = probs.astype(F32)
            ds = (wide * (dp - jnp.sum(wide * dp, axis=-1, keepdims=True))).astype(BF16)
            k_aug = jnp.where(mine, k2, ones).astype(BF16)
            dq_aug = dot_nn(ds, k_aug)
            offsets.append(offset_grads(dq_aug, HEAD * (1 - side)))
            dk = dot_tn(ds, jnp.where(mine, q_wide, 0.0).astype(BF16))
            if side == 0:
                dq2, dk2, dv2 = dq_aug, dk, dv
            else:
                dq2, dk2, dv2 = jnp.where(mine, dq_aug, dq2), dk2 + dk, dv2 + dv
        spread = jnp.concatenate(offsets, axis=1).astype(BF16)
        dq2 = dq2 * HEAD**-0.5 + dot_nt(spread, tables)
        table_grad = table_grad + dot_tn(q2, spread)
        dqkv_ref[:, at : at + LANES] = dq2.astype(BF16)
        dqkv_ref[:, HALF + at : HALF + at + LANES] = (dk2 * HEAD**-0.5).astype(BF16)
        dqkv_ref[:, 2 * HALF + at : 2 * HALF + at + LANES] = dv2.astype(BF16)
    return table_grad[:HEAD, :LANES] + pltpu.roll(table_grad[HEAD:, LANES:], HEAD, 1)


def back_norm_kernel(
    keep_ref, da2_ref, got_ref, mid_ref, g_ref, params_ref, own_ref, other_ref, att_ref,
    dmid_ref, do_ref, dy_ref, sums_ref,
):
    da2 = da2_ref[...] + got_ref[...].astype(F32)
    unit, factor = norm_parts(mid_ref[...])
    dmid = g_ref[...].astype(F32) + norm_back(da2, unit, factor, params_ref[3:4])
    dmid_ref[...] = dmid
    dy = (rate_of(keep_ref, 0) * dmid).astype(BF16)
    dy_ref[...] = dy
    moved = jnp.concatenate(
        [dot_nt(dy, own_ref[:, TIER:]).astype(BF16), dot_nt(dy, other_ref[:, TIER:]).astype(BF16)], axis=1
    )
    rows = dot_nn(moved, att_ref[...]).astype(BF16)
    do_ref[...] = dot_nn(spread_rows(), rows).astype(BF16)
    sums_ref[0:1] = jnp.sum(dy.astype(F32), axis=0, keepdims=True)
    sums_ref[1:2] = jnp.sum(da2 * unit, axis=0, keepdims=True)
    sums_ref[2:3] = jnp.sum(da2, axis=0, keepdims=True)


def back_norm(*args):
    return kernel_call(
        "backnorm",
        back_norm_kernel,
        9,
        [shape_of((AREA, D), F32), shape_of((R, D), BF16), shape_of((AREA, D), BF16), shape_of((3, D), F32)],
        smem=1,
    )(*args)


def back_kernel(tier, do_ref, turned_ref, qkv_ref, p_ref, table_ref, *refs):
    if tier == 0:
        o_ref, dy_ref, *refs = refs
    dqkv_ref, *refs, sums_ref, tab_ref = refs
    tab_ref[...] = heads_back(
        qkv_ref, p_ref, lambda at: do_ref[:, tier * HALF + at : tier * HALF + at + LANES], table_ref[...], dqkv_ref
    )
    wide = lax.axis_size("mp")
    blocks = (wide, 2)[tier]
    rows = HALF // (2 * wide)
    for s in range(2):
        part = dot_nn(turned_ref[s * HALF : (s + 1) * HALF], dqkv_ref[...]).astype(BF16)
        outs = refs[s * blocks : (s + 1) * blocks]
        if tier == 0:
            more = dot_nn(o_ref[s * HALF : (s + 1) * HALF], dy_ref[...]).astype(BF16)
        for x in range(wide):
            if tier == 0:
                outs[x][:, :TIER] = part[2 * x * rows : 2 * (x + 1) * rows]
                outs[x][:, TIER:] = more[2 * x * rows : 2 * (x + 1) * rows]
                continue
            for y in range(2):
                at_row = (x * 2 + y) * rows
                outs[y][x * rows : (x + 1) * rows] = part[at_row : at_row + rows]
    sums_ref[:, :HALF] = jnp.sum(dqkv_ref[:, :HALF].astype(F32), axis=0, keepdims=True)
    sums_ref[:, HALF:] = jnp.sum(dqkv_ref[:, 2 * HALF :].astype(F32), axis=0, keepdims=True)


def back(tier, *args):
    blocks = (lax.axis_size("mp"), 2)[tier]
    dqkv, *grads, sums, table = kernel_call(
        f"back{tier + 1}",
        partial(back_kernel, tier),
        len(args),
        [shape_of((R, TIER), BF16)]
        + [shape_of((HALF // blocks, TIER + D * (tier == 0)), BF16)] * (2 * blocks)
        + [shape_of((1, D), F32), shape_of((HEAD, LANES), F32)],
    )(*args)
    return dqkv, grads[:blocks], grads[blocks:], sums, table


def finish_kernel(
    wide, keep_ref, dq1_ref, dq2_ref, own1_ref, other1_ref, own2_ref, other2_ref, att_ref, x_ref, dmid_ref,
    params_ref, mid_ref, m_ref, mgot_ref, downb_ref, upb_ref, sums0_ref, sums1_ref, sums2_ref, tab1_ref, tab2_ref,
    dx_ref, result_ref, small_ref,
):
    spread = spread_rows()
    dq1, dq2 = dot_tn(spread, dq1_ref[...]).astype(BF16), dot_tn(spread, dq2_ref[...]).astype(BF16)
    halves = []
    for first, second in ((own1_ref, own2_ref), (other1_ref, other2_ref)):
        halves.append(dot_nt(dq1, first[...]) + dot_nt(dq2, second[:, :TIER]))
    moved = jnp.concatenate(halves, axis=1)
    high = moved.astype(BF16)
    low = (moved - high.astype(F32)).astype(BF16)
    da1 = dot_nn(high, att_ref[...]) + dot_nn(low, att_ref[...])
    unit, factor = norm_parts(x_ref[...].astype(F32))
    dx_ref[...] = (dmid_ref[...] + norm_back(da1, unit, factor, params_ref[0:1])).astype(BF16)
    rate = rate_of(keep_ref, 1)
    total = m_ref[...] + mgot_ref[...].astype(F32) + params_ref[5:6]
    result_ref[...] = (mid_ref[...] + rate * total).astype(BF16)

    small_ref[...] = jnp.zeros(small_ref.shape, F32)

    def put(name, value):
        for i in range(D // LANES):
            small_ref[piece(SMALL[name] + i)] = value[:, i * LANES : (i + 1) * LANES]

    put("gain1", jnp.sum(da1 * unit, axis=0, keepdims=True))
    put("shift1", jnp.sum(da1, axis=0, keepdims=True))
    put("projb", sums0_ref[0:1])
    put("gain2", sums0_ref[1:2])
    put("shift2", sums0_ref[2:3])
    put("qbias", jnp.concatenate([sums1_ref[:, :HALF], sums2_ref[:, :HALF]], axis=1))
    put("vbias", jnp.concatenate([sums1_ref[:, HALF:], sums2_ref[:, HALF:]], axis=1))
    put("downb", downb_ref[...])
    table = tab1_ref[...] + tab2_ref[...]
    low, high = table[: HEAD // 2], table[HEAD // 2 :]
    lane = iota(low.shape, 1)
    packed = jnp.where(
        lane < 32,
        low,
        jnp.where(
            lane < 64,
            pltpu.roll(low, (32 - W_START) % LANES, 1),
            jnp.where(lane < 96, pltpu.roll(high, 64, 1), pltpu.roll(high, (96 - W_START) % LANES, 1)),
        ),
    )
    for i in range(HEAD // 2):
        small_ref[piece(SMALL_TABLE + i)] = packed[i : i + 1]
    count = lax.axis_size("dp")
    size = upb_ref.shape[1] // count
    for m in range(wide):
        for i in range(count):
            rows, lanes = piece(SMALL_UP + m * count + i)
            value = upb_ref[:, i * size : (i + 1) * size]
            lanes = slice(lanes.start, lanes.start + size)
            small_ref[rows, lanes] = jnp.where(lax.axis_index("mp") == m, value, 0.0)


def finish(wide, rows, *args):
    return kernel_call(
        "finish",
        partial(finish_kernel, wide),
        21,
        [shape_of((AREA, D), BF16), shape_of((AREA, D), BF16), shape_of((rows, TIER), F32)],
        smem=1, out_far=(0, 1),
    )(*args)


def outputs_kernel(
    n_parts, rows, *refs
):
    parts, refs = refs[:n_parts], refs[n_parts:]
    gain1_ref, shift1_ref, qv_ref, relh_ref, relw_ref, projb_ref, gain2_ref, shift2_ref, upb_ref, downb_ref = refs[:10]
    table_ref, up_ref = refs[10:]
    total = parts[0][...]
    for part in parts[1:]:
        total = total + part[part.shape[0] - rows :].astype(F32)
    flat = {
        "gain1": gain1_ref, "shift1": shift1_ref, "projb": projb_ref, "gain2": gain2_ref, "shift2": shift2_ref,
        "downb": downb_ref,
    }

    def at(place):
        here, lanes = piece(place)
        return total[here, lanes]

    for i in range(D // LANES):
        here = slice(i * LANES, (i + 1) * LANES)
        for name, ref in flat.items():
            ref[here] = at(SMALL[name] + i)[0]
        qv_ref[0:1, here] = at(SMALL["qbias"] + i)
        qv_ref[1:2, here] = at(SMALL["vbias"] + i)
    for i in range(HEAD // 2):
        table_ref[i : i + 1] = at(SMALL_TABLE + i)
    for start, ref in ((0, relh_ref), (32, relw_ref)):
        for half in range(2):
            ref[:, half * 32 : half * 32 + 32] = lax.dot_general(
                table_places(start + 64 * half), table_ref[...], (((1,), (1,)), ((), ())),
                precision=lax.Precision.HIGHEST, preferred_element_type=F32,
            )
    for i in range(up_ref.shape[0]):
        up_ref[i : i + 1] = at(SMALL_UP + i)
    place = lax.axis_index("mp") * lax.axis_size("dp") + lax.axis_index("dp")
    upb_ref[...] = up_ref[place, : upb_ref.shape[0]]


def outputs(parts, size, ups):
    row = shape_of((D,), F32)
    table = shape_of((TABLE, HEAD), F32)
    return kernel_call(
        "outputs",
        partial(outputs_kernel, len(parts), parts[0].shape[0]),
        len(parts),
        [row, row, shape_of((2, D), F32), table, table, row, row, row, shape_of((size,), F32), row],
        scratch=[pltpu.VMEM((HEAD // 2, LANES), F32), pltpu.VMEM((ups, LANES), F32)],
        out_far=range(10),
    )(*parts)


def per_device(
    tokens, ln1_gain, ln1_bias, qkv_weight, qv_bias, rel_pos_h, rel_pos_w, proj_weight, proj_bias,
    ln2_gain, ln2_bias, fc1_weight, fc1_bias, fc2_weight, fc2_bias, keep_mask, key_mask, out_grad,
):
    wide = lax.axis_size("mp")
    hidden = fc1_weight.shape[1]
    first, second, params, dm = pack(
        keep_mask, qkv_weight, proj_weight, ln1_gain, ln1_bias, proj_bias, ln2_gain, ln2_bias, fc2_bias, qv_bias, out_grad
    )
    made, chains = {}, {}

    def gated(value, task, kind):
        others = [made[name] for name in GATES.get(f"{task}:{kind}", ())]
        return after(value, *others) if others else value

    def front(name):
        if name == "dm":
            sent = gated(dm, name, "s")
            return gated([move_x(sent, -s) for s in range(1, wide)], name, "r")
        if name == "prep":
            return prepare(gated(tokens, name, "s"), params, rel_pos_h, rel_pos_w, key_mask, fc1_bias)
        if name == "act0":
            return act_grad(gated(dm, name, "s"), fc2_weight)
        if name == "act1":
            return [act_grad(v, fc2_weight) for v in gated(made["dm"], name, "s")]
        if name == "attend1":
            a1, _, _, _, tables, fill, _ = made["prep"]
            return attend_first(gated(a1, name, "s"), chains["1"], made["c1"], params, tables, fill)
        step, tier = name
        if step == "z":
            sent = gated((first, second)[int(tier) - 1], name, "s")
            chains[tier] = gated(gather_z(sent), name, "r")
            return chains[tier]
        if step == "n":
            return gated(gather_near(gated(chains[tier], name, "s")), name, "r")
        if step == "f":
            made["n" + tier] = gated(made["n" + tier], name, "s")
            return gated(gather_far(made["n" + tier]), name, "r")
        chains[tier] = gated(gather_join(chains[tier], made["n" + tier], made["f" + tier]), name, "s")
        return gated(move_c(chains[tier]), name, "r")

    for name in FRONT:
        made[name] = front(name)
    a1, a1_turned, att_map, feed_map, tables, fill, upb = made["prep"]
    dms = [dm, *made["dm"]]
    acts = [made["act0"], *made["act1"]]
    gacts, downb = [v[0] for v in acts], acts[0][1]
    own1, other1, own2, other2 = chains["1"], made["c1"], chains["2"], made["c2"]
    qkv1, probs1, att1 = made["attend1"]
    qkv2, probs2, att_turned, middle, a2 = attend_second(
        keep_mask, a1, own2, other2, params, tables, fill, att1, tokens, att_map
    )

    a2s = [a2] + [move_x(a2, -s) for s in range(1, wide)]
    fed = [feed(a2, fc1_weight, upb, gacts[0], F32)]
    for j in range(1, wide):
        fed.append(feed(after(a2s[j], fed[-1][2]), fc1_weight, upb, gacts[j], BF16))
    da2 = fed[0][2]
    got = [move_x(fed[s][2], s) for s in range(1, wide)]
    down_keep, down_send, up_keep, up_send, upb_sum, *outs = feed_weights(
        after(feed_map, fed[-1][2]), fc2_weight, dms, [f[0] for f in fed], a2s, [f[1] for f in fed]
    )
    got, down_send, up_send, outs = lax.optimization_barrier((got, down_send, up_send, outs))
    got = got[0] if wide == 2 else add_up(*got)
    depth = lax.axis_size("dp") // 4
    moves = {"x": (move_x, wide), "y": (turn_y, 2), "z": (move_z, depth)}
    small_rows = -(-(SMALL_UP + wide * lax.axis_size("dp")) // PIECES)
    small_rows += -small_rows % 16

    def cores(name, keep, send, axes):
        sent = gated(send, f"{name}c", "s")
        got = gated([move_c(v) for v in sent], f"{name}c", "r")
        chains[name] = (list(zip(keep, got)), axes)
        return got

    def along(name, axis):
        sums, axes = chains[name]
        move, _ = moves[axis]
        sent = [add_up(*v).astype(BF16) for v in sums[1:]]
        if name == "b":
            extra = chains["s"].astype(BF16)
            sent = [jnp.concatenate([v, extra]) for v in sent]
        sent = gated(sent, f"{name}{axis}", "s")
        got = gated([move(v, s + 1) for s, v in enumerate(sent)], f"{name}{axis}", "r")
        rest = [*sums[0], *got]
        if name == "b":
            rows = sums[0][0].shape[0]
            rest = [*sums[0], *[v[:rows] for v in got]]
            if axis == "z":
                chains["s"] = [chains["s"], *got]
            else:
                chains["s"] = add_up(chains["s"], *[v[rows:] for v in got])
        axes = axes[axes.index(axis) + 1 :]
        chains[name] = (split(rest, moves[axes[0]][1]), axes) if axes else (rest, axes)
        return got

    def small_cores():
        flat = gated(made["finish"][2], "sc", "s")
        got = gated(move_c(flat), "sc", "r")
        chains["s"] = flat + got
        return got

    def task(name):
        if name == "norm":
            return back_norm(keep_mask, da2, got, middle, out_grad, params, own2, other2, att_map)
        if name in ("back1", "back2"):
            tier = int(name[-1]) - 1
            do = gated(made["norm"][1], name, "s")
            more = (att_turned, made["norm"][2]) if tier == 0 else ()
            return back(tier, do, a1_turned, (qkv1, qkv2)[tier], (probs1, probs2)[tier], tables, *more)
        if name == "m":
            moved = [move_x(v, s + 1) for s, v in enumerate(gated(outs[1:], "m", "s"))]
            moved = gated(moved, "m", "r")
            return moved[0] if wide == 2 else add_up(*moved)
        if name == "finish":
            first, second = made["back1"], made["back2"]
            mid = gated(middle, "finish", "s")
            return finish(
                wide, small_rows, keep_mask, first[0], second[0], own1, other1, own2, other2, att_map, tokens,
                made["norm"][0], params, mid, outs[0], made["m"], downb, upb_sum, made["norm"][3], first[3], second[3],
                first[4], second[4],
            )
        chain, axis = name
        if chain == "s":
            return small_cores()
        if axis != "c":
            return along(chain, axis)
        if chain in "du":
            keep, send = (down_keep, down_send) if chain == "d" else (up_keep, up_send)
            return cores(chain, keep, send, "zy" if Z_FIRST["du".index(chain)] else "yz")
        tier = "ab".index(chain)
        return cores(chain, made[f"back{tier + 1}"][1], made[f"back{tier + 1}"][2], ("xyz", "yxz")[tier])

    for name in ORDER:
        made[name] = task(name)
    grad_in, result, _ = made["finish"]
    small = chains["s"]
    down_grad, up_grad, rows1, rows2 = (add_up(*chains[name][0]) for name in "duab")
    proj_grad = rows1[:, TIER:]

    pieces = [
        piece
        for i in range(3)
        for piece in (rows1[:, i * HALF : (i + 1) * HALF], rows2[:, i * HALF : (i + 1) * HALF])
    ]
    qkv_grad = jnp.concatenate(pieces, axis=1)

    gain1, shift1, qv_grad, relh_grad, relw_grad, projb, gain2, shift2, up_bias_grad, downb = outputs(
        small, hidden // lax.axis_size("dp"), wide * lax.axis_size("dp")
    )
    return (
        result, grad_in, gain1, shift1, qkv_grad, qv_grad, relh_grad, relw_grad, proj_grad, projb, gain2, shift2,
        up_grad, up_bias_grad, down_grad.T, downb,
    )


def solution(mesh):
    in_specs = (
        P(("dp", "mp"), None),
        P(),
        P(),
        P(("dp", "mp"), None),
        P(),
        P(),
        P(),
        P(("dp", "mp"), None),
        P(),
        P(),
        P(),
        P(None, "mp"),
        P("mp"),
        P("mp", None),
        P(),
        P(("dp", "mp"), None),
        P(("dp", "mp"), None),
        P(("dp", "mp"), None),
    )
    out_specs = (
        P(("dp", "mp"), None),
        P(("dp", "mp"), None),
        P(),
        P(),
        P(("dp", "mp"), None),
        P(),
        P(),
        P(),
        P(("dp", "mp"), None),
        P(),
        P(),
        P(),
        P("dp", "mp"),
        P(("mp", "dp")),
        P("mp", "dp"),
        P(),
    )
    return jax.shard_map(
        per_device, mesh=mesh, in_specs=in_specs, out_specs=out_specs, check_vma=False
    )
```

```python
from functools import partial

import jax
import jax.numpy as jnp
import numpy as np
from jax import lax
from jax.experimental import pallas as pl
from jax.experimental.pallas import tpu as pltpu
from jax.sharding import PartitionSpec as P

D = 768
HEADS = 12
HEAD = 64
WIN = 14
AREA = WIN * WIN
ROW = 16
R = WIN * ROW
PAIRS = HEADS // 2
LANES = 128
TABLE = 2 * WIN - 1
TWICE = 59
W_START = HEAD + ROW + 2
HALF = D // 2
STEP = 384
TIER = 3 * HALF
F32 = jnp.float32
BF16 = jnp.bfloat16
VMEM = pl.BlockSpec(memory_space=pltpu.VMEM)
SMEM = pl.BlockSpec(memory_space=pltpu.SMEM)
LIMIT = 20 * 2**20
Z_FIRST = (False, False)
TREE = (True, True)
FRONT = ('dm', 'z1', 'prep', 'act1', 'z2', 'n1', 'n2', 'act0', 'f2', 'f1', 'c1', 'attend1', 'c2')
ORDER = ('dc', 'dy', 'm', 'norm', 'back2', 'bc', 'back1', 'finish', 'ac', 'sc', 'by', 'bx', 'ax', 'd0', 'd1', 'bz', 'uc', 'uy', 'ay', 'u0', 'u1', 'az')
GATES = {'n1:s': ['prep', 'dm'], 'n2:s': ['z2'], 'f1:s': ['n1'], 'act1:s': ['dm'], 'attend1:s': ['dm', 'f1'], 'z1:s': ['dm'], 'back1:s': ['dc'], 'back2:s': ['m', 'dc', 'norm'], 'finish:s': ['bc'], 'ay:r': ['ac', 'back1', 'd1'], 'uc:s': ['dc'], 'bc:s': ['dy'], 'bx:r': ['dy'], 'bz:r': ['bc'], 'd0:s': ['finish'], 'd1:r': ['dy'], 'az:r': ['bz'], 'u1:r': ['by', 'bx'], 'uc:r': ['back2'], 'sc:r': ['ac']}
ROUTE = {"y": "b", "x": "b", "z": "b"}
CHEAP = pl.CostEstimate(flops=1, bytes_accessed=1, transcendentals=0)
SMALL = {"gain1": 0, "shift1": 6, "qbias": 12, "vbias": 18, "projb": 24, "gain2": 30, "shift2": 36, "downb": 42}
SMALL_TABLE = 48
SMALL_UP = SMALL_TABLE + HEAD // 2
PIECES = TIER // LANES


def piece(place):
    return slice(place // PIECES, place // PIECES + 1), slice(place % PIECES * LANES, (place % PIECES + 1) * LANES)


def shape_of(shape, kind):
    return jax.ShapeDtypeStruct(shape, kind)


def kernel_call(name, body, n_in, outs, *, smem=0, scratch=(), far=(), out_far=()):
    call = pl.pallas_call(
        body,
        name=name,
        in_specs=[SMEM] * smem + [VMEM] * (n_in - smem),
        out_specs=[VMEM] * len(outs),
        out_shape=[o if i in out_far else pltpu.VMEM(o.shape, o.dtype) for i, o in enumerate(outs)],
        scratch_shapes=list(scratch),
        compiler_params=pltpu.CompilerParams(vmem_limit_bytes=LIMIT),
        cost_estimate=CHEAP,
    )

    def run(*args):
        spaces = [pltpu.HBM if i in far else pltpu.VMEM for i in range(smem, n_in)]
        return call(*args[:smem], *map(pltpu.with_memory_space_constraint, args[smem:], spaces))

    return run


def after(value, *others):
    return lax.optimization_barrier((value,) + others)[0]


def dp_pairs(count, dz=0, dy=0, dc=0):
    depth = count // 4
    pairs = []
    for place in range(count):
        z, y, c = place // 4, place // 2 % 2, place % 2
        pairs.append((place, (z + dz) % depth * 4 + (y + dy) % 2 * 2 + (c + dc) % 2))
    return pairs


def move_z(value, step):
    return lax.ppermute(value, "dp", dp_pairs(lax.axis_size("dp"), dz=step))


def swap_z(value, mask):
    pairs = [(place, place ^ (mask * 4)) for place in range(lax.axis_size("dp"))]
    return lax.ppermute(value, "dp", pairs)


def move_y(value):
    return lax.ppermute(value, "dp", dp_pairs(lax.axis_size("dp"), dy=1))


def move_c(value):
    return lax.ppermute(value, "dp", dp_pairs(lax.axis_size("dp"), dc=1))


def move_x(value, step=1):
    count = lax.axis_size("mp")
    return lax.ppermute(value, "mp", [(i, (i + step) % count) for i in range(count)])


def places():
    dp = lax.axis_index("dp")
    return dp // 4, dp // 2 % 2, dp % 2, lax.axis_index("mp")


def row_maps(count, wide):
    depth = count // 4
    place = np.arange(D)
    rows = D // (count * wide)
    block = place // rows
    att = [block % depth, block // depth % 2, block // (2 * depth) % wide, block // (2 * depth * wide), place % rows]
    rows = D // count
    block = place // rows
    feed = [block % depth, block // depth % 2, 0 * block, block // (2 * depth), place % rows]
    return np.stack(att + feed, axis=1).astype(np.int32)


def rows_from(maps_ref, start, rows, wide, paired=False):
    depth = lax.axis_size("dp") // 4
    dp = lax.axis_index("dp")

    def turned(i, here, size):
        there = maps_ref[:, start + i : start + i + 1] + here
        return jnp.where(there >= size, there - size, there)

    across = maps_ref[:, start : start + 1] ^ (dp // 4) if paired else turned(0, dp // 4, depth)
    block = (across * 2 + turned(1, dp // 2 % 2, 2)) * 2 + turned(3, dp % 2, 2)
    if wide > 1:
        block = block * wide + turned(2, lax.axis_index("mp"), wide)
    return block * rows + maps_ref[:, start + 4 : start + 5]


def gather_z(part):
    depth = lax.axis_size("dp") // 4
    return jnp.concatenate([part] + [move_z(part, -s) for s in range(1, depth)])


def gather_near(line):
    wide = lax.axis_size("mp")
    return [move_x(line, -s) for s in range(1, wide)], move_y(line)


def gather_far(near):
    along_x, along_y = near
    half = along_y.shape[1] // 2
    left = [move_y(b[:, :half]) for b in along_x]
    right = [move_x(along_y[:, half:], -s) for s in range(1, lax.axis_size("mp"))]
    return left, right


def gather_join(line, near, far):
    blocks = [line, near[1]]
    for along_x, first, second in zip(near[0], *far):
        blocks += [along_x, jnp.concatenate([first, second], axis=1)]
    return jnp.concatenate(blocks)


def add_up(first, *others):
    total = first.astype(F32)
    for other in others:
        total = total + other.astype(F32)
    return total


def blocks_of(rows, count):
    size = rows.shape[0] // count
    return [rows[i * size : (i + 1) * size] for i in range(count)]


def split(parts, count):
    return list(zip(*[blocks_of(v, count) for v in parts]))


def turn_y(value, step):
    return move_y(value)


def dot_nn(a, b):
    return lax.dot_general(a, b, (((1,), (0,)), ((), ())), preferred_element_type=F32)


def dot_nt(a, b):
    return lax.dot_general(a, b, (((1,), (1,)), ((), ())), preferred_element_type=F32)


def dot_tn(a, b):
    return lax.dot_general(a, b, (((0,), (0,)), ((), ())), preferred_element_type=F32)


def iota(shape, axis):
    return lax.broadcasted_iota(jnp.int32, shape, axis)


def norm_parts(rows_in):
    center = rows_in - jnp.mean(rows_in, axis=-1, keepdims=True)
    factor = lax.rsqrt(jnp.mean(center * center, axis=-1, keepdims=True) + 1e-06)
    return center * factor, factor


def norm_back(grad, unit, factor, gain):
    inner = grad * gain
    return factor * (
        inner
        - jnp.mean(inner, axis=-1, keepdims=True)
        - unit * jnp.mean(inner * unit, axis=-1, keepdims=True)
    )


def spread_rows():
    row, patch = iota((R, AREA), 0), iota((R, AREA), 1)
    return ((row % ROW < WIN) & (patch == row // ROW * WIN + row % ROW)).astype(F32).astype(BF16)


def row_masks(down=False):
    lane = iota((R, LANES), 1) % HEAD
    key = iota((R, LANES), 0)
    column = ROW - 1 - key % ROW if down else key % ROW
    here = jnp.where(lane // ROW % 2 == 0, key // ROW, column)
    return (lane % ROW == here).astype(F32)


def query_offsets(table, base):
    lane = iota((ROW, LANES), 1)
    inside = (lane >= base) & (lane < base + HEAD)
    in_h = inside & (lane // ROW % 2 == 0)
    rounded = lane // (2 * ROW) % 2 == 0
    outs = []
    for a in range(WIN):
        group = table[a * ROW : (a + 1) * ROW]
        at_h = pltpu.roll(group, (base - 13 + a) % LANES, 1)
        at_w = pltpu.roll(group, (base + ROW - TWICE - 13) % LANES, 1, stride=1, stride_axis=0)
        both = jnp.where(in_h, at_h, at_w)
        high = both.astype(BF16).astype(F32)
        outs.append(jnp.where(rounded, high, both - high))
    return jnp.concatenate(outs, axis=0)


def offset_grads(grad, base):
    lane = iota((ROW, LANES), 1)
    in_h = (lane >= base) & (lane < base + ROW)
    in_w = (lane >= base + ROW) & (lane < base + 2 * ROW)
    outs = []
    for a in range(WIN):
        group = grad[a * ROW : (a + 1) * ROW]
        from_h = pltpu.roll(jnp.where(in_h, group, 0.0), (HEAD + 13 - a) % LANES, 1)
        outs.append(from_h + pltpu.roll(jnp.where(in_w, group, 0.0), 0, 1, stride=1, stride_axis=0))
    return jnp.concatenate(outs, axis=0)


def table_places(start, straight=False):
    row, lane = iota((TABLE, LANES), 0), iota((TABLE, LANES), 1)
    return (lane - start == (row if straight else TABLE - 1 - row)).astype(F32)


def rate_of(keep_ref, branch):
    return jnp.where(keep_ref[0, branch] > 0, 1.0 / 0.9, 0.0).astype(F32)


def pack_kernel(
    keep_ref, qkv_ref, proj_ref, gain1_ref, shift1_ref, projb_ref, gain2_ref, shift2_ref, downb_ref, qvb_ref, grad_ref,
    first_ref, second_ref, params_ref, dm_ref,
):
    for tier, out in enumerate((first_ref, second_ref)):
        for i in range(3):
            out[:, i * HALF : (i + 1) * HALF] = qkv_ref[:, i * D + tier * HALF : i * D + (tier + 1) * HALF]
    second_ref[:, TIER:] = proj_ref[...]
    for i, ref in enumerate((gain1_ref, shift1_ref, projb_ref, gain2_ref, shift2_ref, downb_ref)):
        params_ref[i : i + 1] = ref[...].astype(F32).reshape(1, D)
    params_ref[6:8] = qvb_ref[...].astype(F32)
    dm_ref[...] = (rate_of(keep_ref, 1) * grad_ref[...].astype(F32)).astype(BF16)


def pack(keep, qkv_weight, *args):
    rows = qkv_weight.shape[0]
    return kernel_call(
        "pack",
        pack_kernel,
        11,
        [
            shape_of((rows, TIER), BF16), shape_of((rows, TIER + D), BF16), shape_of((8, D), F32),
            shape_of((AREA, D), BF16),
        ],
        smem=1, far=range(1, 11),
    )(keep, qkv_weight, *args)


def prepare_kernel(
    count, wide, tokens_ref, maps_ref, params_ref, relh_ref, relw_ref, mask_ref, upb_ref,
    a1_ref, turned_ref, att_ref, feed_ref, table_ref, twice_ref, fill_ref, wideb_ref,
):
    wideb_ref[...] = upb_ref[...].astype(F32).reshape(wideb_ref.shape)
    spread = spread_rows()
    x = dot_nn(spread, tokens_ref[...])
    source = iota((D, D), 1)
    att = (rows_from(maps_ref, 0, D // (count * wide), wide) == source).astype(F32).astype(BF16)
    att_ref[...] = att
    feed_ref[...] = (rows_from(maps_ref, 5, D // count, 1, paired=True) == source).astype(F32).astype(BF16)
    unit, _ = norm_parts(x)
    a1 = (unit * params_ref[0:1] + params_ref[1:2]).astype(BF16)
    a1_ref[...] = dot_nt(a1, att).astype(BF16)
    turned_ref[...] = dot_nt(att, a1).astype(BF16)
    one = dot_tn(relh_ref[...], table_places(0).astype(BF16)) + dot_tn(
        relw_ref[...], table_places(W_START, straight=True).astype(BF16)
    )
    blank = jnp.zeros((HEAD, LANES), F32)
    table_ref[:HEAD, :] = jnp.concatenate([one, blank], axis=1).astype(BF16)
    table_ref[HEAD:, :] = jnp.concatenate([blank, pltpu.roll(one, HEAD, 1)], axis=1).astype(BF16)
    twice = sum(
        dot_tn(ref[...], table_places(start + more).astype(BF16))
        for ref, start in ((relh_ref, 0), (relw_ref, TWICE))
        for more in (0, 2 * ROW)
    )
    twice_ref[:HEAD, :] = jnp.concatenate([twice, blank], axis=1).astype(BF16)
    twice_ref[HEAD:, :] = jnp.concatenate([blank, twice], axis=1).astype(BF16)
    seen = dot_nt((mask_ref[...] > 0).astype(F32).astype(BF16), spread)
    key = iota((1, R), 1)
    fill_ref[...] = jnp.where(key % ROW >= WIN, -3e38, jnp.where(seen > 0.5, 0.0, -1e9))


def prepare(tokens, params, rel_h, rel_w, mask, upb):
    count, wide = lax.axis_size("dp"), lax.axis_size("mp")
    return kernel_call(
        "prepare",
        partial(prepare_kernel, count, wide),
        7,
        [
            shape_of((R, D), BF16), shape_of((D, R), BF16), shape_of((D, D), BF16), shape_of((D, D), BF16),
            shape_of((LANES, 2 * LANES), BF16), shape_of((LANES, 2 * LANES), BF16), shape_of((1, R), F32),
            shape_of((1, upb.shape[0]), F32),
        ],
        far=(0, 1, 3, 4, 5, 6),
    )(tokens, row_maps(count, wide), params, rel_h, rel_w, mask, upb)


def act_kernel(dm_ref, down_ref, out_ref, sum_ref):
    sum_ref[...] = jnp.sum(dm_ref[...].astype(F32), axis=0, keepdims=True)
    out_ref[...] = dot_nt(dm_ref[...], down_ref[...])


def act_grad(dm, down):
    return kernel_call("act", act_kernel, 2, [shape_of((AREA, down.shape[0]), F32), shape_of((1, D), F32)])(dm, down)


def heads_forward(qkv_ref, tables, fill, p_ref, out):
    ones = row_masks()
    sums = jnp.ones((R, LANES), BF16)
    left = iota((R, LANES), 1) < HEAD
    for pair in range(PAIRS // 2):
        at = pair * LANES
        q2 = qkv_ref[:, at : at + LANES]
        k2 = qkv_ref[:, HALF + at : HALF + at + LANES].astype(F32)
        v2 = jnp.concatenate([qkv_ref[:, 2 * HALF + at : 2 * HALF + at + LANES], sums], axis=1)
        products = dot_nn(q2, tables)
        q2 = q2.astype(F32) * HEAD**-0.5
        outs = []
        for side in range(2):
            mine = left if side == 0 else ~left
            offsets = query_offsets(products[:, side * LANES : (side + 1) * LANES], HEAD * (1 - side))
            q_aug = jnp.where(mine, q2, offsets).astype(BF16)
            k_aug = jnp.where(mine, k2, ones).astype(BF16)
            scores = dot_nt(q_aug, k_aug)
            scores = jnp.where(fill < 0.0, fill, scores)
            expo = jnp.exp(scores - jnp.max(scores, axis=-1, keepdims=True))
            mixed = dot_nn(expo.astype(BF16), v2)
            scale = 1.0 / mixed[:, LANES:]
            scale = jnp.concatenate([scale, scale[:, : R - LANES]], axis=1)
            p_ref[2 * pair + side] = (expo * scale).astype(BF16)
            outs.append(mixed[:, :LANES] * scale[:, :LANES])
        out(at, jnp.where(left, outs[0], outs[1]).astype(BF16))


def project(a1_ref, own_ref, other_ref, bias, qkv_ref):
    total = dot_nn(a1_ref[:, :HALF], own_ref[:, :TIER]) + dot_nn(a1_ref[:, HALF:], other_ref[:, :TIER])
    qkv_ref[...] = (total + bias).astype(BF16)


def tier_bias(params_ref, tier):
    at = tier * HALF
    return jnp.concatenate(
        [
            params_ref[6:7, at : at + HALF],
            jnp.zeros((1, HALF), F32),
            params_ref[7:8, at : at + HALF],
        ],
        axis=1,
    )


def attend_first_kernel(a1_ref, own_ref, other_ref, params_ref, table_ref, fill_ref, qkv_ref, p_ref, o_ref):
    project(a1_ref, own_ref, other_ref, tier_bias(params_ref, 0), qkv_ref)

    def out(at, value):
        o_ref[:, at : at + LANES] = value

    heads_forward(qkv_ref, table_ref[...], fill_ref[...], p_ref, out)


def attend_first(*args):
    return kernel_call(
        "attend1",
        attend_first_kernel,
        6,
        [shape_of((R, TIER), BF16), shape_of((HEADS // 2, R, R), BF16), shape_of((R, HALF), BF16)],
    )(*args)


def attend_second_kernel(
    keep_ref, a1_ref, own_ref, other_ref, params_ref, table_ref, fill_ref, first_ref, x_ref, att_ref,
    qkv_ref, p_ref, turned_ref, mid_ref, a2_ref,
    o_ref,
):
    project(a1_ref, own_ref, other_ref, tier_bias(params_ref, 1), qkv_ref)
    o_ref[:, :HALF] = first_ref[...]

    def out(at, value):
        o_ref[:, HALF + at : HALF + at + LANES] = value

    heads_forward(qkv_ref, table_ref[...], fill_ref[...], p_ref, out)
    rows = dot_tn(spread_rows(), o_ref[...]).astype(BF16)
    moved = dot_nt(rows, att_ref[...]).astype(BF16)
    branch = dot_nn(moved[:, :HALF], own_ref[:, TIER:]) + dot_nn(moved[:, HALF:], other_ref[:, TIER:])
    turned_ref[...] = dot_nt(att_ref[...], rows).astype(BF16)
    rate = rate_of(keep_ref, 0)
    middle = x_ref[...].astype(F32) + rate * (branch + params_ref[2:3])
    mid_ref[...] = middle
    unit, _ = norm_parts(middle)
    a2_ref[...] = (unit * params_ref[3:4] + params_ref[4:5]).astype(BF16)


def attend_second(*args):
    return kernel_call(
        "attend2",
        attend_second_kernel,
        10,
        [
            shape_of((R, TIER), BF16), shape_of((HEADS // 2, R, R), BF16), shape_of((D, AREA), BF16),
            shape_of((AREA, D), F32), shape_of((AREA, D), BF16),
        ],
        smem=1, scratch=[pltpu.VMEM((R, D), BF16)],
    )(*args)


def feed_kernel(a2_ref, up_ref, upb_ref, gact_ref, g_ref, dh_ref, da2_ref):
    total = None
    for at in range(0, up_ref.shape[1], STEP):
        here = slice(at, at + STEP)
        hidden = dot_nn(a2_ref[...], up_ref[:, here]) + upb_ref[:, here]
        phi = 0.5 + 0.5 * lax.erf(hidden * 0.5**0.5)
        g_ref[:, here] = (hidden * phi).astype(BF16)
        slope = phi + hidden * (jnp.exp(-0.5 * hidden * hidden) * 0.3989422804014327)
        dh = (gact_ref[:, here] * slope).astype(BF16)
        dh_ref[:, here] = dh
        part = dot_nt(dh, up_ref[:, here])
        total = part if total is None else total + part
    da2_ref[...] = total.astype(da2_ref.dtype)


def feed(a2, up, upb, gact, kind):
    hidden = up.shape[1]
    return kernel_call(
        "feed",
        feed_kernel,
        4,
        [shape_of((AREA, hidden), BF16), shape_of((AREA, hidden), BF16), shape_of((AREA, D), kind)],
    )(a2, up, upb, gact)


def feed_weights_kernel(count, map_ref, down_ref, *refs):
    dms, acts, a2s, dhs = (refs[i * count : (i + 1) * count] for i in range(4))
    refs = refs[4 * count :]
    depth = lax.axis_size("dp") // 4
    rows = HALF // (2 * depth)
    for lefts, rights, by_z in ((dms, acts, Z_FIRST[0]), (a2s, dhs, Z_FIRST[1])):
        blocks = depth if by_z else 2
        outs, refs = refs[: 2 * blocks], refs[2 * blocks :]
        turned = [dot_nt(map_ref[...], left[...]).astype(BF16) for left in lefts]
        for at in range(0, rights[0].shape[1], STEP):
            here = slice(at, at + STEP)
            total = dot_nn(turned[0], rights[0][:, here])
            for j in range(1, count):
                total = total + dot_nn(turned[j], rights[j][:, here])
            total = total.astype(BF16)
            for s in range(2):
                for y in range(2):
                    if not by_z:
                        start = s * HALF + y * HALF // 2
                        outs[2 * s + y][:, here] = total[start : start + HALF // 2]
                        continue
                    for z in range(depth):
                        start = s * HALF + (y * depth + z) * rows
                        outs[depth * s + z][y * rows : (y + 1) * rows, here] = total[start : start + rows]
    sum_ref, *outs = refs
    for j in range(count):
        outs[j][...] = dot_nn(acts[j][...], down_ref[...]).astype(outs[j].dtype)
    sums = jnp.sum(dhs[0][...].astype(F32), axis=0, keepdims=True)
    for j in range(1, count):
        sums = sums + jnp.sum(dhs[j][...].astype(F32), axis=0, keepdims=True)
    sum_ref[...] = sums


def feed_weights(row_map, down, dms, acts, a2s, dhs):
    count = len(dms)
    columns = acts[0].shape[1]
    blocks = [lax.axis_size("dp") // 4 if by_z else 2 for by_z in Z_FIRST]
    made = kernel_call(
        "feedw",
        partial(feed_weights_kernel, count),
        2 + 4 * count,
        [shape_of((HALF // n, columns), BF16) for n in blocks for _ in range(2 * n)]
        + [shape_of((1, columns), F32)]
        + [shape_of((AREA, D), F32 if j == 0 else BF16) for j in range(count)],
    )(row_map, down, *dms, *acts, *a2s, *dhs)
    grads = []
    for n in blocks:
        grads += [made[:n], made[n : 2 * n]]
        made = made[2 * n :]
    return *grads, *made


def heads_back(qkv_ref, p_ref, do_at, tables, dqkv_ref):
    ones = row_masks(down=True)
    left = iota((R, LANES), 1) < HEAD
    table_grad = jnp.zeros((LANES, 2 * LANES), F32)
    for pair in range(PAIRS // 2):
        at = pair * LANES
        q2 = qkv_ref[:, at : at + LANES]
        q_wide = q2.astype(F32)
        k2 = qkv_ref[:, HALF + at : HALF + at + LANES].astype(F32)
        v2 = qkv_ref[:, 2 * HALF + at : 2 * HALF + at + LANES]
        do2 = do_at(at).astype(F32)
        dq2 = dk2 = dv2 = None
        offsets = []
        for side in range(2):
            mine = left if side == 0 else ~left
            probs = p_ref[2 * pair + side]
            do_mine = jnp.where(mine, do2, 0.0).astype(BF16)
            dv = dot_tn(probs, do_mine)
            dp = dot_nt(do_mine, v2)
            wide = probs.astype(F32)
            ds = (wide * (dp - jnp.sum(wide * dp, axis=-1, keepdims=True))).astype(BF16)
            k_aug = jnp.where(mine, k2, ones).astype(BF16)
            dq_aug = dot_nn(ds, k_aug)
            offsets.append(offset_grads(dq_aug, HEAD * (1 - side)))
            dk = dot_tn(ds, jnp.where(mine, q_wide, 0.0).astype(BF16))
            if side == 0:
                dq2, dk2, dv2 = dq_aug, dk, dv
            else:
                dq2, dk2, dv2 = jnp.where(mine, dq_aug, dq2), dk2 + dk, dv2 + dv
        spread = jnp.concatenate(offsets, axis=1).astype(BF16)
        dq2 = dq2 * HEAD**-0.5 + dot_nt(spread, tables)
        table_grad = table_grad + dot_tn(q2, spread)
        dqkv_ref[:, at : at + LANES] = dq2.astype(BF16)
        dqkv_ref[:, HALF + at : HALF + at + LANES] = (dk2 * HEAD**-0.5).astype(BF16)
        dqkv_ref[:, 2 * HALF + at : 2 * HALF + at + LANES] = dv2.astype(BF16)
    return table_grad[:HEAD, :LANES] + pltpu.roll(table_grad[HEAD:, LANES:], HEAD, 1)


def back_norm_kernel(
    keep_ref, da2_ref, got_ref, mid_ref, g_ref, params_ref, own_ref, other_ref, att_ref,
    dmid_ref, do_ref, dy_ref, sums_ref,
):
    da2 = da2_ref[...] + got_ref[...].astype(F32)
    unit, factor = norm_parts(mid_ref[...])
    dmid = g_ref[...].astype(F32) + norm_back(da2, unit, factor, params_ref[3:4])
    dmid_ref[...] = dmid
    dy = (rate_of(keep_ref, 0) * dmid).astype(BF16)
    dy_ref[...] = dy
    moved = jnp.concatenate(
        [dot_nt(dy, own_ref[:, TIER:]).astype(BF16), dot_nt(dy, other_ref[:, TIER:]).astype(BF16)], axis=1
    )
    rows = dot_nn(moved, att_ref[...]).astype(BF16)
    do_ref[...] = dot_nn(spread_rows(), rows).astype(BF16)
    sums_ref[0:1] = jnp.sum(dy.astype(F32), axis=0, keepdims=True)
    sums_ref[1:2] = jnp.sum(da2 * unit, axis=0, keepdims=True)
    sums_ref[2:3] = jnp.sum(da2, axis=0, keepdims=True)


def back_norm(*args):
    return kernel_call(
        "backnorm",
        back_norm_kernel,
        9,
        [shape_of((AREA, D), F32), shape_of((R, D), BF16), shape_of((AREA, D), BF16), shape_of((3, D), F32)],
        smem=1,
    )(*args)


def back_kernel(tier, do_ref, turned_ref, qkv_ref, p_ref, table_ref, *refs):
    if tier == 0:
        o_ref, dy_ref, *refs = refs
    dqkv_ref, *refs, sums_ref, tab_ref = refs
    tab_ref[...] = heads_back(
        qkv_ref, p_ref, lambda at: do_ref[:, tier * HALF + at : tier * HALF + at + LANES], table_ref[...], dqkv_ref
    )
    wide = lax.axis_size("mp")
    blocks = (wide, 2)[tier]
    rows = HALF // (2 * wide)
    for s in range(2):
        part = dot_nn(turned_ref[s * HALF : (s + 1) * HALF], dqkv_ref[...]).astype(BF16)
        outs = refs[s * blocks : (s + 1) * blocks]
        if tier == 0:
            more = dot_nn(o_ref[s * HALF : (s + 1) * HALF], dy_ref[...]).astype(BF16)
        for x in range(wide):
            if tier == 0:
                outs[x][:, :TIER] = part[2 * x * rows : 2 * (x + 1) * rows]
                outs[x][:, TIER:] = more[2 * x * rows : 2 * (x + 1) * rows]
                continue
            for y in range(2):
                at_row = (x * 2 + y) * rows
                outs[y][x * rows : (x + 1) * rows] = part[at_row : at_row + rows]
    sums_ref[:, :HALF] = jnp.sum(dqkv_ref[:, :HALF].astype(F32), axis=0, keepdims=True)
    sums_ref[:, HALF:] = jnp.sum(dqkv_ref[:, 2 * HALF :].astype(F32), axis=0, keepdims=True)


def back(tier, *args):
    blocks = (lax.axis_size("mp"), 2)[tier]
    dqkv, *grads, sums, table = kernel_call(
        f"back{tier + 1}",
        partial(back_kernel, tier),
        len(args),
        [shape_of((R, TIER), BF16)]
        + [shape_of((HALF // blocks, TIER + D * (tier == 0)), BF16)] * (2 * blocks)
        + [shape_of((1, D), F32), shape_of((HEAD, LANES), F32)],
    )(*args)
    return dqkv, grads[:blocks], grads[blocks:], sums, table


def finish_kernel(
    wide, keep_ref, dq1_ref, dq2_ref, own1_ref, other1_ref, own2_ref, other2_ref, att_ref, x_ref, dmid_ref,
    params_ref, mid_ref, m_ref, mgot_ref, downb_ref, upb_ref, sums0_ref, sums1_ref, sums2_ref, tab1_ref, tab2_ref,
    dx_ref, result_ref, small_ref,
):
    spread = spread_rows()
    dq1, dq2 = dot_tn(spread, dq1_ref[...]).astype(BF16), dot_tn(spread, dq2_ref[...]).astype(BF16)
    halves = []
    for first, second in ((own1_ref, own2_ref), (other1_ref, other2_ref)):
        halves.append(dot_nt(dq1, first[...]) + dot_nt(dq2, second[:, :TIER]))
    moved = jnp.concatenate(halves, axis=1)
    high = moved.astype(BF16)
    low = (moved - high.astype(F32)).astype(BF16)
    da1 = dot_nn(high, att_ref[...]) + dot_nn(low, att_ref[...])
    unit, factor = norm_parts(x_ref[...].astype(F32))
    dx_ref[...] = (dmid_ref[...] + norm_back(da1, unit, factor, params_ref[0:1])).astype(BF16)
    rate = rate_of(keep_ref, 1)
    total = m_ref[...] + mgot_ref[...].astype(F32) + params_ref[5:6]
    result_ref[...] = (mid_ref[...] + rate * total).astype(BF16)

    small_ref[...] = jnp.zeros(small_ref.shape, F32)

    def put(name, value):
        for i in range(D // LANES):
            small_ref[piece(SMALL[name] + i)] = value[:, i * LANES : (i + 1) * LANES]

    put("gain1", jnp.sum(da1 * unit, axis=0, keepdims=True))
    put("shift1", jnp.sum(da1, axis=0, keepdims=True))
    put("projb", sums0_ref[0:1])
    put("gain2", sums0_ref[1:2])
    put("shift2", sums0_ref[2:3])
    put("qbias", jnp.concatenate([sums1_ref[:, :HALF], sums2_ref[:, :HALF]], axis=1))
    put("vbias", jnp.concatenate([sums1_ref[:, HALF:], sums2_ref[:, HALF:]], axis=1))
    put("downb", downb_ref[...])
    table = tab1_ref[...] + tab2_ref[...]
    low, high = table[: HEAD // 2], table[HEAD // 2 :]
    lane = iota(low.shape, 1)
    packed = jnp.where(
        lane < 32,
        low,
        jnp.where(
            lane < 64,
            pltpu.roll(low, (32 - W_START) % LANES, 1),
            jnp.where(lane < 96, pltpu.roll(high, 64, 1), pltpu.roll(high, (96 - W_START) % LANES, 1)),
        ),
    )
    for i in range(HEAD // 2):
        small_ref[piece(SMALL_TABLE + i)] = packed[i : i + 1]
    count = lax.axis_size("dp")
    size = upb_ref.shape[1] // count
    for m in range(wide):
        for i in range(count):
            rows, lanes = piece(SMALL_UP + m * count + i)
            value = upb_ref[:, i * size : (i + 1) * size]
            lanes = slice(lanes.start, lanes.start + size)
            small_ref[rows, lanes] = jnp.where(lax.axis_index("mp") == m, value, 0.0)


def finish(wide, rows, *args):
    return kernel_call(
        "finish",
        partial(finish_kernel, wide),
        21,
        [shape_of((AREA, D), BF16), shape_of((AREA, D), BF16), shape_of((rows, TIER), F32)],
        smem=1, out_far=(0, 1),
    )(*args)


def outputs_kernel(
    n_parts, rows, *refs
):
    parts, refs = refs[:n_parts], refs[n_parts:]
    gain1_ref, shift1_ref, qv_ref, relh_ref, relw_ref, projb_ref, gain2_ref, shift2_ref, upb_ref, downb_ref = refs[:10]
    table_ref, up_ref = refs[10:]
    total = parts[0][...]
    for part in parts[1:]:
        total = total + part[part.shape[0] - rows :].astype(F32)
    flat = {
        "gain1": gain1_ref, "shift1": shift1_ref, "projb": projb_ref, "gain2": gain2_ref, "shift2": shift2_ref,
        "downb": downb_ref,
    }

    def at(place):
        here, lanes = piece(place)
        return total[here, lanes]

    for i in range(D // LANES):
        here = slice(i * LANES, (i + 1) * LANES)
        for name, ref in flat.items():
            ref[here] = at(SMALL[name] + i)[0]
        qv_ref[0:1, here] = at(SMALL["qbias"] + i)
        qv_ref[1:2, here] = at(SMALL["vbias"] + i)
    for i in range(HEAD // 2):
        table_ref[i : i + 1] = at(SMALL_TABLE + i)
    for start, ref in ((0, relh_ref), (32, relw_ref)):
        for half in range(2):
            ref[:, half * 32 : half * 32 + 32] = lax.dot_general(
                table_places(start + 64 * half, straight=start > 0), table_ref[...], (((1,), (1,)), ((), ())),
                precision=lax.Precision.HIGHEST, preferred_element_type=F32,
            )
    for i in range(up_ref.shape[0]):
        up_ref[i : i + 1] = at(SMALL_UP + i)
    place = lax.axis_index("mp") * lax.axis_size("dp") + lax.axis_index("dp")
    upb_ref[...] = up_ref[place, : upb_ref.shape[0]]


def outputs(parts, size, ups):
    row = shape_of((D,), F32)
    table = shape_of((TABLE, HEAD), F32)
    return kernel_call(
        "outputs",
        partial(outputs_kernel, len(parts), parts[0].shape[0]),
        len(parts),
        [row, row, shape_of((2, D), F32), table, table, row, row, row, shape_of((size,), F32), row],
        scratch=[pltpu.VMEM((HEAD // 2, LANES), F32), pltpu.VMEM((ups, LANES), F32)],
        out_far=range(10),
    )(*parts)


def per_device(
    tokens, ln1_gain, ln1_bias, qkv_weight, qv_bias, rel_pos_h, rel_pos_w, proj_weight, proj_bias,
    ln2_gain, ln2_bias, fc1_weight, fc1_bias, fc2_weight, fc2_bias, keep_mask, key_mask, out_grad,
):
    wide = lax.axis_size("mp")
    hidden = fc1_weight.shape[1]
    first, second, params, dm = pack(
        keep_mask, qkv_weight, proj_weight, ln1_gain, ln1_bias, proj_bias, ln2_gain, ln2_bias, fc2_bias, qv_bias, out_grad
    )
    made, chains = {}, {}

    def gated(value, task, kind):
        others = [made[name] for name in GATES.get(f"{task}:{kind}", ())]
        return after(value, *others) if others else value

    def front(name):
        if name == "dm":
            sent = gated(dm, name, "s")
            return gated([move_x(sent, -s) for s in range(1, wide)], name, "r")
        if name == "prep":
            return prepare(gated(tokens, name, "s"), params, rel_pos_h, rel_pos_w, key_mask, fc1_bias)
        if name == "act0":
            return act_grad(gated(dm, name, "s"), fc2_weight)
        if name == "act1":
            return [act_grad(v, fc2_weight) for v in gated(made["dm"], name, "s")]
        if name == "attend1":
            a1, _, _, _, _, twice, fill, _ = made["prep"]
            return attend_first(gated(a1, name, "s"), chains["1"], made["c1"], params, twice, fill)
        step, tier = name
        if step == "z":
            sent = gated((first, second)[int(tier) - 1], name, "s")
            chains[tier] = gated(gather_z(sent), name, "r")
            return chains[tier]
        if step == "n":
            return gated(gather_near(gated(chains[tier], name, "s")), name, "r")
        if step == "f":
            made["n" + tier] = gated(made["n" + tier], name, "s")
            return gated(gather_far(made["n" + tier]), name, "r")
        chains[tier] = gated(gather_join(chains[tier], made["n" + tier], made["f" + tier]), name, "s")
        return gated(move_c(chains[tier]), name, "r")

    for name in FRONT:
        made[name] = front(name)
    a1, a1_turned, att_map, feed_map, tables, twice, fill, upb = made["prep"]
    dms = [dm, *made["dm"]]
    acts = [made["act0"], *made["act1"]]
    gacts, downb = [v[0] for v in acts], acts[0][1]
    own1, other1, own2, other2 = chains["1"], made["c1"], chains["2"], made["c2"]
    qkv1, probs1, att1 = made["attend1"]
    qkv2, probs2, att_turned, middle, a2 = attend_second(
        keep_mask, a1, own2, other2, params, twice, fill, att1, tokens, att_map
    )

    a2s = [a2] + [move_x(a2, -s) for s in range(1, wide)]
    fed = [feed(a2, fc1_weight, upb, gacts[0], F32)]
    for j in range(1, wide):
        fed.append(feed(after(a2s[j], fed[-1][2]), fc1_weight, upb, gacts[j], BF16))
    da2 = fed[0][2]
    got = [move_x(fed[s][2], s) for s in range(1, wide)]
    down_keep, down_send, up_keep, up_send, upb_sum, *outs = feed_weights(
        after(feed_map, fed[-1][2]), fc2_weight, dms, [f[0] for f in fed], a2s, [f[1] for f in fed]
    )
    got, down_send, up_send, outs = lax.optimization_barrier((got, down_send, up_send, outs))
    got = got[0] if wide == 2 else add_up(*got)
    depth = lax.axis_size("dp") // 4
    moves = {"x": (move_x, wide), "y": (turn_y, 2), "z": (move_z, depth)}
    small_rows = -(-(SMALL_UP + wide * lax.axis_size("dp")) // PIECES)
    small_rows += -small_rows % 16

    def cores(name, keep, send, axes):
        sent = gated(send, f"{name}c", "s")
        got = gated([move_c(v) for v in sent], f"{name}c", "r")
        chains[name] = (list(zip(keep, got)), axes)
        return got

    def count_of(axis):
        return depth if axis in "z0" else depth >> int(axis) if axis.isdigit() else moves[axis][1]

    def along(name, axis):
        sums, axes = chains[name]
        carries = ROUTE.get(axis) == name
        if axis.isdigit():
            mask = 1 << int(axis)
            sent = [jnp.concatenate([add_up(*v).astype(BF16) for v in sums[1::2]])]
            sent = gated(sent, f"{name}{axis}", "s")
            got = gated([swap_z(v, mask) for v in sent], f"{name}{axis}", "r")
            size = sums[0][0].shape[0]
            sums = [[*v, got[0][i * size : (i + 1) * size]] for i, v in enumerate(sums[::2])]
            axes = axes[axes.index(axis) + 1 :]
            if axes and axes[0].isdigit():
                chains[name] = (sums, axes)
            else:
                chains[name] = (split(sums[0], count_of(axes[0])), axes) if axes else (sums[0], axes)
            return got
        if axis == "z" and name in "du":
            move = swap_z
        else:
            move, _ = moves[axis]
        sent = [add_up(*v).astype(BF16) for v in sums[1:]]
        if carries:
            extra = chains["s"].astype(BF16)
            sent = [jnp.concatenate([v, extra]) for v in sent]
        sent = gated(sent, f"{name}{axis}", "s")
        got = gated([move(v, s + 1) for s, v in enumerate(sent)], f"{name}{axis}", "r")
        rest = [*sums[0], *got]
        if carries:
            rows = sums[0][0].shape[0]
            rest = [*sums[0], *[v[:rows] for v in got]]
            if axis == "z":
                chains["s"] = [chains["s"], *got]
            else:
                chains["s"] = add_up(chains["s"], *[v[rows:] for v in got])
        axes = axes[axes.index(axis) + 1 :]
        chains[name] = (split(rest, count_of(axes[0])), axes) if axes else (rest, axes)
        return got

    def small_cores():
        flat = gated(made["finish"][2], "sc", "s")
        got = gated(move_c(flat), "sc", "r")
        chains["s"] = flat + got
        return got

    def task(name):
        if name == "norm":
            return back_norm(keep_mask, da2, got, middle, out_grad, params, own2, other2, att_map)
        if name in ("back1", "back2"):
            tier = int(name[-1]) - 1
            do = gated(made["norm"][1], name, "s")
            more = (att_turned, made["norm"][2]) if tier == 0 else ()
            return back(tier, do, a1_turned, (qkv1, qkv2)[tier], (probs1, probs2)[tier], tables, *more)
        if name == "m":
            moved = [move_x(v, s + 1) for s, v in enumerate(gated(outs[1:], "m", "s"))]
            moved = gated(moved, "m", "r")
            return moved[0] if wide == 2 else add_up(*moved)
        if name == "finish":
            first, second = made["back1"], made["back2"]
            mid = gated(middle, "finish", "s")
            return finish(
                wide, small_rows, keep_mask, first[0], second[0], own1, other1, own2, other2, att_map, tokens,
                made["norm"][0], params, mid, outs[0], made["m"], downb, upb_sum, made["norm"][3], first[3], second[3],
                first[4], second[4],
            )
        chain, axis = name
        if chain == "s":
            return small_cores()
        if axis != "c":
            return along(chain, axis)
        if chain in "du":
            keep, send = (down_keep, down_send) if chain == "d" else (up_keep, up_send)
            bits = "".join(str(i) for i in range(depth.bit_length() - 1)) if TREE["du".index(chain)] else "z"
            return cores(chain, keep, send, bits + "y" if Z_FIRST["du".index(chain)] else "y" + bits)
        tier = "ab".index(chain)
        return cores(chain, made[f"back{tier + 1}"][1], made[f"back{tier + 1}"][2], ("xyz", "yxz")[tier])

    for name in ORDER:
        made[name] = task(name)
        while name[-1] == "1" and name[0] in "du" and chains[name[0]][1][:1].isdigit():
            along(name[0], chains[name[0]][1][0])
    grad_in, result, _ = made["finish"]
    small = chains["s"]
    down_grad, up_grad, rows1, rows2 = (add_up(*chains[name][0]) for name in "duab")
    proj_grad = rows1[:, TIER:]

    pieces = [
        piece
        for i in range(3)
        for piece in (rows1[:, i * HALF : (i + 1) * HALF], rows2[:, i * HALF : (i + 1) * HALF])
    ]
    qkv_grad = jnp.concatenate(pieces, axis=1)

    gain1, shift1, qv_grad, relh_grad, relw_grad, projb, gain2, shift2, up_bias_grad, downb = outputs(
        small, hidden // lax.axis_size("dp"), wide * lax.axis_size("dp")
    )
    return (
        result, grad_in, gain1, shift1, qkv_grad, qv_grad, relh_grad, relw_grad, proj_grad, projb, gain2, shift2,
        up_grad, up_bias_grad, down_grad.T, downb,
    )


def solution(mesh):
    in_specs = (
        P(("dp", "mp"), None),
        P(),
        P(),
        P(("dp", "mp"), None),
        P(),
        P(),
        P(),
        P(("dp", "mp"), None),
        P(),
        P(),
        P(),
        P(None, "mp"),
        P("mp"),
        P("mp", None),
        P(),
        P(("dp", "mp"), None),
        P(("dp", "mp"), None),
        P(("dp", "mp"), None),
    )
    out_specs = (
        P(("dp", "mp"), None),
        P(("dp", "mp"), None),
        P(),
        P(),
        P(("dp", "mp"), None),
        P(),
        P(),
        P(),
        P(("dp", "mp"), None),
        P(),
        P(),
        P(),
        P("dp", "mp"),
        P(("mp", "dp")),
        P("mp", "dp"),
        P(),
    )
    return jax.shard_map(
        per_device, mesh=mesh, in_specs=in_specs, out_specs=out_specs, check_vma=False
    )
```

```python
from functools import partial

import jax
import jax.numpy as jnp
import numpy as np
from jax import lax
from jax.experimental import pallas as pl
from jax.experimental.pallas import tpu as pltpu
from jax.sharding import PartitionSpec as P

D = 768
HEADS = 12
HEAD = 64
WIN = 14
AREA = WIN * WIN
ROW = 16
R = WIN * ROW
PAIRS = HEADS // 2
LANES = 128
TABLE = 2 * WIN - 1
TWICE = 59
W_START = HEAD + ROW + 2
HALF = D // 2
STEP = 384
TIER = 3 * HALF
F32 = jnp.float32
BF16 = jnp.bfloat16
VMEM = pl.BlockSpec(memory_space=pltpu.VMEM)
SMEM = pl.BlockSpec(memory_space=pltpu.SMEM)
LIMIT = 20 * 2**20
Z_FIRST = (False, False)
TREE = (True, True)
FRONT = ('dm', 'z1', 'prep', 'act1', 'z2', 'n1', 'n2', 'act0', 'f2', 'f1', 'c1', 'attend1', 'c2')
ORDER = ('dc', 'dy', 'm', 'norm', 'back2', 'bc', 'back1', 'finish', 'ac', 'sc', 'by', 'bx', 'ax', 'd0', 'd1', 'bz', 'uc', 'uy', 'ay', 'u0', 'u1', 'az')
GATES = {'n1:s': ['prep', 'dm'], 'n2:s': ['z2'], 'f1:s': ['n1'], 'act1:s': ['dm'], 'attend1:s': ['dm', 'f1'], 'z1:s': ['dm'], 'back1:s': ['dc'], 'back2:s': ['m', 'dc'], 'finish:s': ['bc'], 'ay:r': ['ac', 'back1', 'd1'], 'uc:s': ['dc'], 'bc:s': ['dy'], 'bx:r': ['dy'], 'bz:r': ['bc'], 'd0:s': ['finish'], 'd1:r': ['dy'], 'az:r': ['bz'], 'u1:r': ['by', 'bx'], 'uc:r': ['back2'], 'sc:r': ['ac'], 'ax:r': ['sc'], 'az:s': ['ay']}
ROUTE = {"y": "b", "x": "b", "z": "b"}
CHEAP = pl.CostEstimate(flops=1, bytes_accessed=1, transcendentals=0)
SMALL = {"gain1": 0, "shift1": 6, "qbias": 12, "vbias": 18, "projb": 24, "gain2": 30, "shift2": 36, "downb": 42}
SMALL_TABLE = 48
SMALL_UP = SMALL_TABLE + HEAD // 2
PIECES = TIER // LANES


def piece(place):
    return slice(place // PIECES, place // PIECES + 1), slice(place % PIECES * LANES, (place % PIECES + 1) * LANES)


def shape_of(shape, kind):
    return jax.ShapeDtypeStruct(shape, kind)


def kernel_call(name, body, n_in, outs, *, smem=0, scratch=(), far=(), out_far=()):
    call = pl.pallas_call(
        body,
        name=name,
        in_specs=[SMEM] * smem + [VMEM] * (n_in - smem),
        out_specs=[VMEM] * len(outs),
        out_shape=[o if i in out_far else pltpu.VMEM(o.shape, o.dtype) for i, o in enumerate(outs)],
        scratch_shapes=list(scratch),
        compiler_params=pltpu.CompilerParams(vmem_limit_bytes=LIMIT),
        cost_estimate=CHEAP,
    )

    def run(*args):
        spaces = [pltpu.HBM if i in far else pltpu.VMEM for i in range(smem, n_in)]
        return call(*args[:smem], *map(pltpu.with_memory_space_constraint, args[smem:], spaces))

    return run


def after(value, *others):
    return lax.optimization_barrier((value,) + others)[0]


def dp_pairs(count, dz=0, dy=0, dc=0):
    depth = count // 4
    pairs = []
    for place in range(count):
        z, y, c = place // 4, place // 2 % 2, place % 2
        pairs.append((place, (z + dz) % depth * 4 + (y + dy) % 2 * 2 + (c + dc) % 2))
    return pairs


def move_z(value, step):
    return lax.ppermute(value, "dp", dp_pairs(lax.axis_size("dp"), dz=step))


def swap_z(value, mask):
    pairs = [(place, place ^ (mask * 4)) for place in range(lax.axis_size("dp"))]
    return lax.ppermute(value, "dp", pairs)


def move_y(value):
    return lax.ppermute(value, "dp", dp_pairs(lax.axis_size("dp"), dy=1))


def move_c(value):
    return lax.ppermute(value, "dp", dp_pairs(lax.axis_size("dp"), dc=1))


def move_x(value, step=1):
    count = lax.axis_size("mp")
    return lax.ppermute(value, "mp", [(i, (i + step) % count) for i in range(count)])


def places():
    dp = lax.axis_index("dp")
    return dp // 4, dp // 2 % 2, dp % 2, lax.axis_index("mp")


def row_maps(count, wide):
    depth = count // 4
    place = np.arange(D)
    rows = D // (count * wide)
    block = place // rows
    att = [block % depth, block // depth % 2, block // (2 * depth) % wide, block // (2 * depth * wide), place % rows]
    rows = D // count
    block = place // rows
    feed = [block % depth, block // depth % 2, 0 * block, block // (2 * depth), place % rows]
    return np.stack(att + feed, axis=1).astype(np.int32)


def rows_from(maps_ref, start, rows, wide, paired=False):
    depth = lax.axis_size("dp") // 4
    dp = lax.axis_index("dp")

    def turned(i, here, size):
        there = maps_ref[:, start + i : start + i + 1] + here
        return jnp.where(there >= size, there - size, there)

    across = maps_ref[:, start : start + 1] ^ (dp // 4) if paired else turned(0, dp // 4, depth)
    block = (across * 2 + turned(1, dp // 2 % 2, 2)) * 2 + turned(3, dp % 2, 2)
    if wide > 1:
        block = block * wide + turned(2, lax.axis_index("mp"), wide)
    return block * rows + maps_ref[:, start + 4 : start + 5]


def gather_z(part):
    depth = lax.axis_size("dp") // 4
    return jnp.concatenate([part] + [move_z(part, -s) for s in range(1, depth)])


def gather_near(line):
    wide = lax.axis_size("mp")
    return [move_x(line, -s) for s in range(1, wide)], move_y(line)


def gather_far(near):
    along_x, along_y = near
    half = along_y.shape[1] // 2
    left = [move_y(b[:, :half]) for b in along_x]
    right = [move_x(along_y[:, half:], -s) for s in range(1, lax.axis_size("mp"))]
    return left, right


def gather_join(line, near, far):
    blocks = [line, near[1]]
    for along_x, first, second in zip(near[0], *far):
        blocks += [along_x, jnp.concatenate([first, second], axis=1)]
    return jnp.concatenate(blocks)


def add_up(first, *others):
    total = first.astype(F32)
    for other in others:
        total = total + other.astype(F32)
    return total


def blocks_of(rows, count):
    size = rows.shape[0] // count
    return [rows[i * size : (i + 1) * size] for i in range(count)]


def split(parts, count):
    return list(zip(*[blocks_of(v, count) for v in parts]))


def turn_y(value, step):
    return move_y(value)


def dot_nn(a, b):
    return lax.dot_general(a, b, (((1,), (0,)), ((), ())), preferred_element_type=F32)


def dot_nt(a, b):
    return lax.dot_general(a, b, (((1,), (1,)), ((), ())), preferred_element_type=F32)


def dot_tn(a, b):
    return lax.dot_general(a, b, (((0,), (0,)), ((), ())), preferred_element_type=F32)


def iota(shape, axis):
    return lax.broadcasted_iota(jnp.int32, shape, axis)


def norm_parts(rows_in):
    center = rows_in - jnp.mean(rows_in, axis=-1, keepdims=True)
    factor = lax.rsqrt(jnp.mean(center * center, axis=-1, keepdims=True) + 1e-06)
    return center * factor, factor


def norm_back(grad, unit, factor, gain):
    inner = grad * gain
    return factor * (
        inner
        - jnp.mean(inner, axis=-1, keepdims=True)
        - unit * jnp.mean(inner * unit, axis=-1, keepdims=True)
    )


def spread_rows():
    row, patch = iota((R, AREA), 0), iota((R, AREA), 1)
    return ((row % ROW < WIN) & (patch == row // ROW * WIN + row % ROW)).astype(F32).astype(BF16)


def row_masks(down=False):
    lane = iota((R, LANES), 1) % HEAD
    key = iota((R, LANES), 0)
    column = ROW - 1 - key % ROW if down else key % ROW
    here = jnp.where(lane // ROW % 2 == 0, key // ROW, column)
    return (lane % ROW == here).astype(F32)


def query_offsets(table, base):
    lane = iota((ROW, LANES), 1)
    inside = (lane >= base) & (lane < base + HEAD)
    in_h = inside & (lane // ROW % 2 == 0)
    rounded = lane // (2 * ROW) % 2 == 0
    outs = []
    for a in range(WIN):
        group = table[a * ROW : (a + 1) * ROW]
        at_h = pltpu.roll(group, (base - 13 + a) % LANES, 1)
        at_w = pltpu.roll(group, (base + ROW - TWICE - 13) % LANES, 1, stride=1, stride_axis=0)
        both = jnp.where(in_h, at_h, at_w)
        high = both.astype(BF16).astype(F32)
        outs.append(jnp.where(rounded, high, both - high))
    return jnp.concatenate(outs, axis=0)


def offset_grads(grad, base):
    lane = iota((ROW, LANES), 1)
    in_h = (lane >= base) & (lane < base + ROW)
    in_w = (lane >= base + ROW) & (lane < base + 2 * ROW)
    outs = []
    for a in range(WIN):
        group = grad[a * ROW : (a + 1) * ROW]
        from_h = pltpu.roll(jnp.where(in_h, group, 0.0), (HEAD + 13 - a) % LANES, 1)
        outs.append(from_h + pltpu.roll(jnp.where(in_w, group, 0.0), 0, 1, stride=1, stride_axis=0))
    return jnp.concatenate(outs, axis=0)


def table_places(start, straight=False):
    row, lane = iota((TABLE, LANES), 0), iota((TABLE, LANES), 1)
    return (lane - start == (row if straight else TABLE - 1 - row)).astype(F32)


def rate_of(keep_ref, branch):
    return jnp.where(keep_ref[0, branch] > 0, 1.0 / 0.9, 0.0).astype(F32)


def pack_kernel(
    keep_ref, qkv_ref, proj_ref, gain1_ref, shift1_ref, projb_ref, gain2_ref, shift2_ref, downb_ref, qvb_ref, grad_ref,
    first_ref, second_ref, params_ref, dm_ref,
):
    for tier, out in enumerate((first_ref, second_ref)):
        for i in range(3):
            out[:, i * HALF : (i + 1) * HALF] = qkv_ref[:, i * D + tier * HALF : i * D + (tier + 1) * HALF]
    second_ref[:, TIER:] = proj_ref[...]
    for i, ref in enumerate((gain1_ref, shift1_ref, projb_ref, gain2_ref, shift2_ref, downb_ref)):
        params_ref[i : i + 1] = ref[...].astype(F32).reshape(1, D)
    params_ref[6:8] = qvb_ref[...].astype(F32)
    dm_ref[...] = (rate_of(keep_ref, 1) * grad_ref[...].astype(F32)).astype(BF16)


def pack(keep, qkv_weight, *args):
    rows = qkv_weight.shape[0]
    return kernel_call(
        "pack",
        pack_kernel,
        11,
        [
            shape_of((rows, TIER), BF16), shape_of((rows, TIER + D), BF16), shape_of((8, D), F32),
            shape_of((AREA, D), BF16),
        ],
        smem=1, far=range(1, 11),
    )(keep, qkv_weight, *args)


def prepare_kernel(
    count, wide, tokens_ref, maps_ref, params_ref, relh_ref, relw_ref, mask_ref, upb_ref,
    a1_ref, turned_ref, att_ref, feed_ref, table_ref, twice_ref, fill_ref, wideb_ref,
):
    wideb_ref[...] = upb_ref[...].astype(F32).reshape(wideb_ref.shape)
    spread = spread_rows()
    x = dot_nn(spread, tokens_ref[...])
    source = iota((D, D), 1)
    att = (rows_from(maps_ref, 0, D // (count * wide), wide) == source).astype(F32).astype(BF16)
    att_ref[...] = att
    feed_ref[...] = (rows_from(maps_ref, 5, D // count, 1, paired=True) == source).astype(F32).astype(BF16)
    unit, _ = norm_parts(x)
    a1 = (unit * params_ref[0:1] + params_ref[1:2]).astype(BF16)
    a1_ref[...] = dot_nt(a1, att).astype(BF16)
    turned_ref[...] = dot_nt(att, a1).astype(BF16)
    one = dot_tn(relh_ref[...], table_places(0).astype(BF16)) + dot_tn(
        relw_ref[...], table_places(W_START, straight=True).astype(BF16)
    )
    blank = jnp.zeros((HEAD, LANES), F32)
    table_ref[:HEAD, :] = jnp.concatenate([one, blank], axis=1).astype(BF16)
    table_ref[HEAD:, :] = jnp.concatenate([blank, pltpu.roll(one, HEAD, 1)], axis=1).astype(BF16)
    twice = sum(
        dot_tn(ref[...], table_places(start + more).astype(BF16))
        for ref, start in ((relh_ref, 0), (relw_ref, TWICE))
        for more in (0, 2 * ROW)
    )
    twice_ref[:HEAD, :] = jnp.concatenate([twice, blank], axis=1).astype(BF16)
    twice_ref[HEAD:, :] = jnp.concatenate([blank, twice], axis=1).astype(BF16)
    seen = dot_nt((mask_ref[...] > 0).astype(F32).astype(BF16), spread)
    key = iota((1, R), 1)
    fill_ref[...] = jnp.where(key % ROW >= WIN, -3e38, jnp.where(seen > 0.5, 0.0, -1e9))


def prepare(tokens, params, rel_h, rel_w, mask, upb):
    count, wide = lax.axis_size("dp"), lax.axis_size("mp")
    return kernel_call(
        "prepare",
        partial(prepare_kernel, count, wide),
        7,
        [
            shape_of((R, D), BF16), shape_of((D, R), BF16), shape_of((D, D), BF16), shape_of((D, D), BF16),
            shape_of((LANES, 2 * LANES), BF16), shape_of((LANES, 2 * LANES), BF16), shape_of((1, R), F32),
            shape_of((1, upb.shape[0]), F32),
        ],
        far=(0, 1, 3, 4, 5, 6),
    )(tokens, row_maps(count, wide), params, rel_h, rel_w, mask, upb)


def act_kernel(dm_ref, down_ref, out_ref, sum_ref):
    sum_ref[...] = jnp.sum(dm_ref[...].astype(F32), axis=0, keepdims=True)
    out_ref[...] = dot_nt(dm_ref[...], down_ref[...])


def act_grad(dm, down):
    return kernel_call("act", act_kernel, 2, [shape_of((AREA, down.shape[0]), F32), shape_of((1, D), F32)])(dm, down)


def heads_forward(qkv_ref, tables, fill, p_ref, out):
    ones = row_masks()
    sums = jnp.ones((R, LANES), BF16)
    left = iota((R, LANES), 1) < HEAD
    for pair in range(PAIRS // 2):
        at = pair * LANES
        q2 = qkv_ref[:, at : at + LANES]
        k2 = qkv_ref[:, HALF + at : HALF + at + LANES].astype(F32)
        v2 = jnp.concatenate([qkv_ref[:, 2 * HALF + at : 2 * HALF + at + LANES], sums], axis=1)
        products = dot_nn(q2, tables)
        q2 = q2.astype(F32) * HEAD**-0.5
        outs = []
        for side in range(2):
            mine = left if side == 0 else ~left
            offsets = query_offsets(products[:, side * LANES : (side + 1) * LANES], HEAD * (1 - side))
            q_aug = jnp.where(mine, q2, offsets).astype(BF16)
            k_aug = jnp.where(mine, k2, ones).astype(BF16)
            scores = dot_nt(q_aug, k_aug)
            scores = jnp.where(fill < 0.0, fill, scores)
            expo = jnp.exp(scores - jnp.max(scores, axis=-1, keepdims=True))
            mixed = dot_nn(expo.astype(BF16), v2)
            scale = 1.0 / mixed[:, LANES:]
            scale = jnp.concatenate([scale, scale[:, : R - LANES]], axis=1)
            p_ref[2 * pair + side] = (expo * scale).astype(BF16)
            outs.append(mixed[:, :LANES] * scale[:, :LANES])
        out(at, jnp.where(left, outs[0], outs[1]).astype(BF16))


def project(a1_ref, own_ref, other_ref, bias, qkv_ref):
    total = dot_nn(a1_ref[:, :HALF], own_ref[:, :TIER]) + dot_nn(a1_ref[:, HALF:], other_ref[:, :TIER])
    qkv_ref[...] = (total + bias).astype(BF16)


def tier_bias(params_ref, tier):
    at = tier * HALF
    return jnp.concatenate(
        [
            params_ref[6:7, at : at + HALF],
            jnp.zeros((1, HALF), F32),
            params_ref[7:8, at : at + HALF],
        ],
        axis=1,
    )


def attend_first_kernel(a1_ref, own_ref, other_ref, params_ref, table_ref, fill_ref, qkv_ref, p_ref, o_ref):
    project(a1_ref, own_ref, other_ref, tier_bias(params_ref, 0), qkv_ref)

    def out(at, value):
        o_ref[:, at : at + LANES] = value

    heads_forward(qkv_ref, table_ref[...], fill_ref[...], p_ref, out)


def attend_first(*args):
    return kernel_call(
        "attend1",
        attend_first_kernel,
        6,
        [shape_of((R, TIER), BF16), shape_of((HEADS // 2, R, R), BF16), shape_of((R, HALF), BF16)],
    )(*args)


def attend_second_kernel(
    keep_ref, a1_ref, own_ref, other_ref, params_ref, table_ref, fill_ref, first_ref, x_ref, att_ref,
    qkv_ref, p_ref, turned_ref, mid_ref, a2_ref,
    o_ref,
):
    project(a1_ref, own_ref, other_ref, tier_bias(params_ref, 1), qkv_ref)
    o_ref[:, :HALF] = first_ref[...]

    def out(at, value):
        o_ref[:, HALF + at : HALF + at + LANES] = value

    heads_forward(qkv_ref, table_ref[...], fill_ref[...], p_ref, out)
    rows = dot_tn(spread_rows(), o_ref[...]).astype(BF16)
    moved = dot_nt(rows, att_ref[...]).astype(BF16)
    branch = dot_nn(moved[:, :HALF], own_ref[:, TIER:]) + dot_nn(moved[:, HALF:], other_ref[:, TIER:])
    turned_ref[...] = dot_nt(att_ref[...], rows).astype(BF16)
    rate = rate_of(keep_ref, 0)
    middle = x_ref[...].astype(F32) + rate * (branch + params_ref[2:3])
    mid_ref[...] = middle
    unit, _ = norm_parts(middle)
    a2_ref[...] = (unit * params_ref[3:4] + params_ref[4:5]).astype(BF16)


def attend_second(*args):
    return kernel_call(
        "attend2",
        attend_second_kernel,
        10,
        [
            shape_of((R, TIER), BF16), shape_of((HEADS // 2, R, R), BF16), shape_of((D, AREA), BF16),
            shape_of((AREA, D), F32), shape_of((AREA, D), BF16),
        ],
        smem=1, scratch=[pltpu.VMEM((R, D), BF16)],
    )(*args)


def feed_kernel(a2_ref, up_ref, upb_ref, gact_ref, g_ref, dh_ref, da2_ref):
    total = None
    for at in range(0, up_ref.shape[1], STEP):
        here = slice(at, at + STEP)
        hidden = dot_nn(a2_ref[...], up_ref[:, here]) + upb_ref[:, here]
        phi = 0.5 + 0.5 * lax.erf(hidden * 0.5**0.5)
        g_ref[:, here] = (hidden * phi).astype(BF16)
        slope = phi + hidden * (jnp.exp(-0.5 * hidden * hidden) * 0.3989422804014327)
        dh = (gact_ref[:, here] * slope).astype(BF16)
        dh_ref[:, here] = dh
        part = dot_nt(dh, up_ref[:, here])
        total = part if total is None else total + part
    da2_ref[...] = total.astype(da2_ref.dtype)


def feed(a2, up, upb, gact, kind):
    hidden = up.shape[1]
    return kernel_call(
        "feed",
        feed_kernel,
        4,
        [shape_of((AREA, hidden), BF16), shape_of((AREA, hidden), BF16), shape_of((AREA, D), kind)],
    )(a2, up, upb, gact)


def feed_weights_kernel(count, map_ref, down_ref, *refs):
    dms, acts, a2s, dhs = (refs[i * count : (i + 1) * count] for i in range(4))
    refs = refs[4 * count :]
    depth = lax.axis_size("dp") // 4
    rows = HALF // (2 * depth)
    for lefts, rights, by_z in ((dms, acts, Z_FIRST[0]), (a2s, dhs, Z_FIRST[1])):
        blocks = depth if by_z else 2
        outs, refs = refs[: 2 * blocks], refs[2 * blocks :]
        turned = [dot_nt(map_ref[...], left[...]).astype(BF16) for left in lefts]
        for at in range(0, rights[0].shape[1], STEP):
            here = slice(at, at + STEP)
            total = dot_nn(turned[0], rights[0][:, here])
            for j in range(1, count):
                total = total + dot_nn(turned[j], rights[j][:, here])
            total = total.astype(BF16)
            for s in range(2):
                for y in range(2):
                    if not by_z:
                        start = s * HALF + y * HALF // 2
                        outs[2 * s + y][:, here] = total[start : start + HALF // 2]
                        continue
                    for z in range(depth):
                        start = s * HALF + (y * depth + z) * rows
                        outs[depth * s + z][y * rows : (y + 1) * rows, here] = total[start : start + rows]
    sum_ref, *outs = refs
    for j in range(count):
        outs[j][...] = dot_nn(acts[j][...], down_ref[...]).astype(outs[j].dtype)
    sums = jnp.sum(dhs[0][...].astype(F32), axis=0, keepdims=True)
    for j in range(1, count):
        sums = sums + jnp.sum(dhs[j][...].astype(F32), axis=0, keepdims=True)
    sum_ref[...] = sums


def feed_weights(row_map, down, dms, acts, a2s, dhs):
    count = len(dms)
    columns = acts[0].shape[1]
    blocks = [lax.axis_size("dp") // 4 if by_z else 2 for by_z in Z_FIRST]
    made = kernel_call(
        "feedw",
        partial(feed_weights_kernel, count),
        2 + 4 * count,
        [shape_of((HALF // n, columns), BF16) for n in blocks for _ in range(2 * n)]
        + [shape_of((1, columns), F32)]
        + [shape_of((AREA, D), F32 if j == 0 else BF16) for j in range(count)],
    )(row_map, down, *dms, *acts, *a2s, *dhs)
    grads = []
    for n in blocks:
        grads += [made[:n], made[n : 2 * n]]
        made = made[2 * n :]
    return *grads, *made


def heads_back(qkv_ref, p_ref, do_at, tables, dqkv_ref):
    ones = row_masks(down=True)
    left = iota((R, LANES), 1) < HEAD
    table_grad = jnp.zeros((LANES, 2 * LANES), F32)
    for pair in range(PAIRS // 2):
        at = pair * LANES
        q2 = qkv_ref[:, at : at + LANES]
        q_wide = q2.astype(F32)
        k2 = qkv_ref[:, HALF + at : HALF + at + LANES].astype(F32)
        v2 = qkv_ref[:, 2 * HALF + at : 2 * HALF + at + LANES]
        do2 = do_at(at).astype(F32)
        dq2 = dk2 = dv2 = None
        offsets = []
        for side in range(2):
            mine = left if side == 0 else ~left
            probs = p_ref[2 * pair + side]
            do_mine = jnp.where(mine, do2, 0.0).astype(BF16)
            dv = dot_tn(probs, do_mine)
            dp = dot_nt(do_mine, v2)
            wide = probs.astype(F32)
            ds = (wide * (dp - jnp.sum(wide * dp, axis=-1, keepdims=True))).astype(BF16)
            k_aug = jnp.where(mine, k2, ones).astype(BF16)
            dq_aug = dot_nn(ds, k_aug)
            offsets.append(offset_grads(dq_aug, HEAD * (1 - side)))
            dk = dot_tn(ds, jnp.where(mine, q_wide, 0.0).astype(BF16))
            if side == 0:
                dq2, dk2, dv2 = dq_aug, dk, dv
            else:
                dq2, dk2, dv2 = jnp.where(mine, dq_aug, dq2), dk2 + dk, dv2 + dv
        spread = jnp.concatenate(offsets, axis=1).astype(BF16)
        dq2 = dq2 * HEAD**-0.5 + dot_nt(spread, tables)
        table_grad = table_grad + dot_tn(q2, spread)
        dqkv_ref[:, at : at + LANES] = dq2.astype(BF16)
        dqkv_ref[:, HALF + at : HALF + at + LANES] = (dk2 * HEAD**-0.5).astype(BF16)
        dqkv_ref[:, 2 * HALF + at : 2 * HALF + at + LANES] = dv2.astype(BF16)
    return table_grad[:HEAD, :LANES] + pltpu.roll(table_grad[HEAD:, LANES:], HEAD, 1)


def back_norm_kernel(
    keep_ref, da2_ref, got_ref, mid_ref, g_ref, params_ref, own_ref, other_ref, att_ref,
    dmid_ref, do_ref, dy_ref, sums_ref,
):
    da2 = da2_ref[...] + got_ref[...].astype(F32)
    unit, factor = norm_parts(mid_ref[...])
    dmid = g_ref[...].astype(F32) + norm_back(da2, unit, factor, params_ref[3:4])
    dmid_ref[...] = dmid
    dy = (rate_of(keep_ref, 0) * dmid).astype(BF16)
    dy_ref[...] = dy
    moved = jnp.concatenate(
        [dot_nt(dy, own_ref[:, TIER:]).astype(BF16), dot_nt(dy, other_ref[:, TIER:]).astype(BF16)], axis=1
    )
    rows = dot_nn(moved, att_ref[...]).astype(BF16)
    do_ref[...] = dot_nn(spread_rows(), rows).astype(BF16)
    sums_ref[0:1] = jnp.sum(dy.astype(F32), axis=0, keepdims=True)
    sums_ref[1:2] = jnp.sum(da2 * unit, axis=0, keepdims=True)
    sums_ref[2:3] = jnp.sum(da2, axis=0, keepdims=True)


def back_norm(*args):
    return kernel_call(
        "backnorm",
        back_norm_kernel,
        9,
        [shape_of((AREA, D), F32), shape_of((R, D), BF16), shape_of((AREA, D), BF16), shape_of((3, D), F32)],
        smem=1,
    )(*args)


def back_kernel(tier, do_ref, turned_ref, qkv_ref, p_ref, table_ref, *refs):
    if tier == 0:
        o_ref, dy_ref, *refs = refs
    dqkv_ref, *refs, sums_ref, tab_ref = refs
    tab_ref[...] = heads_back(
        qkv_ref, p_ref, lambda at: do_ref[:, tier * HALF + at : tier * HALF + at + LANES], table_ref[...], dqkv_ref
    )
    wide = lax.axis_size("mp")
    blocks = (wide, 2)[tier]
    rows = HALF // (2 * wide)
    for s in range(2):
        part = dot_nn(turned_ref[s * HALF : (s + 1) * HALF], dqkv_ref[...]).astype(BF16)
        outs = refs[s * blocks : (s + 1) * blocks]
        if tier == 0:
            more = dot_nn(o_ref[s * HALF : (s + 1) * HALF], dy_ref[...]).astype(BF16)
        for x in range(wide):
            if tier == 0:
                outs[x][:, :TIER] = part[2 * x * rows : 2 * (x + 1) * rows]
                outs[x][:, TIER:] = more[2 * x * rows : 2 * (x + 1) * rows]
                continue
            for y in range(2):
                at_row = (x * 2 + y) * rows
                outs[y][x * rows : (x + 1) * rows] = part[at_row : at_row + rows]
    sums_ref[:, :HALF] = jnp.sum(dqkv_ref[:, :HALF].astype(F32), axis=0, keepdims=True)
    sums_ref[:, HALF:] = jnp.sum(dqkv_ref[:, 2 * HALF :].astype(F32), axis=0, keepdims=True)


def back(tier, *args):
    blocks = (lax.axis_size("mp"), 2)[tier]
    dqkv, *grads, sums, table = kernel_call(
        f"back{tier + 1}",
        partial(back_kernel, tier),
        len(args),
        [shape_of((R, TIER), BF16)]
        + [shape_of((HALF // blocks, TIER + D * (tier == 0)), BF16)] * (2 * blocks)
        + [shape_of((1, D), F32), shape_of((HEAD, LANES), F32)],
    )(*args)
    return dqkv, grads[:blocks], grads[blocks:], sums, table


def finish_kernel(
    wide, keep_ref, dq1_ref, dq2_ref, own1_ref, other1_ref, own2_ref, other2_ref, att_ref, x_ref, dmid_ref,
    params_ref, mid_ref, m_ref, mgot_ref, downb_ref, upb_ref, sums0_ref, sums1_ref, sums2_ref, tab1_ref, tab2_ref,
    dx_ref, result_ref, small_ref,
):
    spread = spread_rows()
    dq1, dq2 = dot_tn(spread, dq1_ref[...]).astype(BF16), dot_tn(spread, dq2_ref[...]).astype(BF16)
    halves = []
    for first, second in ((own1_ref, own2_ref), (other1_ref, other2_ref)):
        halves.append(dot_nt(dq1, first[...]) + dot_nt(dq2, second[:, :TIER]))
    moved = jnp.concatenate(halves, axis=1)
    high = moved.astype(BF16)
    low = (moved - high.astype(F32)).astype(BF16)
    da1 = dot_nn(high, att_ref[...]) + dot_nn(low, att_ref[...])
    unit, factor = norm_parts(x_ref[...].astype(F32))
    dx_ref[...] = (dmid_ref[...] + norm_back(da1, unit, factor, params_ref[0:1])).astype(BF16)
    rate = rate_of(keep_ref, 1)
    total = m_ref[...] + mgot_ref[...].astype(F32) + params_ref[5:6]
    result_ref[...] = (mid_ref[...] + rate * total).astype(BF16)

    small_ref[...] = jnp.zeros(small_ref.shape, F32)

    def put(name, value):
        for i in range(D // LANES):
            small_ref[piece(SMALL[name] + i)] = value[:, i * LANES : (i + 1) * LANES]

    put("gain1", jnp.sum(da1 * unit, axis=0, keepdims=True))
    put("shift1", jnp.sum(da1, axis=0, keepdims=True))
    put("projb", sums0_ref[0:1])
    put("gain2", sums0_ref[1:2])
    put("shift2", sums0_ref[2:3])
    put("qbias", jnp.concatenate([sums1_ref[:, :HALF], sums2_ref[:, :HALF]], axis=1))
    put("vbias", jnp.concatenate([sums1_ref[:, HALF:], sums2_ref[:, HALF:]], axis=1))
    put("downb", downb_ref[...])
    table = tab1_ref[...] + tab2_ref[...]
    low, high = table[: HEAD // 2], table[HEAD // 2 :]
    lane = iota(low.shape, 1)
    packed = jnp.where(
        lane < 32,
        low,
        jnp.where(
            lane < 64,
            pltpu.roll(low, (32 - W_START) % LANES, 1),
            jnp.where(lane < 96, pltpu.roll(high, 64, 1), pltpu.roll(high, (96 - W_START) % LANES, 1)),
        ),
    )
    for i in range(HEAD // 2):
        small_ref[piece(SMALL_TABLE + i)] = packed[i : i + 1]
    count = lax.axis_size("dp")
    size = upb_ref.shape[1] // count
    for m in range(wide):
        for i in range(count):
            rows, lanes = piece(SMALL_UP + m * count + i)
            value = upb_ref[:, i * size : (i + 1) * size]
            lanes = slice(lanes.start, lanes.start + size)
            small_ref[rows, lanes] = jnp.where(lax.axis_index("mp") == m, value, 0.0)


def finish(wide, rows, *args):
    return kernel_call(
        "finish",
        partial(finish_kernel, wide),
        21,
        [shape_of((AREA, D), BF16), shape_of((AREA, D), BF16), shape_of((rows, TIER), F32)],
        smem=1, out_far=(0, 1),
    )(*args)


def outputs_kernel(
    n_parts, rows, *refs
):
    parts, refs = refs[:n_parts], refs[n_parts:]
    gain1_ref, shift1_ref, qv_ref, relh_ref, relw_ref, projb_ref, gain2_ref, shift2_ref, upb_ref, downb_ref = refs[:10]
    table_ref, up_ref = refs[10:]
    total = parts[0][...]
    for part in parts[1:]:
        total = total + part[part.shape[0] - rows :].astype(F32)
    flat = {
        "gain1": gain1_ref, "shift1": shift1_ref, "projb": projb_ref, "gain2": gain2_ref, "shift2": shift2_ref,
        "downb": downb_ref,
    }

    def at(place):
        here, lanes = piece(place)
        return total[here, lanes]

    for i in range(D // LANES):
        here = slice(i * LANES, (i + 1) * LANES)
        for name, ref in flat.items():
            ref[here] = at(SMALL[name] + i)[0]
        qv_ref[0:1, here] = at(SMALL["qbias"] + i)
        qv_ref[1:2, here] = at(SMALL["vbias"] + i)
    for i in range(HEAD // 2):
        table_ref[i : i + 1] = at(SMALL_TABLE + i)
    for start, ref in ((0, relh_ref), (32, relw_ref)):
        for half in range(2):
            ref[:, half * 32 : half * 32 + 32] = lax.dot_general(
                table_places(start + 64 * half, straight=start > 0), table_ref[...], (((1,), (1,)), ((), ())),
                precision=lax.Precision.HIGHEST, preferred_element_type=F32,
            )
    for i in range(up_ref.shape[0]):
        up_ref[i : i + 1] = at(SMALL_UP + i)
    place = lax.axis_index("mp") * lax.axis_size("dp") + lax.axis_index("dp")
    upb_ref[...] = up_ref[place, : upb_ref.shape[0]]


def outputs(parts, size, ups):
    row = shape_of((D,), F32)
    table = shape_of((TABLE, HEAD), F32)
    return kernel_call(
        "outputs",
        partial(outputs_kernel, len(parts), parts[0].shape[0]),
        len(parts),
        [row, row, shape_of((2, D), F32), table, table, row, row, row, shape_of((size,), F32), row],
        scratch=[pltpu.VMEM((HEAD // 2, LANES), F32), pltpu.VMEM((ups, LANES), F32)],
        out_far=range(10),
    )(*parts)


def per_device(
    tokens, ln1_gain, ln1_bias, qkv_weight, qv_bias, rel_pos_h, rel_pos_w, proj_weight, proj_bias,
    ln2_gain, ln2_bias, fc1_weight, fc1_bias, fc2_weight, fc2_bias, keep_mask, key_mask, out_grad,
):
    wide = lax.axis_size("mp")
    hidden = fc1_weight.shape[1]
    first, second, params, dm = pack(
        keep_mask, qkv_weight, proj_weight, ln1_gain, ln1_bias, proj_bias, ln2_gain, ln2_bias, fc2_bias, qv_bias, out_grad
    )
    made, chains = {}, {}

    def gated(value, task, kind):
        others = [made[name] for name in GATES.get(f"{task}:{kind}", ())]
        return after(value, *others) if others else value

    def front(name):
        if name == "dm":
            sent = gated(dm, name, "s")
            return gated([move_x(sent, -s) for s in range(1, wide)], name, "r")
        if name == "prep":
            return prepare(gated(tokens, name, "s"), params, rel_pos_h, rel_pos_w, key_mask, fc1_bias)
        if name == "act0":
            return act_grad(gated(dm, name, "s"), fc2_weight)
        if name == "act1":
            return [act_grad(v, fc2_weight) for v in gated(made["dm"], name, "s")]
        if name == "attend1":
            a1, _, _, _, _, twice, fill, _ = made["prep"]
            return attend_first(gated(a1, name, "s"), chains["1"], made["c1"], params, twice, fill)
        step, tier = name
        if step == "z":
            sent = gated((first, second)[int(tier) - 1], name, "s")
            chains[tier] = gated(gather_z(sent), name, "r")
            return chains[tier]
        if step == "n":
            return gated(gather_near(gated(chains[tier], name, "s")), name, "r")
        if step == "f":
            made["n" + tier] = gated(made["n" + tier], name, "s")
            return gated(gather_far(made["n" + tier]), name, "r")
        chains[tier] = gated(gather_join(chains[tier], made["n" + tier], made["f" + tier]), name, "s")
        return gated(move_c(chains[tier]), name, "r")

    for name in FRONT:
        made[name] = front(name)
    a1, a1_turned, att_map, feed_map, tables, twice, fill, upb = made["prep"]
    dms = [dm, *made["dm"]]
    acts = [made["act0"], *made["act1"]]
    gacts, downb = [v[0] for v in acts], acts[0][1]
    own1, other1, own2, other2 = chains["1"], made["c1"], chains["2"], made["c2"]
    qkv1, probs1, att1 = made["attend1"]
    qkv2, probs2, att_turned, middle, a2 = attend_second(
        keep_mask, a1, own2, other2, params, twice, fill, att1, tokens, att_map
    )

    a2s = [a2] + [move_x(a2, -s) for s in range(1, wide)]
    fed = [feed(a2, fc1_weight, upb, gacts[0], F32)]
    for j in range(1, wide):
        fed.append(feed(after(a2s[j], fed[-1][2]), fc1_weight, upb, gacts[j], BF16))
    da2 = fed[0][2]
    got = [move_x(fed[s][2], s) for s in range(1, wide)]
    down_keep, down_send, up_keep, up_send, upb_sum, *outs = feed_weights(
        after(feed_map, fed[-1][2]), fc2_weight, dms, [f[0] for f in fed], a2s, [f[1] for f in fed]
    )
    got, down_send, up_send, outs = lax.optimization_barrier((got, down_send, up_send, outs))
    got = got[0] if wide == 2 else add_up(*got)
    depth = lax.axis_size("dp") // 4
    moves = {"x": (move_x, wide), "y": (turn_y, 2), "z": (move_z, depth)}
    small_rows = -(-(SMALL_UP + wide * lax.axis_size("dp")) // PIECES)
    small_rows += -small_rows % 16

    def cores(name, keep, send, axes):
        sent = gated(send, f"{name}c", "s")
        got = gated([move_c(v) for v in sent], f"{name}c", "r")
        chains[name] = (list(zip(keep, got)), axes)
        return got

    def count_of(axis):
        return depth if axis in "z0" else depth >> int(axis) if axis.isdigit() else moves[axis][1]

    def along(name, axis):
        sums, axes = chains[name]
        carries = ROUTE.get(axis) == name
        if axis.isdigit():
            mask = 1 << int(axis)
            sent = [jnp.concatenate([add_up(*v).astype(BF16) for v in sums[1::2]])]
            sent = gated(sent, f"{name}{axis}", "s")
            got = gated([swap_z(v, mask) for v in sent], f"{name}{axis}", "r")
            size = sums[0][0].shape[0]
            sums = [[*v, got[0][i * size : (i + 1) * size]] for i, v in enumerate(sums[::2])]
            axes = axes[axes.index(axis) + 1 :]
            if axes and axes[0].isdigit():
                chains[name] = (sums, axes)
            else:
                chains[name] = (split(sums[0], count_of(axes[0])), axes) if axes else (sums[0], axes)
            return got
        if axis == "z" and name in "du":
            move = swap_z
        else:
            move, _ = moves[axis]
        sent = [add_up(*v).astype(BF16) for v in sums[1:]]
        if carries:
            extra = chains["s"].astype(BF16)
            sent = [jnp.concatenate([v, extra]) for v in sent]
        sent = gated(sent, f"{name}{axis}", "s")
        got = gated([move(v, s + 1) for s, v in enumerate(sent)], f"{name}{axis}", "r")
        rest = [*sums[0], *got]
        if carries:
            rows = sums[0][0].shape[0]
            rest = [*sums[0], *[v[:rows] for v in got]]
            if axis == "z":
                chains["s"] = [chains["s"], *got]
            else:
                chains["s"] = add_up(chains["s"], *[v[rows:] for v in got])
        axes = axes[axes.index(axis) + 1 :]
        chains[name] = (split(rest, count_of(axes[0])), axes) if axes else (rest, axes)
        return got

    def small_cores():
        flat = gated(made["finish"][2], "sc", "s")
        got = gated(move_c(flat), "sc", "r")
        chains["s"] = flat + got
        return got

    def task(name):
        if name == "norm":
            return back_norm(keep_mask, da2, got, middle, out_grad, params, own2, other2, att_map)
        if name in ("back1", "back2"):
            tier = int(name[-1]) - 1
            do = gated(made["norm"][1], name, "s")
            more = (att_turned, made["norm"][2]) if tier == 0 else ()
            return back(tier, do, a1_turned, (qkv1, qkv2)[tier], (probs1, probs2)[tier], tables, *more)
        if name == "m":
            moved = [move_x(v, s + 1) for s, v in enumerate(gated(outs[1:], "m", "s"))]
            moved = gated(moved, "m", "r")
            return moved[0] if wide == 2 else add_up(*moved)
        if name == "finish":
            first, second = made["back1"], made["back2"]
            mid = gated(middle, "finish", "s")
            return finish(
                wide, small_rows, keep_mask, first[0], second[0], own1, other1, own2, other2, att_map, tokens,
                made["norm"][0], params, mid, outs[0], made["m"], downb, upb_sum, made["norm"][3], first[3], second[3],
                first[4], second[4],
            )
        chain, axis = name
        if chain == "s":
            return small_cores()
        if axis != "c":
            return along(chain, axis)
        if chain in "du":
            keep, send = (down_keep, down_send) if chain == "d" else (up_keep, up_send)
            bits = "".join(str(i) for i in range(depth.bit_length() - 1)) if TREE["du".index(chain)] else "z"
            return cores(chain, keep, send, bits + "y" if Z_FIRST["du".index(chain)] else "y" + bits)
        tier = "ab".index(chain)
        return cores(chain, made[f"back{tier + 1}"][1], made[f"back{tier + 1}"][2], ("xyz", "yxz")[tier])

    for name in ORDER:
        made[name] = task(name)
        while name[-1] == "1" and name[0] in "du" and chains[name[0]][1][:1].isdigit():
            along(name[0], chains[name[0]][1][0])
    grad_in, result, _ = made["finish"]
    small = chains["s"]
    down_grad, up_grad, rows1, rows2 = (add_up(*chains[name][0]) for name in "duab")
    proj_grad = rows1[:, TIER:]

    pieces = [
        piece
        for i in range(3)
        for piece in (rows1[:, i * HALF : (i + 1) * HALF], rows2[:, i * HALF : (i + 1) * HALF])
    ]
    qkv_grad = jnp.concatenate(pieces, axis=1)

    gain1, shift1, qv_grad, relh_grad, relw_grad, projb, gain2, shift2, up_bias_grad, downb = outputs(
        small, hidden // lax.axis_size("dp"), wide * lax.axis_size("dp")
    )
    return (
        result, grad_in, gain1, shift1, qkv_grad, qv_grad, relh_grad, relw_grad, proj_grad, projb, gain2, shift2,
        up_grad, up_bias_grad, down_grad.T, downb,
    )


def solution(mesh):
    in_specs = (
        P(("dp", "mp"), None),
        P(),
        P(),
        P(("dp", "mp"), None),
        P(),
        P(),
        P(),
        P(("dp", "mp"), None),
        P(),
        P(),
        P(),
        P(None, "mp"),
        P("mp"),
        P("mp", None),
        P(),
        P(("dp", "mp"), None),
        P(("dp", "mp"), None),
        P(("dp", "mp"), None),
    )
    out_specs = (
        P(("dp", "mp"), None),
        P(("dp", "mp"), None),
        P(),
        P(),
        P(("dp", "mp"), None),
        P(),
        P(),
        P(),
        P(("dp", "mp"), None),
        P(),
        P(),
        P(),
        P("dp", "mp"),
        P(("mp", "dp")),
        P("mp", "dp"),
        P(),
    )
    return jax.shard_map(
        per_device, mesh=mesh, in_specs=in_specs, out_specs=out_specs, check_vma=False
    )
```

```python
from functools import partial

import jax
import jax.numpy as jnp
import numpy as np
from jax import lax
from jax.experimental import pallas as pl
from jax.experimental.pallas import tpu as pltpu
from jax.sharding import PartitionSpec as P

D = 768
HEADS = 12
HEAD = 64
WIN = 14
AREA = WIN * WIN
ROW = 16
R = WIN * ROW
PAIRS = HEADS // 2
LANES = 128
TABLE = 2 * WIN - 1
TWICE = 59
W_START = HEAD + ROW + 2
HALF = D // 2
STEP = 384
TIER = 3 * HALF
F32 = jnp.float32
BF16 = jnp.bfloat16
VMEM = pl.BlockSpec(memory_space=pltpu.VMEM)
SMEM = pl.BlockSpec(memory_space=pltpu.SMEM)
LIMIT = 20 * 2**20
Z_FIRST = (False, False)
TREE = (True, True)
FRONT = ('dm', 'z1', 'prep', 'act1', 'z2', 'n1', 'n2', 'act0', 'f2', 'f1', 'c1', 'attend1', 'c2')
ORDER = ('dc', 'dy', 'm', 'norm', 'back2', 'bc', 'back1', 'finish', 'ac', 'sc', 'by', 'bx', 'ax', 'd0', 'd1', 'bz', 'uc', 'uy', 'ay', 'u0', 'u1', 'az')
GATES = {'n1:s': ['prep', 'dm'], 'n2:s': ['z2'], 'f1:s': ['n1'], 'act1:s': ['dm'], 'attend1:s': ['dm', 'f1'], 'z1:s': ['dm'], 'back1:s': ['dc'], 'back2:s': ['m', 'dc'], 'finish:s': ['bc', 'm'], 'ay:r': ['ac', 'back1', 'd1'], 'uc:s': ['dc'], 'bc:s': ['dy'], 'bx:r': ['dy'], 'bz:r': ['bc'], 'd0:s': ['finish'], 'd1:r': ['dy'], 'az:r': ['bz'], 'u1:r': ['by', 'bx'], 'uc:r': ['back2'], 'sc:r': ['ac'], 'ax:r': ['sc'], 'az:s': ['ay']}
ROUTE = {"y": "b", "x": "b", "z": "b"}
CHEAP = pl.CostEstimate(flops=1, bytes_accessed=1, transcendentals=0)
SMALL = {"gain1": 0, "shift1": 6, "qbias": 12, "vbias": 18, "projb": 24, "gain2": 30, "shift2": 36, "downb": 42}
SMALL_TABLE = 48
SMALL_UP = SMALL_TABLE + HEAD // 2
PIECES = TIER // LANES


def piece(place):
    return slice(place // PIECES, place // PIECES + 1), slice(place % PIECES * LANES, (place % PIECES + 1) * LANES)


def shape_of(shape, kind):
    return jax.ShapeDtypeStruct(shape, kind)


def kernel_call(name, body, n_in, outs, *, smem=0, scratch=(), far=(), out_far=()):
    call = pl.pallas_call(
        body,
        name=name,
        in_specs=[SMEM] * smem + [VMEM] * (n_in - smem),
        out_specs=[VMEM] * len(outs),
        out_shape=[o if i in out_far else pltpu.VMEM(o.shape, o.dtype) for i, o in enumerate(outs)],
        scratch_shapes=list(scratch),
        compiler_params=pltpu.CompilerParams(vmem_limit_bytes=LIMIT),
        cost_estimate=CHEAP,
    )

    def run(*args):
        spaces = [pltpu.HBM if i in far else pltpu.VMEM for i in range(smem, n_in)]
        return call(*args[:smem], *map(pltpu.with_memory_space_constraint, args[smem:], spaces))

    return run


def after(value, *others):
    return lax.optimization_barrier((value,) + others)[0]


def dp_pairs(count, dz=0, dy=0, dc=0):
    depth = count // 4
    pairs = []
    for place in range(count):
        z, y, c = place // 4, place // 2 % 2, place % 2
        pairs.append((place, (z + dz) % depth * 4 + (y + dy) % 2 * 2 + (c + dc) % 2))
    return pairs


def move_z(value, step):
    return lax.ppermute(value, "dp", dp_pairs(lax.axis_size("dp"), dz=step))


def swap_z(value, mask):
    pairs = [(place, place ^ (mask * 4)) for place in range(lax.axis_size("dp"))]
    return lax.ppermute(value, "dp", pairs)


def move_y(value):
    return lax.ppermute(value, "dp", dp_pairs(lax.axis_size("dp"), dy=1))


def move_c(value):
    return lax.ppermute(value, "dp", dp_pairs(lax.axis_size("dp"), dc=1))


def move_x(value, step=1):
    count = lax.axis_size("mp")
    return lax.ppermute(value, "mp", [(i, (i + step) % count) for i in range(count)])


def places():
    dp = lax.axis_index("dp")
    return dp // 4, dp // 2 % 2, dp % 2, lax.axis_index("mp")


def row_maps(count, wide):
    depth = count // 4
    place = np.arange(D)
    rows = D // (count * wide)
    block = place // rows
    att = [block % depth, block // depth % 2, block // (2 * depth) % wide, block // (2 * depth * wide), place % rows]
    rows = D // count
    block = place // rows
    feed = [block % depth, block // depth % 2, 0 * block, block // (2 * depth), place % rows]
    return np.stack(att + feed, axis=1).astype(np.int32)


def rows_from(maps_ref, start, rows, wide, paired=False):
    depth = lax.axis_size("dp") // 4
    dp = lax.axis_index("dp")

    def turned(i, here, size):
        there = maps_ref[:, start + i : start + i + 1] + here
        return jnp.where(there >= size, there - size, there)

    across = maps_ref[:, start : start + 1] ^ (dp // 4) if paired else turned(0, dp // 4, depth)
    block = (across * 2 + turned(1, dp // 2 % 2, 2)) * 2 + turned(3, dp % 2, 2)
    if wide > 1:
        block = block * wide + turned(2, lax.axis_index("mp"), wide)
    return block * rows + maps_ref[:, start + 4 : start + 5]


def gather_z(part):
    depth = lax.axis_size("dp") // 4
    return jnp.concatenate([part] + [move_z(part, -s) for s in range(1, depth)])


def gather_near(line):
    wide = lax.axis_size("mp")
    return [move_x(line, -s) for s in range(1, wide)], move_y(line)


def gather_far(near):
    along_x, along_y = near
    half = along_y.shape[1] // 2
    left = [move_y(b[:, :half]) for b in along_x]
    right = [move_x(along_y[:, half:], -s) for s in range(1, lax.axis_size("mp"))]
    return left, right


def gather_join(line, near, far):
    blocks = [line, near[1]]
    for along_x, first, second in zip(near[0], *far):
        blocks += [along_x, jnp.concatenate([first, second], axis=1)]
    return jnp.concatenate(blocks)


def add_up(first, *others):
    total = first.astype(F32)
    for other in others:
        total = total + other.astype(F32)
    return total


def blocks_of(rows, count):
    size = rows.shape[0] // count
    return [rows[i * size : (i + 1) * size] for i in range(count)]


def split(parts, count):
    return list(zip(*[blocks_of(v, count) for v in parts]))


def turn_y(value, step):
    return move_y(value)


def dot_nn(a, b):
    return lax.dot_general(a, b, (((1,), (0,)), ((), ())), preferred_element_type=F32)


def dot_nt(a, b):
    return lax.dot_general(a, b, (((1,), (1,)), ((), ())), preferred_element_type=F32)


def dot_tn(a, b):
    return lax.dot_general(a, b, (((0,), (0,)), ((), ())), preferred_element_type=F32)


def iota(shape, axis):
    return lax.broadcasted_iota(jnp.int32, shape, axis)


def norm_parts(rows_in):
    center = rows_in - jnp.mean(rows_in, axis=-1, keepdims=True)
    factor = lax.rsqrt(jnp.mean(center * center, axis=-1, keepdims=True) + 1e-06)
    return center * factor, factor


def norm_back(grad, unit, factor, gain):
    inner = grad * gain
    return factor * (
        inner
        - jnp.mean(inner, axis=-1, keepdims=True)
        - unit * jnp.mean(inner * unit, axis=-1, keepdims=True)
    )


def spread_rows():
    row, patch = iota((R, AREA), 0), iota((R, AREA), 1)
    return ((row % ROW < WIN) & (patch == row // ROW * WIN + row % ROW)).astype(F32).astype(BF16)


def row_masks(down=False):
    lane = iota((R, LANES), 1) % HEAD
    key = iota((R, LANES), 0)
    column = ROW - 1 - key % ROW if down else key % ROW
    here = jnp.where(lane // ROW % 2 == 0, key // ROW, column)
    return (lane % ROW == here).astype(F32)


def query_offsets(table, base):
    lane = iota((ROW, LANES), 1)
    inside = (lane >= base) & (lane < base + HEAD)
    in_h = inside & (lane // ROW % 2 == 0)
    rounded = lane // (2 * ROW) % 2 == 0
    outs = []
    for a in range(WIN):
        group = table[a * ROW : (a + 1) * ROW]
        at_h = pltpu.roll(group, (base - 13 + a) % LANES, 1)
        at_w = pltpu.roll(group, (base + ROW - TWICE - 13) % LANES, 1, stride=1, stride_axis=0)
        both = jnp.where(in_h, at_h, at_w)
        high = both.astype(BF16).astype(F32)
        outs.append(jnp.where(rounded, high, both - high))
    return jnp.concatenate(outs, axis=0)


def offset_grads(grad, base):
    lane = iota((ROW, LANES), 1)
    in_h = (lane >= base) & (lane < base + ROW)
    in_w = (lane >= base + ROW) & (lane < base + 2 * ROW)
    outs = []
    for a in range(WIN):
        group = grad[a * ROW : (a + 1) * ROW]
        from_h = pltpu.roll(jnp.where(in_h, group, 0.0), (HEAD + 13 - a) % LANES, 1)
        outs.append(from_h + pltpu.roll(jnp.where(in_w, group, 0.0), 0, 1, stride=1, stride_axis=0))
    return jnp.concatenate(outs, axis=0)


def table_places(start, straight=False):
    row, lane = iota((TABLE, LANES), 0), iota((TABLE, LANES), 1)
    return (lane - start == (row if straight else TABLE - 1 - row)).astype(F32)


def rate_of(keep_ref, branch):
    return jnp.where(keep_ref[0, branch] > 0, 1.0 / 0.9, 0.0).astype(F32)


def pack_kernel(
    keep_ref, qkv_ref, proj_ref, gain1_ref, shift1_ref, projb_ref, gain2_ref, shift2_ref, downb_ref, qvb_ref, grad_ref,
    first_ref, second_ref, params_ref, dm_ref,
):
    for tier, out in enumerate((first_ref, second_ref)):
        for i in range(3):
            out[:, i * HALF : (i + 1) * HALF] = qkv_ref[:, i * D + tier * HALF : i * D + (tier + 1) * HALF]
    second_ref[:, TIER:] = proj_ref[...]
    for i, ref in enumerate((gain1_ref, shift1_ref, projb_ref, gain2_ref, shift2_ref, downb_ref)):
        params_ref[i : i + 1] = ref[...].astype(F32).reshape(1, D)
    params_ref[6:8] = qvb_ref[...].astype(F32)
    dm_ref[...] = (rate_of(keep_ref, 1) * grad_ref[...].astype(F32)).astype(BF16)


def pack(keep, qkv_weight, *args):
    rows = qkv_weight.shape[0]
    return kernel_call(
        "pack",
        pack_kernel,
        11,
        [
            shape_of((rows, TIER), BF16), shape_of((rows, TIER + D), BF16), shape_of((8, D), F32),
            shape_of((AREA, D), BF16),
        ],
        smem=1, far=range(1, 11),
    )(keep, qkv_weight, *args)


def prepare_kernel(
    count, wide, tokens_ref, maps_ref, params_ref, relh_ref, relw_ref, mask_ref, upb_ref,
    a1_ref, turned_ref, att_ref, feed_ref, table_ref, twice_ref, fill_ref, wideb_ref,
):
    wideb_ref[...] = upb_ref[...].astype(F32).reshape(wideb_ref.shape)
    spread = spread_rows()
    x = dot_nn(spread, tokens_ref[...])
    source = iota((D, D), 1)
    att = (rows_from(maps_ref, 0, D // (count * wide), wide) == source).astype(F32).astype(BF16)
    att_ref[...] = att
    feed_ref[...] = (rows_from(maps_ref, 5, D // count, 1, paired=True) == source).astype(F32).astype(BF16)
    unit, _ = norm_parts(x)
    a1 = (unit * params_ref[0:1] + params_ref[1:2]).astype(BF16)
    a1_ref[...] = dot_nt(a1, att).astype(BF16)
    turned_ref[...] = dot_nt(att, a1).astype(BF16)
    one = dot_tn(relh_ref[...], table_places(0).astype(BF16)) + dot_tn(
        relw_ref[...], table_places(W_START, straight=True).astype(BF16)
    )
    blank = jnp.zeros((HEAD, LANES), F32)
    table_ref[:HEAD, :] = jnp.concatenate([one, blank], axis=1).astype(BF16)
    table_ref[HEAD:, :] = jnp.concatenate([blank, pltpu.roll(one, HEAD, 1)], axis=1).astype(BF16)
    twice = sum(
        dot_tn(ref[...], table_places(start + more).astype(BF16))
        for ref, start in ((relh_ref, 0), (relw_ref, TWICE))
        for more in (0, 2 * ROW)
    )
    twice_ref[:HEAD, :] = jnp.concatenate([twice, blank], axis=1).astype(BF16)
    twice_ref[HEAD:, :] = jnp.concatenate([blank, twice], axis=1).astype(BF16)
    seen = dot_nt((mask_ref[...] > 0).astype(F32).astype(BF16), spread)
    key = iota((1, R), 1)
    fill_ref[...] = jnp.where(key % ROW >= WIN, -3e38, jnp.where(seen > 0.5, 0.0, -1e9))


def prepare(tokens, params, rel_h, rel_w, mask, upb):
    count, wide = lax.axis_size("dp"), lax.axis_size("mp")
    return kernel_call(
        "prepare",
        partial(prepare_kernel, count, wide),
        7,
        [
            shape_of((R, D), BF16), shape_of((D, R), BF16), shape_of((D, D), BF16), shape_of((D, D), BF16),
            shape_of((LANES, 2 * LANES), BF16), shape_of((LANES, 2 * LANES), BF16), shape_of((1, R), F32),
            shape_of((1, upb.shape[0]), F32),
        ],
        far=(0, 1, 3, 4, 5, 6),
    )(tokens, row_maps(count, wide), params, rel_h, rel_w, mask, upb)


def act_kernel(dm_ref, down_ref, out_ref, sum_ref):
    sum_ref[...] = jnp.sum(dm_ref[...].astype(F32), axis=0, keepdims=True)
    out_ref[...] = dot_nt(dm_ref[...], down_ref[...])


def act_grad(dm, down):
    return kernel_call("act", act_kernel, 2, [shape_of((AREA, down.shape[0]), F32), shape_of((1, D), F32)])(dm, down)


def heads_forward(qkv_ref, tables, fill, p_ref, out):
    ones = row_masks()
    sums = jnp.ones((R, LANES), BF16)
    left = iota((R, LANES), 1) < HEAD
    for pair in range(PAIRS // 2):
        at = pair * LANES
        q2 = qkv_ref[:, at : at + LANES]
        k2 = qkv_ref[:, HALF + at : HALF + at + LANES].astype(F32)
        v2 = jnp.concatenate([qkv_ref[:, 2 * HALF + at : 2 * HALF + at + LANES], sums], axis=1)
        products = dot_nn(q2, tables)
        q2 = q2.astype(F32) * HEAD**-0.5
        outs = []
        for side in range(2):
            mine = left if side == 0 else ~left
            offsets = query_offsets(products[:, side * LANES : (side + 1) * LANES], HEAD * (1 - side))
            q_aug = jnp.where(mine, q2, offsets).astype(BF16)
            k_aug = jnp.where(mine, k2, ones).astype(BF16)
            scores = dot_nt(q_aug, k_aug)
            scores = jnp.where(fill < 0.0, fill, scores)
            expo = jnp.exp(scores - jnp.max(scores, axis=-1, keepdims=True))
            mixed = dot_nn(expo.astype(BF16), v2)
            scale = 1.0 / mixed[:, LANES:]
            scale = jnp.concatenate([scale, scale[:, : R - LANES]], axis=1)
            p_ref[2 * pair + side] = (expo * scale).astype(BF16)
            outs.append(mixed[:, :LANES] * scale[:, :LANES])
        out(at, jnp.where(left, outs[0], outs[1]).astype(BF16))


def project(a1_ref, own_ref, other_ref, bias, qkv_ref):
    total = dot_nn(a1_ref[:, :HALF], own_ref[:, :TIER]) + dot_nn(a1_ref[:, HALF:], other_ref[:, :TIER])
    qkv_ref[...] = (total + bias).astype(BF16)


def tier_bias(params_ref, tier):
    at = tier * HALF
    return jnp.concatenate(
        [
            params_ref[6:7, at : at + HALF],
            jnp.zeros((1, HALF), F32),
            params_ref[7:8, at : at + HALF],
        ],
        axis=1,
    )


def attend_first_kernel(a1_ref, own_ref, other_ref, params_ref, table_ref, fill_ref, qkv_ref, p_ref, o_ref):
    project(a1_ref, own_ref, other_ref, tier_bias(params_ref, 0), qkv_ref)

    def out(at, value):
        o_ref[:, at : at + LANES] = value

    heads_forward(qkv_ref, table_ref[...], fill_ref[...], p_ref, out)


def attend_first(*args):
    return kernel_call(
        "attend1",
        attend_first_kernel,
        6,
        [shape_of((R, TIER), BF16), shape_of((HEADS // 2, R, R), BF16), shape_of((R, HALF), BF16)],
    )(*args)


def attend_second_kernel(
    keep_ref, a1_ref, own_ref, other_ref, params_ref, table_ref, fill_ref, first_ref, x_ref, att_ref,
    qkv_ref, p_ref, turned_ref, mid_ref, a2_ref,
    o_ref,
):
    project(a1_ref, own_ref, other_ref, tier_bias(params_ref, 1), qkv_ref)
    o_ref[:, :HALF] = first_ref[...]

    def out(at, value):
        o_ref[:, HALF + at : HALF + at + LANES] = value

    heads_forward(qkv_ref, table_ref[...], fill_ref[...], p_ref, out)
    rows = dot_tn(spread_rows(), o_ref[...]).astype(BF16)
    moved = dot_nt(rows, att_ref[...]).astype(BF16)
    branch = dot_nn(moved[:, :HALF], own_ref[:, TIER:]) + dot_nn(moved[:, HALF:], other_ref[:, TIER:])
    turned_ref[...] = dot_nt(att_ref[...], rows).astype(BF16)
    rate = rate_of(keep_ref, 0)
    middle = x_ref[...].astype(F32) + rate * (branch + params_ref[2:3])
    mid_ref[...] = middle
    unit, _ = norm_parts(middle)
    a2_ref[...] = (unit * params_ref[3:4] + params_ref[4:5]).astype(BF16)


def attend_second(*args):
    return kernel_call(
        "attend2",
        attend_second_kernel,
        10,
        [
            shape_of((R, TIER), BF16), shape_of((HEADS // 2, R, R), BF16), shape_of((D, AREA), BF16),
            shape_of((AREA, D), F32), shape_of((AREA, D), BF16),
        ],
        smem=1, scratch=[pltpu.VMEM((R, D), BF16)],
    )(*args)


def feed_kernel(a2_ref, up_ref, upb_ref, gact_ref, g_ref, dh_ref, da2_ref):
    total = None
    for at in range(0, up_ref.shape[1], STEP):
        here = slice(at, at + STEP)
        hidden = dot_nn(a2_ref[...], up_ref[:, here]) + upb_ref[:, here]
        phi = 0.5 + 0.5 * lax.erf(hidden * 0.5**0.5)
        g_ref[:, here] = (hidden * phi).astype(BF16)
        slope = phi + hidden * (jnp.exp(-0.5 * hidden * hidden) * 0.3989422804014327)
        dh = (gact_ref[:, here] * slope).astype(BF16)
        dh_ref[:, here] = dh
        part = dot_nt(dh, up_ref[:, here])
        total = part if total is None else total + part
    da2_ref[...] = total.astype(da2_ref.dtype)


def feed(a2, up, upb, gact, kind):
    hidden = up.shape[1]
    return kernel_call(
        "feed",
        feed_kernel,
        4,
        [shape_of((AREA, hidden), BF16), shape_of((AREA, hidden), BF16), shape_of((AREA, D), kind)],
    )(a2, up, upb, gact)


def feed_weights_kernel(count, map_ref, down_ref, *refs):
    dms, acts, a2s, dhs = (refs[i * count : (i + 1) * count] for i in range(4))
    refs = refs[4 * count :]
    depth = lax.axis_size("dp") // 4
    rows = HALF // (2 * depth)
    for lefts, rights, by_z in ((dms, acts, Z_FIRST[0]), (a2s, dhs, Z_FIRST[1])):
        blocks = depth if by_z else 2
        outs, refs = refs[: 2 * blocks], refs[2 * blocks :]
        turned = [dot_nt(map_ref[...], left[...]).astype(BF16) for left in lefts]
        for at in range(0, rights[0].shape[1], STEP):
            here = slice(at, at + STEP)
            total = dot_nn(turned[0], rights[0][:, here])
            for j in range(1, count):
                total = total + dot_nn(turned[j], rights[j][:, here])
            total = total.astype(BF16)
            for s in range(2):
                for y in range(2):
                    if not by_z:
                        start = s * HALF + y * HALF // 2
                        outs[2 * s + y][:, here] = total[start : start + HALF // 2]
                        continue
                    for z in range(depth):
                        start = s * HALF + (y * depth + z) * rows
                        outs[depth * s + z][y * rows : (y + 1) * rows, here] = total[start : start + rows]
    sum_ref, *outs = refs
    for j in range(count):
        outs[j][...] = dot_nn(acts[j][...], down_ref[...]).astype(outs[j].dtype)
    sums = jnp.sum(dhs[0][...].astype(F32), axis=0, keepdims=True)
    for j in range(1, count):
        sums = sums + jnp.sum(dhs[j][...].astype(F32), axis=0, keepdims=True)
    sum_ref[...] = sums


def feed_weights(row_map, down, dms, acts, a2s, dhs):
    count = len(dms)
    columns = acts[0].shape[1]
    blocks = [lax.axis_size("dp") // 4 if by_z else 2 for by_z in Z_FIRST]
    made = kernel_call(
        "feedw",
        partial(feed_weights_kernel, count),
        2 + 4 * count,
        [shape_of((HALF // n, columns), BF16) for n in blocks for _ in range(2 * n)]
        + [shape_of((1, columns), F32)]
        + [shape_of((AREA, D), F32 if j == 0 else BF16) for j in range(count)],
    )(row_map, down, *dms, *acts, *a2s, *dhs)
    grads = []
    for n in blocks:
        grads += [made[:n], made[n : 2 * n]]
        made = made[2 * n :]
    return *grads, *made


def heads_back(qkv_ref, p_ref, do_at, tables, dqkv_ref):
    ones = row_masks(down=True)
    left = iota((R, LANES), 1) < HEAD
    table_grad = jnp.zeros((LANES, 2 * LANES), F32)
    for pair in range(PAIRS // 2):
        at = pair * LANES
        q2 = qkv_ref[:, at : at + LANES]
        q_wide = q2.astype(F32)
        k2 = qkv_ref[:, HALF + at : HALF + at + LANES].astype(F32)
        v2 = qkv_ref[:, 2 * HALF + at : 2 * HALF + at + LANES]
        do2 = do_at(at).astype(F32)
        dq2 = dk2 = dv2 = None
        offsets = []
        for side in range(2):
            mine = left if side == 0 else ~left
            probs = p_ref[2 * pair + side]
            do_mine = jnp.where(mine, do2, 0.0).astype(BF16)
            dv = dot_tn(probs, do_mine)
            dp = dot_nt(do_mine, v2)
            wide = probs.astype(F32)
            ds = (wide * (dp - jnp.sum(wide * dp, axis=-1, keepdims=True))).astype(BF16)
            k_aug = jnp.where(mine, k2, ones).astype(BF16)
            dq_aug = dot_nn(ds, k_aug)
            offsets.append(offset_grads(dq_aug, HEAD * (1 - side)))
            dk = dot_tn(ds, jnp.where(mine, q_wide, 0.0).astype(BF16))
            if side == 0:
                dq2, dk2, dv2 = dq_aug, dk, dv
            else:
                dq2, dk2, dv2 = jnp.where(mine, dq_aug, dq2), dk2 + dk, dv2 + dv
        spread = jnp.concatenate(offsets, axis=1).astype(BF16)
        dq2 = dq2 * HEAD**-0.5 + dot_nt(spread, tables)
        table_grad = table_grad + dot_tn(q2, spread)
        dqkv_ref[:, at : at + LANES] = dq2.astype(BF16)
        dqkv_ref[:, HALF + at : HALF + at + LANES] = (dk2 * HEAD**-0.5).astype(BF16)
        dqkv_ref[:, 2 * HALF + at : 2 * HALF + at + LANES] = dv2.astype(BF16)
    return table_grad[:HEAD, :LANES] + pltpu.roll(table_grad[HEAD:, LANES:], HEAD, 1)


def back_norm_kernel(
    keep_ref, da2_ref, got_ref, mid_ref, g_ref, params_ref, own_ref, other_ref, att_ref,
    dmid_ref, do_ref, dy_ref, sums_ref,
):
    da2 = da2_ref[...] + got_ref[...].astype(F32)
    unit, factor = norm_parts(mid_ref[...])
    dmid = g_ref[...].astype(F32) + norm_back(da2, unit, factor, params_ref[3:4])
    dmid_ref[...] = dmid
    dy = (rate_of(keep_ref, 0) * dmid).astype(BF16)
    dy_ref[...] = dy
    moved = jnp.concatenate(
        [dot_nt(dy, own_ref[:, TIER:]).astype(BF16), dot_nt(dy, other_ref[:, TIER:]).astype(BF16)], axis=1
    )
    rows = dot_nn(moved, att_ref[...]).astype(BF16)
    do_ref[...] = dot_nn(spread_rows(), rows).astype(BF16)
    sums_ref[0:1] = jnp.sum(dy.astype(F32), axis=0, keepdims=True)
    sums_ref[1:2] = jnp.sum(da2 * unit, axis=0, keepdims=True)
    sums_ref[2:3] = jnp.sum(da2, axis=0, keepdims=True)


def back_norm(*args):
    return kernel_call(
        "backnorm",
        back_norm_kernel,
        9,
        [shape_of((AREA, D), F32), shape_of((R, D), BF16), shape_of((AREA, D), BF16), shape_of((3, D), F32)],
        smem=1,
    )(*args)


def back_kernel(tier, do_ref, turned_ref, qkv_ref, p_ref, table_ref, *refs):
    if tier == 0:
        o_ref, dy_ref, *refs = refs
    dqkv_ref, *refs, sums_ref, tab_ref = refs
    tab_ref[...] = heads_back(
        qkv_ref, p_ref, lambda at: do_ref[:, tier * HALF + at : tier * HALF + at + LANES], table_ref[...], dqkv_ref
    )
    wide = lax.axis_size("mp")
    blocks = (wide, 2)[tier]
    rows = HALF // (2 * wide)
    for s in range(2):
        part = dot_nn(turned_ref[s * HALF : (s + 1) * HALF], dqkv_ref[...]).astype(BF16)
        outs = refs[s * blocks : (s + 1) * blocks]
        if tier == 0:
            more = dot_nn(o_ref[s * HALF : (s + 1) * HALF], dy_ref[...]).astype(BF16)
        for x in range(wide):
            if tier == 0:
                outs[x][:, :TIER] = part[2 * x * rows : 2 * (x + 1) * rows]
                outs[x][:, TIER:] = more[2 * x * rows : 2 * (x + 1) * rows]
                continue
            for y in range(2):
                at_row = (x * 2 + y) * rows
                outs[y][x * rows : (x + 1) * rows] = part[at_row : at_row + rows]
    sums_ref[:, :HALF] = jnp.sum(dqkv_ref[:, :HALF].astype(F32), axis=0, keepdims=True)
    sums_ref[:, HALF:] = jnp.sum(dqkv_ref[:, 2 * HALF :].astype(F32), axis=0, keepdims=True)


def back(tier, *args):
    blocks = (lax.axis_size("mp"), 2)[tier]
    dqkv, *grads, sums, table = kernel_call(
        f"back{tier + 1}",
        partial(back_kernel, tier),
        len(args),
        [shape_of((R, TIER), BF16)]
        + [shape_of((HALF // blocks, TIER + D * (tier == 0)), BF16)] * (2 * blocks)
        + [shape_of((1, D), F32), shape_of((HEAD, LANES), F32)],
    )(*args)
    return dqkv, grads[:blocks], grads[blocks:], sums, table


def finish_kernel(
    wide, dq1_ref, dq2_ref, own1_ref, other1_ref, own2_ref, other2_ref, att_ref, x_ref,
    downb_ref, upb_ref, sums0_ref, sums1_ref, sums2_ref, tab1_ref, tab2_ref,
    da1_ref, small_ref,
):
    spread = spread_rows()
    dq1, dq2 = dot_tn(spread, dq1_ref[...]).astype(BF16), dot_tn(spread, dq2_ref[...]).astype(BF16)
    halves = []
    for first, second in ((own1_ref, own2_ref), (other1_ref, other2_ref)):
        halves.append(dot_nt(dq1, first[...]) + dot_nt(dq2, second[:, :TIER]))
    moved = jnp.concatenate(halves, axis=1)
    high = moved.astype(BF16)
    low = (moved - high.astype(F32)).astype(BF16)
    da1 = dot_nn(high, att_ref[...]) + dot_nn(low, att_ref[...])
    da1_ref[...] = da1
    unit, _ = norm_parts(x_ref[...].astype(F32))
    small_ref[...] = jnp.zeros(small_ref.shape, F32)

    def put(name, value):
        for i in range(D // LANES):
            small_ref[piece(SMALL[name] + i)] = value[:, i * LANES : (i + 1) * LANES]

    put("gain1", jnp.sum(da1 * unit, axis=0, keepdims=True))
    put("shift1", jnp.sum(da1, axis=0, keepdims=True))
    put("projb", sums0_ref[0:1])
    put("gain2", sums0_ref[1:2])
    put("shift2", sums0_ref[2:3])
    put("qbias", jnp.concatenate([sums1_ref[:, :HALF], sums2_ref[:, :HALF]], axis=1))
    put("vbias", jnp.concatenate([sums1_ref[:, HALF:], sums2_ref[:, HALF:]], axis=1))
    put("downb", downb_ref[...])
    table = tab1_ref[...] + tab2_ref[...]
    low, high = table[: HEAD // 2], table[HEAD // 2 :]
    lane = iota(low.shape, 1)
    packed = jnp.where(
        lane < 32,
        low,
        jnp.where(
            lane < 64,
            pltpu.roll(low, (32 - W_START) % LANES, 1),
            jnp.where(lane < 96, pltpu.roll(high, 64, 1), pltpu.roll(high, (96 - W_START) % LANES, 1)),
        ),
    )
    for i in range(HEAD // 2):
        small_ref[piece(SMALL_TABLE + i)] = packed[i : i + 1]
    count = lax.axis_size("dp")
    size = upb_ref.shape[1] // count
    for m in range(wide):
        for i in range(count):
            rows, lanes = piece(SMALL_UP + m * count + i)
            value = upb_ref[:, i * size : (i + 1) * size]
            lanes = slice(lanes.start, lanes.start + size)
            small_ref[rows, lanes] = jnp.where(lax.axis_index("mp") == m, value, 0.0)


def finish(wide, rows, *args):
    return kernel_call(
        "finish",
        partial(finish_kernel, wide),
        15,
        [shape_of((AREA, D), F32), shape_of((rows, TIER), F32)],
    )(*args)


def outputs_kernel(
    n_parts, rows, keep_ref, da1_ref, x_ref, dmid_ref, params_ref, mid_ref, m_ref, mgot_ref, *refs
):
    parts, refs = refs[:n_parts], refs[n_parts:]
    *refs, dx_ref, result_ref, table_ref, up_ref = refs
    unit, factor = norm_parts(x_ref[...].astype(F32))
    dx_ref[...] = (dmid_ref[...] + norm_back(da1_ref[...], unit, factor, params_ref[0:1])).astype(BF16)
    feed_sum = m_ref[...] + mgot_ref[...].astype(F32) + params_ref[5:6]
    result_ref[...] = (mid_ref[...] + rate_of(keep_ref, 1) * feed_sum).astype(BF16)
    gain1_ref, shift1_ref, qv_ref, relh_ref, relw_ref, projb_ref, gain2_ref, shift2_ref, upb_ref, downb_ref = refs
    total = parts[0][...]
    for part in parts[1:]:
        total = total + part[part.shape[0] - rows :].astype(F32)
    flat = {
        "gain1": gain1_ref, "shift1": shift1_ref, "projb": projb_ref, "gain2": gain2_ref, "shift2": shift2_ref,
        "downb": downb_ref,
    }

    def at(place):
        here, lanes = piece(place)
        return total[here, lanes]

    for i in range(D // LANES):
        here = slice(i * LANES, (i + 1) * LANES)
        for name, ref in flat.items():
            ref[here] = at(SMALL[name] + i)[0]
        qv_ref[0:1, here] = at(SMALL["qbias"] + i)
        qv_ref[1:2, here] = at(SMALL["vbias"] + i)
    for i in range(HEAD // 2):
        table_ref[i : i + 1] = at(SMALL_TABLE + i)
    for start, ref in ((0, relh_ref), (32, relw_ref)):
        for half in range(2):
            ref[:, half * 32 : half * 32 + 32] = lax.dot_general(
                table_places(start + 64 * half, straight=start > 0), table_ref[...], (((1,), (1,)), ((), ())),
                precision=lax.Precision.HIGHEST, preferred_element_type=F32,
            )
    for i in range(up_ref.shape[0]):
        up_ref[i : i + 1] = at(SMALL_UP + i)
    place = lax.axis_index("mp") * lax.axis_size("dp") + lax.axis_index("dp")
    upb_ref[...] = up_ref[place, : upb_ref.shape[0]]


def outputs(parts, size, ups, *rows):
    row = shape_of((D,), F32)
    table = shape_of((TABLE, HEAD), F32)
    return kernel_call(
        "outputs",
        partial(outputs_kernel, len(parts), parts[0].shape[0]),
        8 + len(parts),
        [row, row, shape_of((2, D), F32), table, table, row, row, row, shape_of((size,), F32), row]
        + [shape_of((AREA, D), BF16)] * 2,
        smem=1,
        scratch=[pltpu.VMEM((HEAD // 2, LANES), F32), pltpu.VMEM((ups, LANES), F32)],
        out_far=range(12),
    )(*rows, *parts)


def per_device(
    tokens, ln1_gain, ln1_bias, qkv_weight, qv_bias, rel_pos_h, rel_pos_w, proj_weight, proj_bias,
    ln2_gain, ln2_bias, fc1_weight, fc1_bias, fc2_weight, fc2_bias, keep_mask, key_mask, out_grad,
):
    wide = lax.axis_size("mp")
    hidden = fc1_weight.shape[1]
    first, second, params, dm = pack(
        keep_mask, qkv_weight, proj_weight, ln1_gain, ln1_bias, proj_bias, ln2_gain, ln2_bias, fc2_bias, qv_bias, out_grad
    )
    made, chains = {}, {}

    def gated(value, task, kind):
        others = [made[name] for name in GATES.get(f"{task}:{kind}", ())]
        return after(value, *others) if others else value

    def front(name):
        if name == "dm":
            sent = gated(dm, name, "s")
            return gated([move_x(sent, -s) for s in range(1, wide)], name, "r")
        if name == "prep":
            return prepare(gated(tokens, name, "s"), params, rel_pos_h, rel_pos_w, key_mask, fc1_bias)
        if name == "act0":
            return act_grad(gated(dm, name, "s"), fc2_weight)
        if name == "act1":
            return [act_grad(v, fc2_weight) for v in gated(made["dm"], name, "s")]
        if name == "attend1":
            a1, _, _, _, _, twice, fill, _ = made["prep"]
            return attend_first(gated(a1, name, "s"), chains["1"], made["c1"], params, twice, fill)
        step, tier = name
        if step == "z":
            sent = gated((first, second)[int(tier) - 1], name, "s")
            chains[tier] = gated(gather_z(sent), name, "r")
            return chains[tier]
        if step == "n":
            return gated(gather_near(gated(chains[tier], name, "s")), name, "r")
        if step == "f":
            made["n" + tier] = gated(made["n" + tier], name, "s")
            return gated(gather_far(made["n" + tier]), name, "r")
        chains[tier] = gated(gather_join(chains[tier], made["n" + tier], made["f" + tier]), name, "s")
        return gated(move_c(chains[tier]), name, "r")

    for name in FRONT:
        made[name] = front(name)
    a1, a1_turned, att_map, feed_map, tables, twice, fill, upb = made["prep"]
    dms = [dm, *made["dm"]]
    acts = [made["act0"], *made["act1"]]
    gacts, downb = [v[0] for v in acts], acts[0][1]
    own1, other1, own2, other2 = chains["1"], made["c1"], chains["2"], made["c2"]
    qkv1, probs1, att1 = made["attend1"]
    qkv2, probs2, att_turned, middle, a2 = attend_second(
        keep_mask, a1, own2, other2, params, twice, fill, att1, tokens, att_map
    )

    a2s = [a2] + [move_x(a2, -s) for s in range(1, wide)]
    fed = [feed(a2, fc1_weight, upb, gacts[0], F32)]
    for j in range(1, wide):
        fed.append(feed(after(a2s[j], fed[-1][2]), fc1_weight, upb, gacts[j], BF16))
    da2 = fed[0][2]
    got = [move_x(fed[s][2], s) for s in range(1, wide)]
    down_keep, down_send, up_keep, up_send, upb_sum, *outs = feed_weights(
        after(feed_map, fed[-1][2]), fc2_weight, dms, [f[0] for f in fed], a2s, [f[1] for f in fed]
    )
    got, down_send, up_send, outs = lax.optimization_barrier((got, down_send, up_send, outs))
    got = got[0] if wide == 2 else add_up(*got)
    depth = lax.axis_size("dp") // 4
    moves = {"x": (move_x, wide), "y": (turn_y, 2), "z": (move_z, depth)}
    small_rows = -(-(SMALL_UP + wide * lax.axis_size("dp")) // PIECES)
    small_rows += -small_rows % 16

    def cores(name, keep, send, axes):
        sent = gated(send, f"{name}c", "s")
        got = gated([move_c(v) for v in sent], f"{name}c", "r")
        chains[name] = (list(zip(keep, got)), axes)
        return got

    def count_of(axis):
        return depth if axis in "z0" else depth >> int(axis) if axis.isdigit() else moves[axis][1]

    def along(name, axis):
        sums, axes = chains[name]
        carries = ROUTE.get(axis) == name
        if axis.isdigit():
            mask = 1 << int(axis)
            sent = [jnp.concatenate([add_up(*v).astype(BF16) for v in sums[1::2]])]
            sent = gated(sent, f"{name}{axis}", "s")
            got = gated([swap_z(v, mask) for v in sent], f"{name}{axis}", "r")
            size = sums[0][0].shape[0]
            sums = [[*v, got[0][i * size : (i + 1) * size]] for i, v in enumerate(sums[::2])]
            axes = axes[axes.index(axis) + 1 :]
            if axes and axes[0].isdigit():
                chains[name] = (sums, axes)
            else:
                chains[name] = (split(sums[0], count_of(axes[0])), axes) if axes else (sums[0], axes)
            return got
        if axis == "z" and name in "du":
            move = swap_z
        else:
            move, _ = moves[axis]
        sent = [add_up(*v).astype(BF16) for v in sums[1:]]
        if carries:
            extra = chains["s"].astype(BF16)
            sent = [jnp.concatenate([v, extra]) for v in sent]
        sent = gated(sent, f"{name}{axis}", "s")
        got = gated([move(v, s + 1) for s, v in enumerate(sent)], f"{name}{axis}", "r")
        rest = [*sums[0], *got]
        if carries:
            rows = sums[0][0].shape[0]
            rest = [*sums[0], *[v[:rows] for v in got]]
            if axis == "z":
                chains["s"] = [chains["s"], *got]
            else:
                chains["s"] = add_up(chains["s"], *[v[rows:] for v in got])
        axes = axes[axes.index(axis) + 1 :]
        chains[name] = (split(rest, count_of(axes[0])), axes) if axes else (rest, axes)
        return got

    def small_cores():
        flat = gated(made["finish"][1], "sc", "s")
        got = gated(move_c(flat), "sc", "r")
        chains["s"] = flat + got
        return got

    def task(name):
        if name == "norm":
            return back_norm(keep_mask, da2, got, middle, out_grad, params, own2, other2, att_map)
        if name in ("back1", "back2"):
            tier = int(name[-1]) - 1
            do = gated(made["norm"][1], name, "s")
            more = (att_turned, made["norm"][2]) if tier == 0 else ()
            return back(tier, do, a1_turned, (qkv1, qkv2)[tier], (probs1, probs2)[tier], tables, *more)
        if name == "m":
            moved = [move_x(v, s + 1) for s, v in enumerate(gated(outs[1:], "m", "s"))]
            moved = gated(moved, "m", "r")
            return moved[0] if wide == 2 else add_up(*moved)
        if name == "finish":
            first, second = made["back1"], made["back2"]
            row_map = gated(att_map, "finish", "s")
            return finish(
                wide, small_rows, first[0], second[0], own1, other1, own2, other2, row_map, tokens,
                downb, upb_sum, made["norm"][3], first[3], second[3], first[4], second[4],
            )
        chain, axis = name
        if chain == "s":
            return small_cores()
        if axis != "c":
            return along(chain, axis)
        if chain in "du":
            keep, send = (down_keep, down_send) if chain == "d" else (up_keep, up_send)
            bits = "".join(str(i) for i in range(depth.bit_length() - 1)) if TREE["du".index(chain)] else "z"
            return cores(chain, keep, send, bits + "y" if Z_FIRST["du".index(chain)] else "y" + bits)
        tier = "ab".index(chain)
        return cores(chain, made[f"back{tier + 1}"][1], made[f"back{tier + 1}"][2], ("xyz", "yxz")[tier])

    for name in ORDER:
        made[name] = task(name)
        while name[-1] == "1" and name[0] in "du" and chains[name[0]][1][:1].isdigit():
            along(name[0], chains[name[0]][1][0])
    small = chains["s"]
    down_grad, up_grad, rows1, rows2 = (add_up(*chains[name][0]) for name in "duab")
    proj_grad = rows1[:, TIER:]

    pieces = [
        piece
        for i in range(3)
        for piece in (rows1[:, i * HALF : (i + 1) * HALF], rows2[:, i * HALF : (i + 1) * HALF])
    ]
    qkv_grad = jnp.concatenate(pieces, axis=1)

    gain1, shift1, qv_grad, relh_grad, relw_grad, projb, gain2, shift2, up_bias_grad, downb, grad_in, result = outputs(
        small, hidden // lax.axis_size("dp"), wide * lax.axis_size("dp"),
        keep_mask, made["finish"][0], tokens, made["norm"][0], params, middle, outs[0], made["m"],
    )
    return (
        result, grad_in, gain1, shift1, qkv_grad, qv_grad, relh_grad, relw_grad, proj_grad, projb, gain2, shift2,
        up_grad, up_bias_grad, down_grad.T, downb,
    )


def solution(mesh):
    in_specs = (
        P(("dp", "mp"), None),
        P(),
        P(),
        P(("dp", "mp"), None),
        P(),
        P(),
        P(),
        P(("dp", "mp"), None),
        P(),
        P(),
        P(),
        P(None, "mp"),
        P("mp"),
        P("mp", None),
        P(),
        P(("dp", "mp"), None),
        P(("dp", "mp"), None),
        P(("dp", "mp"), None),
    )
    out_specs = (
        P(("dp", "mp"), None),
        P(("dp", "mp"), None),
        P(),
        P(),
        P(("dp", "mp"), None),
        P(),
        P(),
        P(),
        P(("dp", "mp"), None),
        P(),
        P(),
        P(),
        P("dp", "mp"),
        P(("mp", "dp")),
        P("mp", "dp"),
        P(),
    )
    return jax.shard_map(
        per_device, mesh=mesh, in_specs=in_specs, out_specs=out_specs, check_vma=False
    )
```
